32 devices in a mesh: dp: 16 (over z, y, core), pre: 2 (over x).
Axes of the slice: x: 2, y: 2, z: 4, core: 2. Of those that a mesh axis runs over, the one named last changes fastest.
Arguments:
- inputs: bfloat16 [2048, 4096], P('dp'), may hold values from -12 to 12, as said below
- weight: bfloat16 [4096, 1024], P(None, 'pre'), may hold values from -0.09375 to 0.09375
- cotangent: bfloat16 [2048, 1024], P('dp', 'pre'), may hold values from -12 to 12, as said below
Outputs:
- outputs: bfloat16 [2048, 1024], P('dp', 'pre')
- update: bfloat16 [8, 512, 1024], P(None, 'pre')
The draws below stay inside these ranges and needn't reach their ends.
Inputs may be any that keep to these rules, and one draw needn't show every extreme that they name: `inputs`: activations with unequal scales across features. `cotangent`: gradients with unequal scales across features.
All inputs are finite; a program needn't handle non-finite values.
Results may differ from the reference program's by a relative error of at most 0.0079.
Values may be sent and summed in bfloat16 or wider, within the bound.
No kernel may reach another device: no remote copies, remote signals or barrier semaphores. Data moves between devices by JAX's collectives and lax.ppermute only.
A program may use at most 64 MiB of HBM per device.

```python
import math
import jax
import jax.numpy as jnp
from jax import lax

D = 4096
BLOCK = 512
CB = 2
ITERS = 3
C = 1024
RB = 8
TOKENS = 2048


def draw_inputs(key, part):
    key = jax.random.fold_in(key, 11)
    key_base, key_scale = jax.random.split(key, 2)
    base_draw = jax.random.normal(key_base, (TOKENS, D), jnp.float32)
    scales = jnp.exp(jax.random.uniform(key_scale, (1, D), jnp.float32, -1.2, 1.2))
    return jnp.clip(base_draw * scales, -12.0, 12.0).astype(jnp.bfloat16)


def draw_cotangent(key, part):
    key = jax.random.fold_in(key, 23)
    key_base, key_scale = jax.random.split(key, 2)
    base_draw = jax.random.normal(key_base, (TOKENS, CB * BLOCK), jnp.float32)
    scales = jnp.exp(jax.random.uniform(key_scale, (1, CB * BLOCK), jnp.float32, -1.2, 1.2))
    return jnp.clip(base_draw * scales, -12.0, 12.0).astype(jnp.bfloat16)


def block_scale(stream_key, shape, cuts, low, largest):
    loudness = 1.0
    for position, shards_of in cuts:
        steps = jax.random.uniform(jax.random.fold_in(jax.random.fold_in(stream_key, 6), position), (shards_of,), jnp.float32, low / len(cuts), largest / len(cuts))
        loudness = loudness * jnp.repeat(jnp.exp(steps), shape[position] // shards_of).reshape((-1,) + (1,) * (len(shape) - 1 - position))
    return loudness


def bell_draw(stream_key, shape, scale, reach, cuts=(), held_as=jnp.bfloat16):
    level = block_scale(stream_key, shape, cuts, -0.22, 0.18) if cuts else 1.0
    drawn = jax.random.normal(stream_key, shape, jnp.float32) * scale * level
    return jnp.minimum(jnp.maximum(drawn, -reach), reach).astype(held_as)


def setup_inputs(seed: int = 0) -> dict:
    splits = jax.random.split(jax.random.key(seed), 4)
    return {
        "inputs": draw_inputs(jax.random.fold_in(splits[3], 71), 0),
        "weight": bell_draw(splits[1], (D, C), D ** -0.5, 0.09375, ((1, 2),)),
        "cotangent": draw_cotangent(jax.random.fold_in(splits[3], 71), 0),
    }


DAMPING = 0.1
HIGH = lax.Precision.HIGHEST

def inverse_root(statistic):
    order_n = statistic.shape[0]
    unit_eye = jnp.eye(order_n, dtype=jnp.float32)
    damp_shift = DAMPING * jnp.trace(statistic) / order_n
    matrix = statistic + damp_shift * unit_eye
    frob_norm = jnp.sqrt(jnp.sum(matrix * matrix))
    normalized = matrix / frob_norm
    root_now = unit_eye * frob_norm ** (-0.25)
    for iteration in range(ITERS):
        factor = (5.0 * unit_eye - normalized) * 0.25
        square = jnp.dot(factor, factor, precision=HIGH)
        fourth = jnp.dot(square, square, precision=HIGH)
        normalized = jnp.dot(fourth, normalized, precision=HIGH)
        root_now = jnp.dot(root_now, factor, precision=HIGH)
    return root_now

def one_block(grad_block):
    left_stat = jnp.dot(grad_block, grad_block.T, precision=HIGH)
    right_stat = jnp.dot(grad_block.T, grad_block, precision=HIGH)
    root_left = inverse_root(left_stat).astype(jnp.bfloat16)
    root_right = inverse_root(right_stat).astype(jnp.bfloat16)
    half_prod = jnp.dot(root_left, grad_block.astype(jnp.bfloat16), preferred_element_type=jnp.float32).astype(jnp.bfloat16)
    full_prod = jnp.dot(half_prod, root_right, preferred_element_type=jnp.float32)
    return (full_prod * math.sqrt(BLOCK)).astype(jnp.bfloat16)

def reference(inputs, weight, cotangent):
    outputs = jnp.dot(inputs, weight, preferred_element_type=jnp.float32).astype(jnp.bfloat16)
    gradient = jnp.dot(inputs.T, cotangent, preferred_element_type=jnp.float32)
    grad_blocks = gradient.reshape(RB, BLOCK, CB, BLOCK).transpose(0, 2, 1, 3).reshape(RB * CB, BLOCK, BLOCK)
    pieces = lax.map(one_block, grad_blocks)
    update = pieces.reshape(RB, CB, BLOCK, BLOCK).transpose(0, 2, 1, 3).reshape(RB, BLOCK, CB * BLOCK)
    return (outputs, update)
```

```python
import math

import jax
import jax.numpy as jnp
from jax import lax
from jax.experimental import pallas as pl
from jax.experimental.pallas import tpu as pltpu
from jax.sharding import PartitionSpec as P

D = 4096
BLOCK = 512
CB = 2
ITERS = 3


DAMPING = 0.1
HIGH = lax.Precision.HIGHEST


def batch_dot(former, latter):
    return jnp.einsum(
        "sij,sjk->sik", former, latter, precision=HIGH, preferred_element_type=jnp.float32
    )


def on_device_general(inputs, weight, cotangent):
    groups = lax.axis_size("dp")
    members = lax.axis_size("pre")
    group_id = lax.axis_index("dp")
    member_id = lax.axis_index("pre")
    slab_rows = BLOCK // members
    blocks_all = D // BLOCK * CB
    rounds = max(1, blocks_all // groups)
    sharers = max(1, groups // blocks_all)
    col_width = BLOCK // sharers
    copy_id = group_id // blocks_all
    outputs = jnp.dot(inputs, weight, preferred_element_type=jnp.float32).astype(jnp.bfloat16)
    partial_value = lax.dot_general(
        inputs, cotangent, (((0,), (0,)), ((), ())), preferred_element_type=jnp.float32
    )
    owned_ids = (group_id + groups * jnp.arange(rounds, dtype=jnp.int32)) % blocks_all
    row_offsets = owned_ids // CB * BLOCK
    col_offsets = owned_ids % CB * BLOCK
    gradient = lax.psum(partial_value, "dp")
    row_bands = jax.vmap(lambda offset: lax.dynamic_slice_in_dim(gradient, offset, BLOCK, 0))(
        row_offsets
    )
    wide_band = lax.all_gather(row_bands, "pre", axis=2, tiled=True)
    tile_grad = jax.vmap(
        lambda row_band, offset: lax.dynamic_slice_in_dim(row_band, offset, BLOCK, 1)
    )(wide_band, col_offsets)
    first_row = member_id * slab_rows
    own_rows = lax.dynamic_slice_in_dim(tile_grad, first_row, slab_rows, 1)
    own_cols = lax.dynamic_slice_in_dim(tile_grad, first_row, slab_rows, 2)
    left_rows = jnp.einsum(
        "sij,skj->sik", own_rows, tile_grad, precision=HIGH, preferred_element_type=jnp.float32
    )
    right_rows = jnp.einsum(
        "sji,sjk->sik", own_cols, tile_grad, precision=HIGH, preferred_element_type=jnp.float32
    )
    stat_rows = jnp.stack([left_rows, right_rows], axis=1).reshape(rounds * 2, slab_rows, BLOCK)
    tile_energy = jnp.sum(tile_grad * tile_grad, axis=(1, 2))
    energy = jnp.stack([tile_energy, tile_energy], axis=1).reshape(rounds * 2)
    unit_rows = (jnp.arange(BLOCK)[None, :] == (first_row + jnp.arange(slab_rows))[:, None]).astype(
        jnp.float32
    )
    unit_eye = jnp.eye(BLOCK, dtype=jnp.float32)
    state_rows = stat_rows + (DAMPING * energy / BLOCK)[:, None, None] * unit_rows[None]
    root_rows = unit_rows[None]
    for iteration in range(ITERS):
        full_state = lax.all_gather(state_rows, "pre", axis=1, tiled=True)
        if iteration == 0:
            frob_norm = jnp.sqrt(jnp.sum(full_state * full_state, axis=(1, 2)))
            full_state = full_state / frob_norm[:, None, None]
            state_rows = state_rows / frob_norm[:, None, None]
            root_rows = unit_rows[None] * (frob_norm ** (-0.25))[:, None, None]
        factor = (5.0 * unit_eye - full_state) * 0.25
        square = batch_dot(factor, factor)
        square_rows = lax.dynamic_slice_in_dim(square, first_row, slab_rows, 1)
        fourth_rows = batch_dot(square_rows, square)
        state_rows = batch_dot(fourth_rows, full_state)
        root_rows = batch_dot(root_rows, factor)
    root_half = root_rows.astype(jnp.bfloat16).reshape(rounds, 2, slab_rows, BLOCK)
    right_full = lax.all_gather(root_half[:, 1], "pre", axis=1, tiled=True)
    right_cols = lax.dynamic_slice_in_dim(right_full, copy_id * col_width, col_width, 2)
    tile_half = tile_grad.astype(jnp.bfloat16)
    half_prod = jnp.einsum(
        "sij,sjk->sik", root_half[:, 0], tile_half, preferred_element_type=jnp.float32
    ).astype(jnp.bfloat16)
    piece_rows = jnp.einsum(
        "sij,sjk->sik", half_prod, right_cols, preferred_element_type=jnp.float32
    )
    piece_rows = (piece_rows * math.sqrt(BLOCK)).astype(jnp.bfloat16)
    collected = lax.all_gather(piece_rows[None], "dp", axis=0, tiled=True)
    if sharers == 1:
        ordered = jnp.swapaxes(collected, 0, 1).reshape(blocks_all, slab_rows, BLOCK)
    else:
        ordered = (
            collected[:, 0]
            .reshape(sharers, blocks_all, slab_rows, col_width)
            .transpose(1, 2, 0, 3)
            .reshape(blocks_all, slab_rows, BLOCK)
        )
    update = (
        ordered.reshape(D // BLOCK, CB, slab_rows, BLOCK)
        .transpose(0, 2, 1, 3)
        .reshape(D // BLOCK, slab_rows, CB * BLOCK)
    )
    return (outputs, update)


def contract(former, latter, former_dim, latter_dim):
    return lax.dot_general(
        former,
        latter,
        (((former_dim,), (latter_dim,)), ((), ())),
        preferred_element_type=jnp.float32,
    )


def product(former, latter):
    return contract(former.astype(jnp.bfloat16), latter.astype(jnp.bfloat16), 1, 0)


def total(array):
    return jnp.sum(jnp.sum(array, axis=0, keepdims=True), axis=1, keepdims=True)


def newton_step(state):
    excess = product(state, state) * (1.0 / 16.0) - 0.625 * state
    growth = 3.125 * excess + product(excess, excess)
    return (625.0 / 256.0) * state + product(state, growth)


def newton_kernel(side_ref, mine_ref, other_ref, tile_ref, root_ref, stat_ref):
    tile = mine_ref[...] + other_ref[...]
    tile_half = tile.astype(jnp.bfloat16)
    tile_ref[...] = tile_half

    @pl.when(side_ref[0] == 0)
    def _():
        stat_ref[...] = contract(tile_half, tile_half, 1, 1)

    @pl.when(side_ref[0] != 0)
    def _():
        stat_ref[...] = contract(tile_half, tile_half, 0, 0)

    order = tile.shape[0]
    row_ids = lax.broadcasted_iota(jnp.int32, (order, order), 0)
    col_ids = lax.broadcasted_iota(jnp.int32, (order, order), 1)
    on_diagonal = row_ids == col_ids
    damp = (DAMPING / order) * total(tile * tile)
    matrix = stat_ref[...]
    matrix = jnp.where(on_diagonal, matrix + damp, matrix)
    norm = jnp.sqrt(total(matrix * matrix))
    first = matrix / norm
    second = newton_step(first)
    third = newton_step(second)
    cross = product(first, second) * (1.0 / 16.0) - (5.0 / 16.0) * (first + second)
    last = product(cross, third)
    root = 1.25 * cross - 0.25 * last - (25.0 / 64.0) * third
    root = jnp.where(on_diagonal, root + 125.0 / 64.0, root)
    scale = 1.0 / jnp.sqrt(jnp.sqrt(norm))
    root_ref[...] = (root * scale).astype(jnp.bfloat16)


OFFSETS = ((1, 4, 7, 2), (3, 5, 6, 2))


def pack_kernel(place_ref, inputs_ref, *piece_refs):
    for step, piece_ref in enumerate(piece_refs):
        rows = piece_ref.shape[0]
        last = step == len(piece_refs) - 1
        first_row = pl.multiple_of(place_ref[0], rows) if last else 0
        first_col = pl.multiple_of(place_ref[1 + step] * BLOCK, BLOCK)
        piece_ref[...] = inputs_ref[pl.ds(first_row, rows), pl.ds(first_col, BLOCK)]


def ring_band(position, bands):
    position = (position + 2 * bands) % bands
    return jnp.where(position < bands // 2, 2 * position, 2 * (bands - 1 - position) + 1)


def tile_kernel(place_ref, own_ref, *refs):
    hops = len(OFFSETS[0])
    near_refs, far_refs = refs[:hops], refs[hops : 2 * hops]
    cot_refs = refs[2 * hops : -3]
    partial_ref, band_ref, cot_ref = refs[-3:]
    plane, band, spot = place_ref[0], place_ref[1], place_ref[2]
    tokens = own_ref.shape[0]

    def put(to_ref, piece_ref, source, part):
        rows = piece_ref.shape[0]
        first_row = pl.multiple_of(source * tokens + part * rows, rows)
        to_ref[pl.ds(first_row, rows), :] = piece_ref[...]

    put(band_ref, own_ref, band, 0)
    for hop in range(hops):
        last = hop == hops - 1
        for piece_ref, member in ((near_refs[hop], plane), (far_refs[hop], 1 - plane)):
            offset = jnp.where(member == 0, OFFSETS[0][hop], OFFSETS[1][hop])
            put(band_ref, piece_ref, band ^ offset, member if last else 0)
    for step, piece_ref in enumerate(cot_refs):
        put(cot_ref, piece_ref, ring_band(spot - step, len(cot_refs)), 0)
    partial_ref[...] = contract(band_ref[...], cot_ref[...], 0, 0)


def update_kernel(side_ref, mine_ref, other_ref, tile_ref, near_ref, far_ref):
    rows = near_ref.shape[0]
    tile = tile_ref[...]
    core, plane = side_ref[0], side_ref[1]

    def write(left_ref, right_ref):
        for out_ref, member in ((near_ref, plane), (far_ref, 1 - plane)):
            first_row = pl.multiple_of(member * rows, rows)
            left = left_ref[pl.ds(first_row, rows), :]
            half = contract(left, tile, 1, 0).astype(jnp.bfloat16)
            piece = contract(half, right_ref[...], 1, 0) * math.sqrt(BLOCK)
            out_ref[...] = piece.astype(jnp.bfloat16)

    @pl.when(core == 0)
    def _():
        write(mine_ref, other_ref)

    @pl.when(core != 0)
    def _():
        write(other_ref, mine_ref)


def place_kernel(place_ref, *refs):
    hops = (len(refs) - 4) // 4
    update_ref, sems = refs[-2:]
    core, plane, spot = place_ref[0], place_ref[1], place_ref[2]
    bands = update_ref.shape[0]
    ahead = 1 - 2 * core
    copies = []

    def put(piece_ref, position, part, chunk):
        rows = piece_ref.shape[0]
        member = plane if chunk == 0 else 1 - plane
        first_row = pl.multiple_of(part * rows, rows)
        first_col = pl.multiple_of(member * BLOCK, BLOCK)
        to_ref = update_ref.at[
            ring_band(position, bands), pl.ds(first_row, rows), pl.ds(first_col, BLOCK)
        ]
        copy = pltpu.make_async_copy(piece_ref, to_ref, sems.at[len(copies)])
        copy.start()
        copies.append(copy)

    for chunk in range(2):
        put(refs[chunk], spot, 0, chunk)
    for hop in range(1, hops + 1):
        last = hop == hops
        for chunk in range(2):
            mine_ref, other_ref = refs[2 + 4 * (hop - 1) + 2 * chunk :][:2]
            put(mine_ref, spot - ahead * hop, core if last else 0, chunk)
            put(other_ref, spot + ahead * hop, 1 - core if last else 0, chunk)
    for copy in copies:
        copy.wait()


def call(kernel, out_shapes, scratch_shapes, *operands):
    in_specs = [pl.BlockSpec(memory_space=pltpu.SMEM)]
    in_specs += [pl.BlockSpec(memory_space=pltpu.VMEM)] * (len(operands) - 1)
    return pl.pallas_call(
        kernel,
        out_shape=out_shapes,
        in_specs=in_specs,
        out_specs=[pl.BlockSpec(memory_space=pltpu.VMEM)] * len(out_shapes),
        scratch_shapes=scratch_shapes,
        compiler_params=pltpu.CompilerParams(vmem_limit_bytes=32 * 1024 * 1024),
    )(*operands)


def on_device_paired(inputs, weight, cotangent):
    bands = D // BLOCK
    groups = lax.axis_size("dp")
    cores = groups // bands
    members = lax.axis_size("pre")
    core = lax.axis_index("dp") % cores
    band = lax.axis_index("dp") // cores
    plane = lax.axis_index("pre")
    tokens = inputs.shape[0]
    spot = jnp.where(band % 2 == 0, band // 2, bands - 1 - band // 2)

    ring = list(range(0, bands, 2)) + list(range(bands - 1, 0, -2))

    def shift(array, distance):
        pairs = [
            (ring[k] * cores + c, ring[(k + distance) % bands] * cores + c)
            for k in range(bands)
            for c in range(cores)
        ]
        return lax.ppermute(array, "dp", pairs)

    def swap_core(array):
        return lax.ppermute(array, "dp", [(g, g ^ 1) for g in range(groups)])

    def swap_plane(array):
        return lax.ppermute(array, "pre", [(c, members - 1 - c) for c in range(members)])

    def around(array):
        pieces = [array] + [None] * (bands - 1)
        for step in range(1, bands // 2 + 1):
            pieces[step] = shift(pieces[step - 1], 1)
            if step < bands // 2:
                pieces[bands - step] = shift(pieces[(bands - step + 1) % bands], -1)
        return pieces

    def deal(array, hop):
        pairs = [
            (
                (k * cores + c) * members + m,
                ((k ^ OFFSETS[m][hop]) * cores + c) * members + m,
            )
            for k in range(bands)
            for c in range(cores)
            for m in range(members)
        ]
        return lax.ppermute(array, ("dp", "pre"), pairs)

    hops = range(len(OFFSETS[0]))
    bands_out = [band ^ jnp.where(plane == 0, OFFSETS[0][hop], OFFSETS[1][hop]) for hop in hops]
    own_band, *packed = call(
        pack_kernel,
        [jax.ShapeDtypeStruct((tokens, BLOCK), inputs.dtype)] * len(hops)
        + [jax.ShapeDtypeStruct((tokens // 2, BLOCK), inputs.dtype)],
        [],
        jnp.stack([plane * (tokens // 2), band] + bands_out).astype(jnp.int32),
        inputs,
    )
    cots = around(cotangent)
    near = [deal(piece, hop) for hop, piece in zip(hops, packed)]
    far = [swap_plane(piece) for piece in near]
    outputs = jnp.dot(inputs, weight, preferred_element_type=jnp.float32).astype(jnp.bfloat16)
    own_band, outputs = lax.optimization_barrier((own_band, outputs))
    (partial_tile,) = call(
        tile_kernel,
        [jax.ShapeDtypeStruct((BLOCK, BLOCK), jnp.float32)],
        [pltpu.VMEM((bands * tokens, BLOCK), inputs.dtype)] * 2,
        jnp.stack([plane, band, spot]).astype(jnp.int32),
        own_band,
        *near,
        *far,
        *cots,
    )
    other_partial = swap_core(partial_tile)
    side = jnp.stack([core, plane]).astype(jnp.int32)
    tile_half, root = call(
        newton_kernel,
        [
            jax.ShapeDtypeStruct((BLOCK, BLOCK), jnp.bfloat16),
            jax.ShapeDtypeStruct((BLOCK, BLOCK), jnp.bfloat16),
        ],
        [pltpu.VMEM((BLOCK, BLOCK), jnp.float32)],
        side,
        partial_tile,
        other_partial,
    )
    other_root = swap_core(root)
    rows = BLOCK // members
    near_piece, far_piece = call(
        update_kernel,
        [jax.ShapeDtypeStruct((rows, BLOCK), jnp.bfloat16)] * 2,
        [],
        side,
        root,
        other_root,
        tile_half,
    )

    def turn(array):
        pairs = [
            (ring[k] * cores + c, ring[(k + 1 - 2 * c) % bands] * cores + c)
            for k in range(bands)
            for c in range(cores)
        ]
        return lax.ppermute(array, "dp", pairs)

    half_way = bands // 2
    heads = [near_piece, swap_plane(far_piece)]
    pieces = list(heads)
    for hop in range(1, half_way + 1):
        for chunk in range(2):
            head = heads[chunk]
            if hop == half_way:
                head = lax.dynamic_slice_in_dim(head.reshape(2, -1, BLOCK), core, 1, 0)[0]
            heads[chunk] = turn(head)
            pieces += [heads[chunk], swap_core(heads[chunk])]
    update = pl.pallas_call(
        place_kernel,
        out_shape=jax.ShapeDtypeStruct((bands, rows, CB * BLOCK), jnp.bfloat16),
        in_specs=[pl.BlockSpec(memory_space=pltpu.SMEM)]
        + [pl.BlockSpec(memory_space=pltpu.VMEM)] * len(pieces),
        out_specs=pl.BlockSpec(memory_space=pl.ANY),
        scratch_shapes=[pltpu.SemaphoreType.DMA((len(pieces),))],
    )(jnp.stack([core, plane, spot]).astype(jnp.int32), *pieces)
    return (outputs, update)


def solution(mesh):
    placed = (P("dp", None), P(None, "pre"), P("dp", "pre"))
    paired = mesh.shape["dp"] == 2 * D // BLOCK and mesh.shape["pre"] == CB == 2
    return jax.shard_map(
        on_device_paired if paired else on_device_general,
        mesh=mesh,
        in_specs=placed,
        out_specs=(P("dp", "pre"), P(None, "pre", None)),
        check_vma=False,
    )
```

```python
import math

import jax
import jax.numpy as jnp
from jax import lax
from jax.experimental import pallas as pl
from jax.experimental.pallas import tpu as pltpu
from jax.sharding import PartitionSpec as P

D = 4096
BLOCK = 512
CB = 2
ITERS = 3


DAMPING = 0.1
HIGH = lax.Precision.HIGHEST


def batch_dot(former, latter):
    return jnp.einsum(
        "sij,sjk->sik", former, latter, precision=HIGH, preferred_element_type=jnp.float32
    )


def on_device_general(inputs, weight, cotangent):
    groups = lax.axis_size("dp")
    members = lax.axis_size("pre")
    group_id = lax.axis_index("dp")
    member_id = lax.axis_index("pre")
    slab_rows = BLOCK // members
    blocks_all = D // BLOCK * CB
    rounds = max(1, blocks_all // groups)
    sharers = max(1, groups // blocks_all)
    col_width = BLOCK // sharers
    copy_id = group_id // blocks_all
    outputs = jnp.dot(inputs, weight, preferred_element_type=jnp.float32).astype(jnp.bfloat16)
    partial_value = lax.dot_general(
        inputs, cotangent, (((0,), (0,)), ((), ())), preferred_element_type=jnp.float32
    )
    owned_ids = (group_id + groups * jnp.arange(rounds, dtype=jnp.int32)) % blocks_all
    row_offsets = owned_ids // CB * BLOCK
    col_offsets = owned_ids % CB * BLOCK
    gradient = lax.psum(partial_value, "dp")
    row_bands = jax.vmap(lambda offset: lax.dynamic_slice_in_dim(gradient, offset, BLOCK, 0))(
        row_offsets
    )
    wide_band = lax.all_gather(row_bands, "pre", axis=2, tiled=True)
    tile_grad = jax.vmap(
        lambda row_band, offset: lax.dynamic_slice_in_dim(row_band, offset, BLOCK, 1)
    )(wide_band, col_offsets)
    first_row = member_id * slab_rows
    own_rows = lax.dynamic_slice_in_dim(tile_grad, first_row, slab_rows, 1)
    own_cols = lax.dynamic_slice_in_dim(tile_grad, first_row, slab_rows, 2)
    left_rows = jnp.einsum(
        "sij,skj->sik", own_rows, tile_grad, precision=HIGH, preferred_element_type=jnp.float32
    )
    right_rows = jnp.einsum(
        "sji,sjk->sik", own_cols, tile_grad, precision=HIGH, preferred_element_type=jnp.float32
    )
    stat_rows = jnp.stack([left_rows, right_rows], axis=1).reshape(rounds * 2, slab_rows, BLOCK)
    tile_energy = jnp.sum(tile_grad * tile_grad, axis=(1, 2))
    energy = jnp.stack([tile_energy, tile_energy], axis=1).reshape(rounds * 2)
    unit_rows = (jnp.arange(BLOCK)[None, :] == (first_row + jnp.arange(slab_rows))[:, None]).astype(
        jnp.float32
    )
    unit_eye = jnp.eye(BLOCK, dtype=jnp.float32)
    state_rows = stat_rows + (DAMPING * energy / BLOCK)[:, None, None] * unit_rows[None]
    root_rows = unit_rows[None]
    for iteration in range(ITERS):
        full_state = lax.all_gather(state_rows, "pre", axis=1, tiled=True)
        if iteration == 0:
            frob_norm = jnp.sqrt(jnp.sum(full_state * full_state, axis=(1, 2)))
            full_state = full_state / frob_norm[:, None, None]
            state_rows = state_rows / frob_norm[:, None, None]
            root_rows = unit_rows[None] * (frob_norm ** (-0.25))[:, None, None]
        factor = (5.0 * unit_eye - full_state) * 0.25
        square = batch_dot(factor, factor)
        square_rows = lax.dynamic_slice_in_dim(square, first_row, slab_rows, 1)
        fourth_rows = batch_dot(square_rows, square)
        state_rows = batch_dot(fourth_rows, full_state)
        root_rows = batch_dot(root_rows, factor)
    root_half = root_rows.astype(jnp.bfloat16).reshape(rounds, 2, slab_rows, BLOCK)
    right_full = lax.all_gather(root_half[:, 1], "pre", axis=1, tiled=True)
    right_cols = lax.dynamic_slice_in_dim(right_full, copy_id * col_width, col_width, 2)
    tile_half = tile_grad.astype(jnp.bfloat16)
    half_prod = jnp.einsum(
        "sij,sjk->sik", root_half[:, 0], tile_half, preferred_element_type=jnp.float32
    ).astype(jnp.bfloat16)
    piece_rows = jnp.einsum(
        "sij,sjk->sik", half_prod, right_cols, preferred_element_type=jnp.float32
    )
    piece_rows = (piece_rows * math.sqrt(BLOCK)).astype(jnp.bfloat16)
    collected = lax.all_gather(piece_rows[None], "dp", axis=0, tiled=True)
    if sharers == 1:
        ordered = jnp.swapaxes(collected, 0, 1).reshape(blocks_all, slab_rows, BLOCK)
    else:
        ordered = (
            collected[:, 0]
            .reshape(sharers, blocks_all, slab_rows, col_width)
            .transpose(1, 2, 0, 3)
            .reshape(blocks_all, slab_rows, BLOCK)
        )
    update = (
        ordered.reshape(D // BLOCK, CB, slab_rows, BLOCK)
        .transpose(0, 2, 1, 3)
        .reshape(D // BLOCK, slab_rows, CB * BLOCK)
    )
    return (outputs, update)


def contract(former, latter, former_dim, latter_dim):
    return lax.dot_general(
        former,
        latter,
        (((former_dim,), (latter_dim,)), ((), ())),
        preferred_element_type=jnp.float32,
    )


def product(former, latter):
    return contract(former.astype(jnp.bfloat16), latter.astype(jnp.bfloat16), 1, 0)


def total(array):
    return jnp.sum(jnp.sum(array, axis=0, keepdims=True), axis=1, keepdims=True)


def newton_step(state):
    excess = product(state, state) * (1.0 / 16.0) - 0.625 * state
    growth = 3.125 * excess + product(excess, excess)
    return (625.0 / 256.0) * state + product(state, growth)


def newton_kernel(side_ref, mine_ref, other_ref, tile_ref, root_ref, stat_ref):
    tile = mine_ref[...] + other_ref[...]
    tile_half = tile.astype(jnp.bfloat16)
    tile_ref[...] = tile_half

    @pl.when(side_ref[0] == 0)
    def _():
        stat_ref[...] = contract(tile_half, tile_half, 1, 1)

    @pl.when(side_ref[0] != 0)
    def _():
        stat_ref[...] = contract(tile_half, tile_half, 0, 0)

    order = tile.shape[0]
    row_ids = lax.broadcasted_iota(jnp.int32, (order, order), 0)
    col_ids = lax.broadcasted_iota(jnp.int32, (order, order), 1)
    on_diagonal = row_ids == col_ids
    damp = (DAMPING / order) * total(tile * tile)
    matrix = stat_ref[...]
    matrix = jnp.where(on_diagonal, matrix + damp, matrix)
    norm = jnp.sqrt(total(matrix * matrix))
    first = matrix / norm
    second = newton_step(first)
    third = newton_step(second)
    cross = product(first, second) * (1.0 / 16.0) - (5.0 / 16.0) * (first + second)
    last = product(cross, third)
    root = 1.25 * cross - 0.25 * last - (25.0 / 64.0) * third
    root = jnp.where(on_diagonal, root + 125.0 / 64.0, root)
    scale = 1.0 / jnp.sqrt(jnp.sqrt(norm))
    root_ref[...] = (root * scale).astype(jnp.bfloat16)


OFFSETS = ((4, 7, 1, 2), (5, 6, 3, 2))


def pack_kernel(place_ref, inputs_ref, *piece_refs):
    for step, piece_ref in enumerate(piece_refs):
        rows = piece_ref.shape[0]
        last = step == len(piece_refs) - 1
        first_row = pl.multiple_of(place_ref[0], rows) if last else 0
        first_col = pl.multiple_of(place_ref[1 + step] * BLOCK, BLOCK)
        piece_ref[...] = inputs_ref[pl.ds(first_row, rows), pl.ds(first_col, BLOCK)]


def ring_band(position, bands):
    position = (position + 2 * bands) % bands
    return jnp.where(position < bands // 2, 2 * position, 2 * (bands - 1 - position) + 1)


def tile_kernel(place_ref, own_ref, *refs):
    hops = len(OFFSETS[0])
    near_refs, far_refs = refs[:hops], refs[hops : 2 * hops]
    cot_refs = refs[2 * hops : -3]
    partial_ref, band_ref, cot_ref = refs[-3:]
    plane, band, spot = place_ref[0], place_ref[1], place_ref[2]
    tokens = own_ref.shape[0]

    def put(to_ref, piece_ref, source, part):
        rows = piece_ref.shape[0]
        first_row = pl.multiple_of(source * tokens + part * rows, rows)
        to_ref[pl.ds(first_row, rows), :] = piece_ref[...]

    put(band_ref, own_ref, band, 0)
    for hop in range(hops):
        last = hop == hops - 1
        for piece_ref, member in ((near_refs[hop], plane), (far_refs[hop], 1 - plane)):
            offset = jnp.where(member == 0, OFFSETS[0][hop], OFFSETS[1][hop])
            put(band_ref, piece_ref, band ^ offset, member if last else 0)
    for step, piece_ref in enumerate(cot_refs):
        put(cot_ref, piece_ref, ring_band(spot - step, len(cot_refs)), 0)
    partial_ref[...] = contract(band_ref[...], cot_ref[...], 0, 0)


def update_kernel(side_ref, mine_ref, other_ref, tile_ref, near_ref, far_ref):
    rows, far_rows = near_ref.shape[0], far_ref.shape[0]
    tile = tile_ref[...]
    core, plane = side_ref[0], side_ref[1]

    def write(left_ref, right_ref):
        for out_ref, first_row in (
            (near_ref, plane * rows),
            (far_ref, (1 - plane) * rows + core * far_rows),
        ):
            count = out_ref.shape[0]
            left = left_ref[pl.ds(pl.multiple_of(first_row, count), count), :]
            half = contract(left, tile, 1, 0).astype(jnp.bfloat16)
            piece = contract(half, right_ref[...], 1, 0) * math.sqrt(BLOCK)
            out_ref[...] = piece.astype(jnp.bfloat16)

    @pl.when(core == 0)
    def _():
        write(mine_ref, other_ref)

    @pl.when(core != 0)
    def _():
        write(other_ref, mine_ref)


def place_kernel(place_ref, *refs):
    hops = (len(refs) - 4) // 4
    update_ref, sems = refs[-2:]
    core, plane, spot = place_ref[0], place_ref[1], place_ref[2]
    bands = update_ref.shape[0]
    ahead = 1 - 2 * core
    copies = []

    def put(piece_ref, position, part, chunk):
        rows = piece_ref.shape[0]
        member = plane if chunk == 0 else 1 - plane
        first_row = pl.multiple_of(part * rows, rows)
        first_col = pl.multiple_of(member * BLOCK, BLOCK)
        to_ref = update_ref.at[
            ring_band(position, bands), pl.ds(first_row, rows), pl.ds(first_col, BLOCK)
        ]
        copy = pltpu.make_async_copy(piece_ref, to_ref, sems.at[len(copies)])
        copy.start()
        copies.append(copy)

    for chunk in range(2):
        put(refs[chunk], spot, 0, chunk)
    for hop in range(1, hops + 1):
        last = hop == hops
        for chunk in range(2):
            mine_ref, other_ref = refs[2 + 4 * (hop - 1) + 2 * chunk :][:2]
            put(mine_ref, spot - ahead * hop, core if last else 0, chunk)
            put(other_ref, spot + ahead * hop, 1 - core if last else 0, chunk)
    for copy in copies:
        copy.wait()


def call(kernel, out_shapes, scratch_shapes, *operands):
    in_specs = [pl.BlockSpec(memory_space=pltpu.SMEM)]
    in_specs += [pl.BlockSpec(memory_space=pltpu.VMEM)] * (len(operands) - 1)
    return pl.pallas_call(
        kernel,
        out_shape=out_shapes,
        in_specs=in_specs,
        out_specs=[pl.BlockSpec(memory_space=pltpu.VMEM)] * len(out_shapes),
        scratch_shapes=scratch_shapes,
        compiler_params=pltpu.CompilerParams(vmem_limit_bytes=32 * 1024 * 1024),
    )(*operands)


def on_device_paired(inputs, weight, cotangent):
    bands = D // BLOCK
    groups = lax.axis_size("dp")
    cores = groups // bands
    members = lax.axis_size("pre")
    core = lax.axis_index("dp") % cores
    band = lax.axis_index("dp") // cores
    plane = lax.axis_index("pre")
    tokens = inputs.shape[0]
    spot = jnp.where(band % 2 == 0, band // 2, bands - 1 - band // 2)

    ring = list(range(0, bands, 2)) + list(range(bands - 1, 0, -2))

    def shift(array, distance):
        pairs = [
            (ring[k] * cores + c, ring[(k + distance) % bands] * cores + c)
            for k in range(bands)
            for c in range(cores)
        ]
        return lax.ppermute(array, "dp", pairs)

    def swap_core(array):
        return lax.ppermute(array, "dp", [(g, g ^ 1) for g in range(groups)])

    def swap_plane(array):
        return lax.ppermute(array, "pre", [(c, members - 1 - c) for c in range(members)])

    def deal(array, hop):
        pairs = [
            (
                (k * cores + c) * members + m,
                ((k ^ OFFSETS[m][hop]) * cores + c) * members + m,
            )
            for k in range(bands)
            for c in range(cores)
            for m in range(members)
        ]
        return lax.ppermute(array, ("dp", "pre"), pairs)

    hops = range(len(OFFSETS[0]))
    bands_out = [band ^ jnp.where(plane == 0, OFFSETS[0][hop], OFFSETS[1][hop]) for hop in hops]
    own_band, *packed = call(
        pack_kernel,
        [jax.ShapeDtypeStruct((tokens, BLOCK), inputs.dtype)] * len(hops)
        + [jax.ShapeDtypeStruct((tokens // 2, BLOCK), inputs.dtype)],
        [],
        jnp.stack([plane * (tokens // 2), band] + bands_out).astype(jnp.int32),
        inputs,
    )
    near = [deal(piece, hop) for hop, piece in zip(hops, packed)]
    cots = [cotangent] + [None] * (bands - 1)
    for step in range(1, bands // 2 + 1):
        behind, further = cots[step - 1], cots[(bands - step + 1) % bands]
        if step == 3:
            behind, further, near[0] = lax.optimization_barrier((behind, further, near[0]))
        cots[step] = shift(behind, 1)
        if step < bands // 2:
            cots[bands - step] = shift(further, -1)
    far = [swap_plane(piece) for piece in near]
    outputs = jnp.dot(inputs, weight, preferred_element_type=jnp.float32).astype(jnp.bfloat16)
    own_band, outputs = lax.optimization_barrier((own_band, outputs))
    (partial_tile,) = call(
        tile_kernel,
        [jax.ShapeDtypeStruct((BLOCK, BLOCK), jnp.float32)],
        [pltpu.VMEM((bands * tokens, BLOCK), inputs.dtype)] * 2,
        jnp.stack([plane, band, spot]).astype(jnp.int32),
        own_band,
        *near,
        *far,
        *cots,
    )
    other_partial = swap_core(partial_tile)
    side = jnp.stack([core, plane]).astype(jnp.int32)
    tile_half, root = call(
        newton_kernel,
        [
            jax.ShapeDtypeStruct((BLOCK, BLOCK), jnp.bfloat16),
            jax.ShapeDtypeStruct((BLOCK, BLOCK), jnp.bfloat16),
        ],
        [pltpu.VMEM((BLOCK, BLOCK), jnp.float32)],
        side,
        partial_tile,
        other_partial,
    )
    other_root = swap_core(root)
    rows = BLOCK // members
    near_piece, far_piece = call(
        update_kernel,
        [
            jax.ShapeDtypeStruct((rows, BLOCK), jnp.bfloat16),
            jax.ShapeDtypeStruct((rows // cores, BLOCK), jnp.bfloat16),
        ],
        [],
        side,
        root,
        other_root,
        tile_half,
    )

    def turn(array):
        pairs = [
            (ring[k] * cores + c, ring[(k + 1 - 2 * c) % bands] * cores + c)
            for k in range(bands)
            for c in range(cores)
        ]
        return lax.ppermute(array, "dp", pairs)

    half_way = bands // 2
    crossed = swap_plane(far_piece)
    other_crossed = swap_core(crossed)
    far_head = jnp.where(
        core == 0,
        jnp.concatenate([crossed, other_crossed]),
        jnp.concatenate([other_crossed, crossed]),
    )
    heads = [near_piece, far_head]
    pieces = list(heads)
    for hop in range(1, half_way + 1):
        for chunk in range(2):
            head = heads[chunk]
            if hop == half_way:
                head = lax.dynamic_slice_in_dim(head.reshape(2, -1, BLOCK), core, 1, 0)[0]
            heads[chunk] = turn(head)
            pieces += [heads[chunk], swap_core(heads[chunk])]
    update = pl.pallas_call(
        place_kernel,
        out_shape=jax.ShapeDtypeStruct((bands, rows, CB * BLOCK), jnp.bfloat16),
        in_specs=[pl.BlockSpec(memory_space=pltpu.SMEM)]
        + [pl.BlockSpec(memory_space=pl.ANY)] * len(pieces),
        out_specs=pl.BlockSpec(memory_space=pl.ANY),
        scratch_shapes=[pltpu.SemaphoreType.DMA((len(pieces),))],
        compiler_params=pltpu.CompilerParams(vmem_limit_bytes=1024 * 1024),
    )(jnp.stack([core, plane, spot]).astype(jnp.int32), *pieces)
    return (outputs, update)


def solution(mesh):
    placed = (P("dp", None), P(None, "pre"), P("dp", "pre"))
    paired = mesh.shape["dp"] == 2 * D // BLOCK and mesh.shape["pre"] == CB == 2
    return jax.shard_map(
        on_device_paired if paired else on_device_general,
        mesh=mesh,
        in_specs=placed,
        out_specs=(P("dp", "pre"), P(None, "pre", None)),
        check_vma=False,
    )
```

```python
import functools
import math

import jax
import jax.numpy as jnp
from jax import lax
from jax.experimental import pallas as pl
from jax.experimental.pallas import tpu as pltpu
from jax.sharding import PartitionSpec as P

D = 4096
BLOCK = 512
CB = 2
ITERS = 3


DAMPING = 0.1
HIGH = lax.Precision.HIGHEST


def batch_dot(former, latter):
    return jnp.einsum(
        "sij,sjk->sik", former, latter, precision=HIGH, preferred_element_type=jnp.float32
    )


def on_device_general(inputs, weight, cotangent):
    groups = lax.axis_size("dp")
    members = lax.axis_size("pre")
    group_id = lax.axis_index("dp")
    member_id = lax.axis_index("pre")
    slab_rows = BLOCK // members
    blocks_all = D // BLOCK * CB
    rounds = max(1, blocks_all // groups)
    sharers = max(1, groups // blocks_all)
    col_width = BLOCK // sharers
    copy_id = group_id // blocks_all
    outputs = jnp.dot(inputs, weight, preferred_element_type=jnp.float32).astype(jnp.bfloat16)
    partial_value = lax.dot_general(
        inputs, cotangent, (((0,), (0,)), ((), ())), preferred_element_type=jnp.float32
    )
    owned_ids = (group_id + groups * jnp.arange(rounds, dtype=jnp.int32)) % blocks_all
    row_offsets = owned_ids // CB * BLOCK
    col_offsets = owned_ids % CB * BLOCK
    gradient = lax.psum(partial_value, "dp")
    row_bands = jax.vmap(lambda offset: lax.dynamic_slice_in_dim(gradient, offset, BLOCK, 0))(
        row_offsets
    )
    wide_band = lax.all_gather(row_bands, "pre", axis=2, tiled=True)
    tile_grad = jax.vmap(
        lambda row_band, offset: lax.dynamic_slice_in_dim(row_band, offset, BLOCK, 1)
    )(wide_band, col_offsets)
    first_row = member_id * slab_rows
    own_rows = lax.dynamic_slice_in_dim(tile_grad, first_row, slab_rows, 1)
    own_cols = lax.dynamic_slice_in_dim(tile_grad, first_row, slab_rows, 2)
    left_rows = jnp.einsum(
        "sij,skj->sik", own_rows, tile_grad, precision=HIGH, preferred_element_type=jnp.float32
    )
    right_rows = jnp.einsum(
        "sji,sjk->sik", own_cols, tile_grad, precision=HIGH, preferred_element_type=jnp.float32
    )
    stat_rows = jnp.stack([left_rows, right_rows], axis=1).reshape(rounds * 2, slab_rows, BLOCK)
    tile_energy = jnp.sum(tile_grad * tile_grad, axis=(1, 2))
    energy = jnp.stack([tile_energy, tile_energy], axis=1).reshape(rounds * 2)
    unit_rows = (jnp.arange(BLOCK)[None, :] == (first_row + jnp.arange(slab_rows))[:, None]).astype(
        jnp.float32
    )
    unit_eye = jnp.eye(BLOCK, dtype=jnp.float32)
    state_rows = stat_rows + (DAMPING * energy / BLOCK)[:, None, None] * unit_rows[None]
    root_rows = unit_rows[None]
    for iteration in range(ITERS):
        full_state = lax.all_gather(state_rows, "pre", axis=1, tiled=True)
        if iteration == 0:
            frob_norm = jnp.sqrt(jnp.sum(full_state * full_state, axis=(1, 2)))
            full_state = full_state / frob_norm[:, None, None]
            state_rows = state_rows / frob_norm[:, None, None]
            root_rows = unit_rows[None] * (frob_norm ** (-0.25))[:, None, None]
        factor = (5.0 * unit_eye - full_state) * 0.25
        square = batch_dot(factor, factor)
        square_rows = lax.dynamic_slice_in_dim(square, first_row, slab_rows, 1)
        fourth_rows = batch_dot(square_rows, square)
        state_rows = batch_dot(fourth_rows, full_state)
        root_rows = batch_dot(root_rows, factor)
    root_half = root_rows.astype(jnp.bfloat16).reshape(rounds, 2, slab_rows, BLOCK)
    right_full = lax.all_gather(root_half[:, 1], "pre", axis=1, tiled=True)
    right_cols = lax.dynamic_slice_in_dim(right_full, copy_id * col_width, col_width, 2)
    tile_half = tile_grad.astype(jnp.bfloat16)
    half_prod = jnp.einsum(
        "sij,sjk->sik", root_half[:, 0], tile_half, preferred_element_type=jnp.float32
    ).astype(jnp.bfloat16)
    piece_rows = jnp.einsum(
        "sij,sjk->sik", half_prod, right_cols, preferred_element_type=jnp.float32
    )
    piece_rows = (piece_rows * math.sqrt(BLOCK)).astype(jnp.bfloat16)
    collected = lax.all_gather(piece_rows[None], "dp", axis=0, tiled=True)
    if sharers == 1:
        ordered = jnp.swapaxes(collected, 0, 1).reshape(blocks_all, slab_rows, BLOCK)
    else:
        ordered = (
            collected[:, 0]
            .reshape(sharers, blocks_all, slab_rows, col_width)
            .transpose(1, 2, 0, 3)
            .reshape(blocks_all, slab_rows, BLOCK)
        )
    update = (
        ordered.reshape(D // BLOCK, CB, slab_rows, BLOCK)
        .transpose(0, 2, 1, 3)
        .reshape(D // BLOCK, slab_rows, CB * BLOCK)
    )
    return (outputs, update)


def contract(former, latter, former_dim, latter_dim):
    return lax.dot_general(
        former,
        latter,
        (((former_dim,), (latter_dim,)), ((), ())),
        preferred_element_type=jnp.float32,
    )


def product(former, latter):
    return contract(former.astype(jnp.bfloat16), latter.astype(jnp.bfloat16), 1, 0)


def total(array):
    return jnp.sum(jnp.sum(array, axis=0, keepdims=True), axis=1, keepdims=True)


def newton_step(state):
    excess = product(state, state) * (1.0 / 16.0) - 0.625 * state
    growth = 3.125 * excess + product(excess, excess)
    return (625.0 / 256.0) * state + product(state, growth)


def newton_kernel(side_ref, mine_ref, other_ref, tile_ref, root_ref, stat_ref):
    tile = mine_ref[...] + other_ref[...]
    tile_half = tile.astype(jnp.bfloat16)
    tile_ref[...] = tile_half

    @pl.when(side_ref[0] == 0)
    def _():
        stat_ref[...] = contract(tile_half, tile_half, 1, 1)

    @pl.when(side_ref[0] != 0)
    def _():
        stat_ref[...] = contract(tile_half, tile_half, 0, 0)

    order = tile.shape[0]
    row_ids = lax.broadcasted_iota(jnp.int32, (order, order), 0)
    col_ids = lax.broadcasted_iota(jnp.int32, (order, order), 1)
    on_diagonal = row_ids == col_ids
    damp = (DAMPING / order) * total(tile * tile)
    matrix = stat_ref[...]
    matrix = jnp.where(on_diagonal, matrix + damp, matrix)
    norm = jnp.sqrt(total(matrix * matrix))
    first = matrix / norm
    second = newton_step(first)
    third = newton_step(second)
    cross = product(first, second) * (1.0 / 16.0) - (5.0 / 16.0) * (first + second)
    last = product(cross, third)
    root = 1.25 * cross - 0.25 * last - (25.0 / 64.0) * third
    root = jnp.where(on_diagonal, root + 125.0 / 64.0, root)
    scale = 1.0 / jnp.sqrt(jnp.sqrt(norm))
    root_ref[...] = (root * scale).astype(jnp.bfloat16)


OFFSETS = ((4, 7, 1, 2), (5, 6, 3, 2))


def pack_kernel(place_ref, inputs_ref, *piece_refs):
    for step, piece_ref in enumerate(piece_refs):
        rows = piece_ref.shape[0]
        last = step == len(piece_refs) - 1
        first_row = pl.multiple_of(place_ref[0], rows) if last else 0
        first_col = pl.multiple_of(place_ref[1 + step] * BLOCK, BLOCK)
        piece_ref[...] = inputs_ref[pl.ds(first_row, rows), pl.ds(first_col, BLOCK)]


def ring_band(position, bands):
    position = (position + 2 * bands) % bands
    return jnp.where(position < bands // 2, 2 * position, 2 * (bands - 1 - position) + 1)


def tile_kernel(place_ref, own_ref, *refs):
    hops = len(OFFSETS[0])
    near_refs, far_refs = refs[:hops], refs[hops : 2 * hops]
    cot_refs = refs[2 * hops : -3]
    partial_ref, band_ref, cot_ref = refs[-3:]
    plane, band, spot = place_ref[0], place_ref[1], place_ref[2]
    tokens = own_ref.shape[0]

    def put(to_ref, piece_ref, source, part):
        rows = piece_ref.shape[0]
        first_row = pl.multiple_of(source * tokens + part * rows, rows)
        to_ref[pl.ds(first_row, rows), :] = piece_ref[...]

    put(band_ref, own_ref, band, 0)
    for hop in range(hops):
        last = hop == hops - 1
        for piece_ref, member in ((near_refs[hop], plane), (far_refs[hop], 1 - plane)):
            offset = jnp.where(member == 0, OFFSETS[0][hop], OFFSETS[1][hop])
            put(band_ref, piece_ref, band ^ offset, member if last else 0)
    for step, piece_ref in enumerate(cot_refs):
        put(cot_ref, piece_ref, ring_band(spot - step, len(cot_refs)), 0)
    partial_ref[...] = contract(band_ref[...], cot_ref[...], 0, 0)


def update_kernel(side_ref, mine_ref, other_ref, tile_ref, near_ref, far_ref):
    rows, far_rows = near_ref.shape[0], far_ref.shape[0]
    tile = tile_ref[...]
    core, plane = side_ref[0], side_ref[1]

    def write(left_ref, right_ref):
        for out_ref, first_row in (
            (near_ref, plane * rows),
            (far_ref, (1 - plane) * rows + core * far_rows),
        ):
            count = out_ref.shape[0]
            left = left_ref[pl.ds(pl.multiple_of(first_row, count), count), :]
            half = contract(left, tile, 1, 0).astype(jnp.bfloat16)
            piece = contract(half, right_ref[...], 1, 0) * math.sqrt(BLOCK)
            out_ref[...] = piece.astype(jnp.bfloat16)

    @pl.when(core == 0)
    def _():
        write(mine_ref, other_ref)

    @pl.when(core != 0)
    def _():
        write(other_ref, mine_ref)


def place_kernel(plan, place_ref, *refs):
    update_ref, sems = refs[-2:]
    pieces = refs[-2 - len(plan) : -2]
    core, plane, spot = place_ref[0], place_ref[1], place_ref[2]
    bands = update_ref.shape[0]
    ahead = 1 - 2 * core
    copies = []
    for index, (hop, chunk, other, half) in enumerate(plan):
        rows = pieces[index].shape[0]
        member = plane if chunk == 0 else 1 - plane
        position = spot + ahead * hop if other else spot - ahead * hop
        part = 0
        if half:
            part = 1 - core if other else core
        first_row = pl.multiple_of(part * rows, rows)
        first_col = pl.multiple_of(member * BLOCK, BLOCK)
        to_ref = update_ref.at[
            ring_band(position, bands), pl.ds(first_row, rows), pl.ds(first_col, BLOCK)
        ]
        copies.append(pltpu.make_async_copy(pieces[index], to_ref, sems.at[index]))
        copies[-1].start()
    for copy in copies:
        copy.wait()


def put_pieces(plan, shape, place, pieces, update=None):
    operands = ([] if update is None else [update]) + pieces
    return pl.pallas_call(
        functools.partial(place_kernel, plan),
        out_shape=jax.ShapeDtypeStruct(shape, jnp.bfloat16),
        in_specs=[pl.BlockSpec(memory_space=pltpu.SMEM)]
        + [pl.BlockSpec(memory_space=pl.ANY)] * len(operands),
        out_specs=pl.BlockSpec(memory_space=pl.ANY),
        scratch_shapes=[pltpu.SemaphoreType.DMA((len(pieces),))],
        input_output_aliases={} if update is None else {1: 0},
        compiler_params=pltpu.CompilerParams(vmem_limit_bytes=1024 * 1024),
    )(place, *operands)


def call(kernel, out_shapes, scratch_shapes, *operands):
    in_specs = [pl.BlockSpec(memory_space=pltpu.SMEM)]
    in_specs += [pl.BlockSpec(memory_space=pltpu.VMEM)] * (len(operands) - 1)
    return pl.pallas_call(
        kernel,
        out_shape=out_shapes,
        in_specs=in_specs,
        out_specs=[pl.BlockSpec(memory_space=pltpu.VMEM)] * len(out_shapes),
        scratch_shapes=scratch_shapes,
        compiler_params=pltpu.CompilerParams(vmem_limit_bytes=32 * 1024 * 1024),
    )(*operands)


def on_device_paired(inputs, weight, cotangent):
    bands = D // BLOCK
    groups = lax.axis_size("dp")
    cores = groups // bands
    members = lax.axis_size("pre")
    core = lax.axis_index("dp") % cores
    band = lax.axis_index("dp") // cores
    plane = lax.axis_index("pre")
    tokens = inputs.shape[0]
    spot = jnp.where(band % 2 == 0, band // 2, bands - 1 - band // 2)

    ring = list(range(0, bands, 2)) + list(range(bands - 1, 0, -2))

    def shift(array, distance):
        pairs = [
            (ring[k] * cores + c, ring[(k + distance) % bands] * cores + c)
            for k in range(bands)
            for c in range(cores)
        ]
        return lax.ppermute(array, "dp", pairs)

    def swap_core(array):
        return lax.ppermute(array, "dp", [(g, g ^ 1) for g in range(groups)])

    def swap_plane(array):
        return lax.ppermute(array, "pre", [(c, members - 1 - c) for c in range(members)])

    def deal(array, hop):
        pairs = [
            (
                (k * cores + c) * members + m,
                ((k ^ OFFSETS[m][hop]) * cores + c) * members + m,
            )
            for k in range(bands)
            for c in range(cores)
            for m in range(members)
        ]
        return lax.ppermute(array, ("dp", "pre"), pairs)

    hops = range(len(OFFSETS[0]))
    bands_out = [band ^ jnp.where(plane == 0, OFFSETS[0][hop], OFFSETS[1][hop]) for hop in hops]
    own_band, *packed = call(
        pack_kernel,
        [jax.ShapeDtypeStruct((tokens, BLOCK), inputs.dtype)] * len(hops)
        + [jax.ShapeDtypeStruct((tokens // 2, BLOCK), inputs.dtype)],
        [],
        jnp.stack([plane * (tokens // 2), band] + bands_out).astype(jnp.int32),
        inputs,
    )
    outputs = jnp.dot(inputs, weight, preferred_element_type=jnp.float32).astype(jnp.bfloat16)
    near = [deal(piece, hop) for hop, piece in zip(hops, packed)]
    cots = [cotangent] + [None] * (bands - 1)
    for step in range(1, bands // 2 + 1):
        behind, further = cots[step - 1], cots[(bands - step + 1) % bands]
        if step == 3:
            behind, further, near[0], outputs = lax.optimization_barrier(
                (behind, further, near[0], outputs)
            )
        cots[step] = shift(behind, 1)
        if step < bands // 2:
            cots[bands - step] = shift(further, -1)
    far = [swap_plane(piece) for piece in near]
    (partial_tile,) = call(
        tile_kernel,
        [jax.ShapeDtypeStruct((BLOCK, BLOCK), jnp.float32)],
        [pltpu.VMEM((bands * tokens, BLOCK), inputs.dtype)] * 2,
        jnp.stack([plane, band, spot]).astype(jnp.int32),
        own_band,
        *near,
        *far,
        *cots,
    )
    other_partial = swap_core(partial_tile)
    side = jnp.stack([core, plane]).astype(jnp.int32)
    tile_half, root = call(
        newton_kernel,
        [
            jax.ShapeDtypeStruct((BLOCK, BLOCK), jnp.bfloat16),
            jax.ShapeDtypeStruct((BLOCK, BLOCK), jnp.bfloat16),
        ],
        [pltpu.VMEM((BLOCK, BLOCK), jnp.float32)],
        side,
        partial_tile,
        other_partial,
    )
    other_root = swap_core(root)
    rows = BLOCK // members
    near_piece, far_piece = call(
        update_kernel,
        [
            jax.ShapeDtypeStruct((rows, BLOCK), jnp.bfloat16),
            jax.ShapeDtypeStruct((rows // cores, BLOCK), jnp.bfloat16),
        ],
        [],
        side,
        root,
        other_root,
        tile_half,
    )

    def turn(array):
        pairs = [
            (ring[k] * cores + c, ring[(k + 1 - 2 * c) % bands] * cores + c)
            for k in range(bands)
            for c in range(cores)
        ]
        return lax.ppermute(array, "dp", pairs)

    half_way = bands // 2
    crossed, first_turn = lax.optimization_barrier((swap_plane(far_piece), turn(near_piece)))
    other_crossed = swap_core(crossed)
    far_head = jnp.where(
        core == 0,
        jnp.concatenate([crossed, other_crossed]),
        jnp.concatenate([other_crossed, crossed]),
    )
    heads = [near_piece, far_head]
    plan, pieces = [(0, 0, False, False), (0, 1, False, False)], list(heads)
    place = jnp.stack([core, plane, spot]).astype(jnp.int32)
    shape = (bands, rows, CB * BLOCK)
    update = None
    for hop in range(1, half_way + 1):
        half = hop == half_way
        for chunk in range(2):
            head = heads[chunk]
            if half:
                head = lax.dynamic_slice_in_dim(head.reshape(2, -1, BLOCK), core, 1, 0)[0]
            heads[chunk] = first_turn if (hop, chunk) == (1, 0) else turn(head)
            pieces += [heads[chunk], swap_core(heads[chunk])]
            plan += [(hop, chunk, False, half), (hop, chunk, True, half)]
        if hop == half_way - 1:
            update = put_pieces(plan[:-4], shape, place, pieces[:-4])
            update, *heads = lax.optimization_barrier((update, *heads))
            plan, pieces = plan[-4:], pieces[-4:]
    update = put_pieces(plan, shape, place, pieces, update)
    return (outputs, update)


def solution(mesh):
    placed = (P("dp", None), P(None, "pre"), P("dp", "pre"))
    paired = mesh.shape["dp"] == 2 * D // BLOCK and mesh.shape["pre"] == CB == 2
    return jax.shard_map(
        on_device_paired if paired else on_device_general,
        mesh=mesh,
        in_specs=placed,
        out_specs=(P("dp", "pre"), P(None, "pre", None)),
        check_vma=False,
    )
```

```python
import functools
import math

import jax
import jax.numpy as jnp
from jax import lax
from jax.experimental import pallas as pl
from jax.experimental.pallas import tpu as pltpu
from jax.sharding import PartitionSpec as P

D = 4096
BLOCK = 512
CB = 2
ITERS = 3


DAMPING = 0.1
HIGH = lax.Precision.HIGHEST


def batch_dot(former, latter):
    return jnp.einsum(
        "sij,sjk->sik", former, latter, precision=HIGH, preferred_element_type=jnp.float32
    )


def on_device_general(inputs, weight, cotangent):
    groups = lax.axis_size("dp")
    members = lax.axis_size("pre")
    group_id = lax.axis_index("dp")
    member_id = lax.axis_index("pre")
    slab_rows = BLOCK // members
    blocks_all = D // BLOCK * CB
    rounds = max(1, blocks_all // groups)
    sharers = max(1, groups // blocks_all)
    col_width = BLOCK // sharers
    copy_id = group_id // blocks_all
    outputs = jnp.dot(inputs, weight, preferred_element_type=jnp.float32).astype(jnp.bfloat16)
    partial_value = lax.dot_general(
        inputs, cotangent, (((0,), (0,)), ((), ())), preferred_element_type=jnp.float32
    )
    owned_ids = (group_id + groups * jnp.arange(rounds, dtype=jnp.int32)) % blocks_all
    row_offsets = owned_ids // CB * BLOCK
    col_offsets = owned_ids % CB * BLOCK
    gradient = lax.psum(partial_value, "dp")
    row_bands = jax.vmap(lambda offset: lax.dynamic_slice_in_dim(gradient, offset, BLOCK, 0))(
        row_offsets
    )
    wide_band = lax.all_gather(row_bands, "pre", axis=2, tiled=True)
    tile_grad = jax.vmap(
        lambda row_band, offset: lax.dynamic_slice_in_dim(row_band, offset, BLOCK, 1)
    )(wide_band, col_offsets)
    first_row = member_id * slab_rows
    own_rows = lax.dynamic_slice_in_dim(tile_grad, first_row, slab_rows, 1)
    own_cols = lax.dynamic_slice_in_dim(tile_grad, first_row, slab_rows, 2)
    left_rows = jnp.einsum(
        "sij,skj->sik", own_rows, tile_grad, precision=HIGH, preferred_element_type=jnp.float32
    )
    right_rows = jnp.einsum(
        "sji,sjk->sik", own_cols, tile_grad, precision=HIGH, preferred_element_type=jnp.float32
    )
    stat_rows = jnp.stack([left_rows, right_rows], axis=1).reshape(rounds * 2, slab_rows, BLOCK)
    tile_energy = jnp.sum(tile_grad * tile_grad, axis=(1, 2))
    energy = jnp.stack([tile_energy, tile_energy], axis=1).reshape(rounds * 2)
    unit_rows = (jnp.arange(BLOCK)[None, :] == (first_row + jnp.arange(slab_rows))[:, None]).astype(
        jnp.float32
    )
    unit_eye = jnp.eye(BLOCK, dtype=jnp.float32)
    state_rows = stat_rows + (DAMPING * energy / BLOCK)[:, None, None] * unit_rows[None]
    root_rows = unit_rows[None]
    for iteration in range(ITERS):
        full_state = lax.all_gather(state_rows, "pre", axis=1, tiled=True)
        if iteration == 0:
            frob_norm = jnp.sqrt(jnp.sum(full_state * full_state, axis=(1, 2)))
            full_state = full_state / frob_norm[:, None, None]
            state_rows = state_rows / frob_norm[:, None, None]
            root_rows = unit_rows[None] * (frob_norm ** (-0.25))[:, None, None]
        factor = (5.0 * unit_eye - full_state) * 0.25
        square = batch_dot(factor, factor)
        square_rows = lax.dynamic_slice_in_dim(square, first_row, slab_rows, 1)
        fourth_rows = batch_dot(square_rows, square)
        state_rows = batch_dot(fourth_rows, full_state)
        root_rows = batch_dot(root_rows, factor)
    root_half = root_rows.astype(jnp.bfloat16).reshape(rounds, 2, slab_rows, BLOCK)
    right_full = lax.all_gather(root_half[:, 1], "pre", axis=1, tiled=True)
    right_cols = lax.dynamic_slice_in_dim(right_full, copy_id * col_width, col_width, 2)
    tile_half = tile_grad.astype(jnp.bfloat16)
    half_prod = jnp.einsum(
        "sij,sjk->sik", root_half[:, 0], tile_half, preferred_element_type=jnp.float32
    ).astype(jnp.bfloat16)
    piece_rows = jnp.einsum(
        "sij,sjk->sik", half_prod, right_cols, preferred_element_type=jnp.float32
    )
    piece_rows = (piece_rows * math.sqrt(BLOCK)).astype(jnp.bfloat16)
    collected = lax.all_gather(piece_rows[None], "dp", axis=0, tiled=True)
    if sharers == 1:
        ordered = jnp.swapaxes(collected, 0, 1).reshape(blocks_all, slab_rows, BLOCK)
    else:
        ordered = (
            collected[:, 0]
            .reshape(sharers, blocks_all, slab_rows, col_width)
            .transpose(1, 2, 0, 3)
            .reshape(blocks_all, slab_rows, BLOCK)
        )
    update = (
        ordered.reshape(D // BLOCK, CB, slab_rows, BLOCK)
        .transpose(0, 2, 1, 3)
        .reshape(D // BLOCK, slab_rows, CB * BLOCK)
    )
    return (outputs, update)


def contract(former, latter, former_dim, latter_dim):
    return lax.dot_general(
        former,
        latter,
        (((former_dim,), (latter_dim,)), ((), ())),
        preferred_element_type=jnp.float32,
    )


def product(former, latter):
    return contract(former.astype(jnp.bfloat16), latter.astype(jnp.bfloat16), 1, 0)


def total(array):
    return jnp.sum(jnp.sum(array, axis=0, keepdims=True), axis=1, keepdims=True)


def newton_step(state):
    excess = product(state, state) * (1.0 / 16.0) - 0.625 * state
    growth = 3.125 * excess + product(excess, excess)
    return (625.0 / 256.0) * state + product(state, growth)


def newton_kernel(side_ref, mine_ref, other_ref, tile_ref, root_ref, stat_ref):
    tile = mine_ref[...] + other_ref[...]
    tile_half = tile.astype(jnp.bfloat16)
    tile_ref[...] = tile_half

    @pl.when(side_ref[0] == 0)
    def _():
        stat_ref[...] = contract(tile_half, tile_half, 1, 1)

    @pl.when(side_ref[0] != 0)
    def _():
        stat_ref[...] = contract(tile_half, tile_half, 0, 0)

    order = tile.shape[0]
    row_ids = lax.broadcasted_iota(jnp.int32, (order, order), 0)
    col_ids = lax.broadcasted_iota(jnp.int32, (order, order), 1)
    on_diagonal = row_ids == col_ids
    damp = (DAMPING / order) * total(tile * tile)
    matrix = stat_ref[...]
    matrix = jnp.where(on_diagonal, matrix + damp, matrix)
    norm = jnp.sqrt(total(matrix * matrix))
    first = matrix / norm
    second = newton_step(first)
    third = newton_step(second)
    cross = product(first, second) * (1.0 / 16.0) - (5.0 / 16.0) * (first + second)
    last = product(cross, third)
    root = 1.25 * cross - 0.25 * last - (25.0 / 64.0) * third
    root = jnp.where(on_diagonal, root + 125.0 / 64.0, root)
    scale = 1.0 / jnp.sqrt(jnp.sqrt(norm))
    root_ref[...] = (root * scale).astype(jnp.bfloat16)


OFFSETS = ((4, 7, 1, 2), (5, 6, 3, 2))


def pack_kernel(place_ref, inputs_ref, *piece_refs):
    for step, piece_ref in enumerate(piece_refs):
        rows = piece_ref.shape[0]
        last = step == len(piece_refs) - 1
        first_row = pl.multiple_of(place_ref[0], rows) if last else 0
        first_col = pl.multiple_of(place_ref[1 + step] * BLOCK, BLOCK)
        piece_ref[...] = inputs_ref[pl.ds(first_row, rows), pl.ds(first_col, BLOCK)]


def ring_band(position, bands):
    position = (position + 2 * bands) % bands
    return jnp.where(position < bands // 2, 2 * position, 2 * (bands - 1 - position) + 1)


def tile_kernel(place_ref, own_ref, *refs):
    hops = len(OFFSETS[0])
    near_refs, far_refs = refs[:hops], refs[hops : 2 * hops]
    cot_refs = refs[2 * hops : -3]
    partial_ref, band_ref, cot_ref = refs[-3:]
    plane, band = place_ref[0], place_ref[1]
    tokens = own_ref.shape[0]

    def put(to_ref, piece_ref, source, part):
        rows = piece_ref.shape[0]
        first_row = pl.multiple_of(source * tokens + part * rows, rows)
        to_ref[pl.ds(first_row, rows), :] = piece_ref[...]

    put(band_ref, own_ref, band, 0)
    for hop in range(hops):
        last = hop == hops - 1
        for piece_ref, member in ((near_refs[hop], plane), (far_refs[hop], 1 - plane)):
            offset = jnp.where(member == 0, OFFSETS[0][hop], OFFSETS[1][hop])
            put(band_ref, piece_ref, band ^ offset, member if last else 0)
    for offset, pair_ref in enumerate(cot_refs):
        for part, source in enumerate((band ^ offset, band ^ offset ^ 4)):
            put(cot_ref, pair_ref.at[pl.ds(part * tokens, tokens)], source, 0)
    partial_ref[...] = contract(band_ref[...], cot_ref[...], 0, 0)


def update_kernel(side_ref, mine_ref, other_ref, tile_ref, near_ref, far_ref):
    rows, far_rows = near_ref.shape[0], far_ref.shape[0]
    tile = tile_ref[...]
    core, plane = side_ref[0], side_ref[1]

    def write(left_ref, right_ref):
        for out_ref, first_row in (
            (near_ref, plane * rows),
            (far_ref, (1 - plane) * rows + core * far_rows),
        ):
            count = out_ref.shape[0]
            left = left_ref[pl.ds(pl.multiple_of(first_row, count), count), :]
            half = contract(left, tile, 1, 0).astype(jnp.bfloat16)
            piece = contract(half, right_ref[...], 1, 0) * math.sqrt(BLOCK)
            out_ref[...] = piece.astype(jnp.bfloat16)

    @pl.when(core == 0)
    def _():
        write(mine_ref, other_ref)

    @pl.when(core != 0)
    def _():
        write(other_ref, mine_ref)


WHOLE, MINE, OTHERS = 0, 1, -1


def place_kernel(plan, place_ref, *refs):
    pieces = refs[: len(plan)]
    update_ref, sems = refs[len(plan) :]
    core, plane, spot = place_ref[0], place_ref[1], place_ref[2]
    bands = update_ref.shape[0]
    ahead = 1 - 2 * core
    copies = []
    for index, (hop, chunk, other, part) in enumerate(plan):
        rows = pieces[index].shape[0]
        member = plane if chunk == 0 else 1 - plane
        position = spot + ahead * hop if other else spot - ahead * hop
        number = {WHOLE: 0, MINE: core, OTHERS: 1 - core}[part]
        first_row = pl.multiple_of(number * rows, rows)
        first_col = pl.multiple_of(member * BLOCK, BLOCK)
        to_ref = update_ref.at[
            ring_band(position, bands), pl.ds(first_row, rows), pl.ds(first_col, BLOCK)
        ]
        copies.append(pltpu.make_async_copy(pieces[index], to_ref, sems.at[index]))
        copies[-1].start()
    for copy in copies:
        copy.wait()


def put_pieces(plan, shape, place, pieces):
    return pl.pallas_call(
        functools.partial(place_kernel, plan),
        out_shape=jax.ShapeDtypeStruct(shape, jnp.bfloat16),
        in_specs=[pl.BlockSpec(memory_space=pltpu.SMEM)]
        + [pl.BlockSpec(memory_space=pl.ANY)] * len(pieces),
        out_specs=pl.BlockSpec(memory_space=pl.ANY),
        scratch_shapes=[pltpu.SemaphoreType.DMA((len(pieces),))],
        compiler_params=pltpu.CompilerParams(vmem_limit_bytes=1024 * 1024),
    )(place, *pieces)


def call(kernel, out_shapes, scratch_shapes, *operands):
    in_specs = [pl.BlockSpec(memory_space=pltpu.SMEM)]
    in_specs += [pl.BlockSpec(memory_space=pltpu.VMEM)] * (len(operands) - 1)
    return pl.pallas_call(
        kernel,
        out_shape=out_shapes,
        in_specs=in_specs,
        out_specs=[pl.BlockSpec(memory_space=pltpu.VMEM)] * len(out_shapes),
        scratch_shapes=scratch_shapes,
        compiler_params=pltpu.CompilerParams(vmem_limit_bytes=32 * 1024 * 1024),
    )(*operands)


def on_device_paired(inputs, weight, cotangent):
    bands = D // BLOCK
    groups = lax.axis_size("dp")
    cores = groups // bands
    members = lax.axis_size("pre")
    core = lax.axis_index("dp") % cores
    band = lax.axis_index("dp") // cores
    plane = lax.axis_index("pre")
    tokens = inputs.shape[0]
    spot = jnp.where(band % 2 == 0, band // 2, bands - 1 - band // 2)

    ring = list(range(0, bands, 2)) + list(range(bands - 1, 0, -2))

    def swap_core(array):
        return lax.ppermute(array, "dp", [(g, g ^ 1) for g in range(groups)])

    def swap_plane(array):
        return lax.ppermute(array, "pre", [(c, members - 1 - c) for c in range(members)])

    def deal(array, hop):
        pairs = [
            (
                (k * cores + c) * members + m,
                ((k ^ OFFSETS[m][hop]) * cores + c) * members + m,
            )
            for k in range(bands)
            for c in range(cores)
            for m in range(members)
        ]
        return lax.ppermute(array, ("dp", "pre"), pairs)

    hops = range(len(OFFSETS[0]))
    bands_out = [band ^ jnp.where(plane == 0, OFFSETS[0][hop], OFFSETS[1][hop]) for hop in hops]
    own_band, *packed = call(
        pack_kernel,
        [jax.ShapeDtypeStruct((tokens, BLOCK), inputs.dtype)] * len(hops)
        + [jax.ShapeDtypeStruct((tokens // 2, BLOCK), inputs.dtype)],
        [],
        jnp.stack([plane * (tokens // 2), band] + bands_out).astype(jnp.int32),
        inputs,
    )
    def exchange(array, offset):
        pairs = [
            (k * cores + c, (k ^ offset) * cores + c) for k in range(bands) for c in range(cores)
        ]
        return lax.ppermute(array, "dp", pairs)

    outputs = jnp.dot(inputs, weight, preferred_element_type=jnp.float32).astype(jnp.bfloat16)
    far_cot, outputs, packed = lax.optimization_barrier((exchange(cotangent, 4), outputs, packed))
    pair = jnp.concatenate([cotangent, far_cot])
    near = [deal(packed[0], 0), deal(packed[1], 1)]
    next_pair, packed = lax.optimization_barrier((exchange(pair, 2), packed))
    cots = [pair, exchange(pair, 1), next_pair, exchange(next_pair, 1)]
    near += [deal(packed[2], 2), deal(packed[3], 3)]
    far = [swap_plane(piece) for piece in near]
    (partial_tile,) = call(
        tile_kernel,
        [jax.ShapeDtypeStruct((BLOCK, BLOCK), jnp.float32)],
        [pltpu.VMEM((bands * tokens, BLOCK), inputs.dtype)] * 2,
        jnp.stack([plane, band]).astype(jnp.int32),
        own_band,
        *near,
        *far,
        *cots,
    )
    other_partial = swap_core(partial_tile)
    side = jnp.stack([core, plane]).astype(jnp.int32)
    tile_half, root = call(
        newton_kernel,
        [
            jax.ShapeDtypeStruct((BLOCK, BLOCK), jnp.bfloat16),
            jax.ShapeDtypeStruct((BLOCK, BLOCK), jnp.bfloat16),
        ],
        [pltpu.VMEM((BLOCK, BLOCK), jnp.float32)],
        side,
        partial_tile,
        other_partial,
    )
    other_root = swap_core(root)
    rows = BLOCK // members
    near_piece, far_piece = call(
        update_kernel,
        [
            jax.ShapeDtypeStruct((rows, BLOCK), jnp.bfloat16),
            jax.ShapeDtypeStruct((rows // cores, BLOCK), jnp.bfloat16),
        ],
        [],
        side,
        root,
        other_root,
        tile_half,
    )

    def turn(array):
        pairs = [
            (ring[k] * cores + c, ring[(k + 1 - 2 * c) % bands] * cores + c)
            for k in range(bands)
            for c in range(cores)
        ]
        return lax.ppermute(array, "dp", pairs)

    half_way = bands // 2
    near_turned, crossed = lax.optimization_barrier((turn(near_piece), swap_plane(far_piece)))
    other_crossed = swap_core(crossed)
    heads = [near_piece, crossed, other_crossed]
    parts = [WHOLE, MINE, OTHERS]
    plan = [(0, min(k, 1), False, parts[k]) for k in range(3)]
    pieces = list(heads)
    for hop in range(1, half_way + 1):
        for k, part in enumerate(parts):
            chunk = min(k, 1)
            if hop == half_way and part == OTHERS:
                continue
            if hop == half_way and part == WHOLE:
                heads[k] = lax.dynamic_slice_in_dim(heads[k].reshape(2, -1, BLOCK), core, 1, 0)[0]
                part = MINE
            heads[k] = near_turned if (hop, k) == (1, 0) else turn(heads[k])
            pieces += [heads[k], swap_core(heads[k])]
            plan += [(hop, chunk, False, part), (hop, chunk, True, -part)]
    update = put_pieces(
        plan,
        (bands, rows, CB * BLOCK),
        jnp.stack([core, plane, spot]).astype(jnp.int32),
        pieces,
    )
    return (outputs, update)


def solution(mesh):
    placed = (P("dp", None), P(None, "pre"), P("dp", "pre"))
    paired = mesh.shape["dp"] == 2 * D // BLOCK and mesh.shape["pre"] == CB == 2
    return jax.shard_map(
        on_device_paired if paired else on_device_general,
        mesh=mesh,
        in_specs=placed,
        out_specs=(P("dp", "pre"), P(None, "pre", None)),
        check_vma=False,
    )
```

```python
import math

import jax
import jax.numpy as jnp
from jax import lax
from jax.experimental import pallas as pl
from jax.experimental.pallas import tpu as pltpu
from jax.sharding import PartitionSpec as P

D = 4096
BLOCK = 512
CB = 2
ITERS = 3


DAMPING = 0.1
HIGH = lax.Precision.HIGHEST


def batch_dot(former, latter):
    return jnp.einsum(
        "sij,sjk->sik", former, latter, precision=HIGH, preferred_element_type=jnp.float32
    )


def on_device_general(inputs, weight, cotangent):
    groups = lax.axis_size("dp")
    members = lax.axis_size("pre")
    group_id = lax.axis_index("dp")
    member_id = lax.axis_index("pre")
    slab_rows = BLOCK // members
    blocks_all = D // BLOCK * CB
    rounds = max(1, blocks_all // groups)
    sharers = max(1, groups // blocks_all)
    col_width = BLOCK // sharers
    copy_id = group_id // blocks_all
    outputs = jnp.dot(inputs, weight, preferred_element_type=jnp.float32).astype(jnp.bfloat16)
    partial_value = lax.dot_general(
        inputs, cotangent, (((0,), (0,)), ((), ())), preferred_element_type=jnp.float32
    )
    owned_ids = (group_id + groups * jnp.arange(rounds, dtype=jnp.int32)) % blocks_all
    row_offsets = owned_ids // CB * BLOCK
    col_offsets = owned_ids % CB * BLOCK
    gradient = lax.psum(partial_value, "dp")
    row_bands = jax.vmap(lambda offset: lax.dynamic_slice_in_dim(gradient, offset, BLOCK, 0))(
        row_offsets
    )
    wide_band = lax.all_gather(row_bands, "pre", axis=2, tiled=True)
    tile_grad = jax.vmap(
        lambda row_band, offset: lax.dynamic_slice_in_dim(row_band, offset, BLOCK, 1)
    )(wide_band, col_offsets)
    first_row = member_id * slab_rows
    own_rows = lax.dynamic_slice_in_dim(tile_grad, first_row, slab_rows, 1)
    own_cols = lax.dynamic_slice_in_dim(tile_grad, first_row, slab_rows, 2)
    left_rows = jnp.einsum(
        "sij,skj->sik", own_rows, tile_grad, precision=HIGH, preferred_element_type=jnp.float32
    )
    right_rows = jnp.einsum(
        "sji,sjk->sik", own_cols, tile_grad, precision=HIGH, preferred_element_type=jnp.float32
    )
    stat_rows = jnp.stack([left_rows, right_rows], axis=1).reshape(rounds * 2, slab_rows, BLOCK)
    tile_energy = jnp.sum(tile_grad * tile_grad, axis=(1, 2))
    energy = jnp.stack([tile_energy, tile_energy], axis=1).reshape(rounds * 2)
    unit_rows = (jnp.arange(BLOCK)[None, :] == (first_row + jnp.arange(slab_rows))[:, None]).astype(
        jnp.float32
    )
    unit_eye = jnp.eye(BLOCK, dtype=jnp.float32)
    state_rows = stat_rows + (DAMPING * energy / BLOCK)[:, None, None] * unit_rows[None]
    root_rows = unit_rows[None]
    for iteration in range(ITERS):
        full_state = lax.all_gather(state_rows, "pre", axis=1, tiled=True)
        if iteration == 0:
            frob_norm = jnp.sqrt(jnp.sum(full_state * full_state, axis=(1, 2)))
            full_state = full_state / frob_norm[:, None, None]
            state_rows = state_rows / frob_norm[:, None, None]
            root_rows = unit_rows[None] * (frob_norm ** (-0.25))[:, None, None]
        factor = (5.0 * unit_eye - full_state) * 0.25
        square = batch_dot(factor, factor)
        square_rows = lax.dynamic_slice_in_dim(square, first_row, slab_rows, 1)
        fourth_rows = batch_dot(square_rows, square)
        state_rows = batch_dot(fourth_rows, full_state)
        root_rows = batch_dot(root_rows, factor)
    root_half = root_rows.astype(jnp.bfloat16).reshape(rounds, 2, slab_rows, BLOCK)
    right_full = lax.all_gather(root_half[:, 1], "pre", axis=1, tiled=True)
    right_cols = lax.dynamic_slice_in_dim(right_full, copy_id * col_width, col_width, 2)
    tile_half = tile_grad.astype(jnp.bfloat16)
    half_prod = jnp.einsum(
        "sij,sjk->sik", root_half[:, 0], tile_half, preferred_element_type=jnp.float32
    ).astype(jnp.bfloat16)
    piece_rows = jnp.einsum(
        "sij,sjk->sik", half_prod, right_cols, preferred_element_type=jnp.float32
    )
    piece_rows = (piece_rows * math.sqrt(BLOCK)).astype(jnp.bfloat16)
    collected = lax.all_gather(piece_rows[None], "dp", axis=0, tiled=True)
    if sharers == 1:
        ordered = jnp.swapaxes(collected, 0, 1).reshape(blocks_all, slab_rows, BLOCK)
    else:
        ordered = (
            collected[:, 0]
            .reshape(sharers, blocks_all, slab_rows, col_width)
            .transpose(1, 2, 0, 3)
            .reshape(blocks_all, slab_rows, BLOCK)
        )
    update = (
        ordered.reshape(D // BLOCK, CB, slab_rows, BLOCK)
        .transpose(0, 2, 1, 3)
        .reshape(D // BLOCK, slab_rows, CB * BLOCK)
    )
    return (outputs, update)


def contract(former, latter, former_dim, latter_dim):
    return lax.dot_general(
        former,
        latter,
        (((former_dim,), (latter_dim,)), ((), ())),
        preferred_element_type=jnp.float32,
    )


def product(former, latter):
    return contract(former.astype(jnp.bfloat16), latter.astype(jnp.bfloat16), 1, 0)


def total(array):
    return jnp.sum(jnp.sum(array, axis=0, keepdims=True), axis=1, keepdims=True)


def newton_step(state):
    excess = product(state, state) * (1.0 / 16.0) - 0.625 * state
    growth = 3.125 * excess + product(excess, excess)
    return (625.0 / 256.0) * state + product(state, growth)


def newton_kernel(side_ref, mine_ref, other_ref, tile_ref, root_ref, stat_ref):
    tile = mine_ref[...] + other_ref[...]
    tile_half = tile.astype(jnp.bfloat16)
    tile_ref[...] = tile_half

    @pl.when(side_ref[0] == 0)
    def _():
        stat_ref[...] = contract(tile_half, tile_half, 1, 1)

    @pl.when(side_ref[0] != 0)
    def _():
        stat_ref[...] = contract(tile_half, tile_half, 0, 0)

    order = tile.shape[0]
    row_ids = lax.broadcasted_iota(jnp.int32, (order, order), 0)
    col_ids = lax.broadcasted_iota(jnp.int32, (order, order), 1)
    on_diagonal = row_ids == col_ids
    damp = (DAMPING / order) * total(tile * tile)
    matrix = stat_ref[...]
    matrix = jnp.where(on_diagonal, matrix + damp, matrix)
    norm = jnp.sqrt(total(matrix * matrix))
    first = matrix / norm
    second = newton_step(first)
    third = newton_step(second)
    cross = product(first, second) * (1.0 / 16.0) - (5.0 / 16.0) * (first + second)
    last = product(cross, third)
    root = 1.25 * cross - 0.25 * last - (25.0 / 64.0) * third
    root = jnp.where(on_diagonal, root + 125.0 / 64.0, root)
    scale = 1.0 / jnp.sqrt(jnp.sqrt(norm))
    root_ref[...] = (root * scale).astype(jnp.bfloat16)


OFFSETS = ((4, 7, 1, 2), (5, 6, 3, 2))


def pack_kernel(place_ref, inputs_ref, *piece_refs):
    for step, piece_ref in enumerate(piece_refs):
        rows = piece_ref.shape[0]
        last = step == len(piece_refs) - 1
        first_row = pl.multiple_of(place_ref[0], rows) if last else 0
        first_col = pl.multiple_of(place_ref[1 + step] * BLOCK, BLOCK)
        piece_ref[...] = inputs_ref[pl.ds(first_row, rows), pl.ds(first_col, BLOCK)]


def ring_band(position, bands):
    position = (position + 2 * bands) % bands
    return jnp.where(position < bands // 2, 2 * position, 2 * (bands - 1 - position) + 1)


def tile_kernel(place_ref, own_ref, *refs):
    hops = len(OFFSETS[0])
    near_refs, far_refs = refs[:hops], refs[hops : 2 * hops]
    cot_refs = refs[2 * hops : -3]
    partial_ref, band_ref, cot_ref = refs[-3:]
    plane, band = place_ref[0], place_ref[1]
    tokens = own_ref.shape[0]

    def put(to_ref, piece_ref, source, part):
        rows = piece_ref.shape[0]
        first_row = pl.multiple_of(source * tokens + part * rows, rows)
        to_ref[pl.ds(first_row, rows), :] = piece_ref[...]

    put(band_ref, own_ref, band, 0)
    for hop in range(hops):
        last = hop == hops - 1
        for piece_ref, member in ((near_refs[hop], plane), (far_refs[hop], 1 - plane)):
            offset = jnp.where(member == 0, OFFSETS[0][hop], OFFSETS[1][hop])
            put(band_ref, piece_ref, band ^ offset, member if last else 0)
    for offset, pair_ref in enumerate(cot_refs):
        for part, source in enumerate((band ^ offset, band ^ offset ^ 4)):
            put(cot_ref, pair_ref.at[pl.ds(part * tokens, tokens)], source, 0)
    partial_ref[...] = contract(band_ref[...], cot_ref[...], 0, 0)


def update_kernel(side_ref, mine_ref, other_ref, tile_ref, near_ref, next_ref, far_ref):
    rows = near_ref.shape[0]
    tile = tile_ref[...]
    core, plane = side_ref[0], side_ref[1]

    def write(left_ref, right_ref):
        for out_ref, part in (
            (near_ref, 2 * plane + core),
            (next_ref, 2 * plane + 1 - core),
            (far_ref, 2 * (1 - plane) + core),
        ):
            left = left_ref[pl.ds(pl.multiple_of(part * rows, rows), rows), :]
            half = contract(left, tile, 1, 0).astype(jnp.bfloat16)
            piece = contract(half, right_ref[...], 1, 0) * math.sqrt(BLOCK)
            out_ref[...] = piece.astype(jnp.bfloat16)

    @pl.when(core == 0)
    def _():
        write(mine_ref, other_ref)

    @pl.when(core != 0)
    def _():
        write(other_ref, mine_ref)


def call(kernel, out_shapes, scratch_shapes, *operands):
    in_specs = [pl.BlockSpec(memory_space=pltpu.SMEM)]
    in_specs += [pl.BlockSpec(memory_space=pltpu.VMEM)] * (len(operands) - 1)
    return pl.pallas_call(
        kernel,
        out_shape=out_shapes,
        in_specs=in_specs,
        out_specs=[pl.BlockSpec(memory_space=pltpu.VMEM)] * len(out_shapes),
        scratch_shapes=scratch_shapes,
        compiler_params=pltpu.CompilerParams(vmem_limit_bytes=32 * 1024 * 1024),
    )(*operands)


def on_device_paired(inputs, weight, cotangent):
    bands = D // BLOCK
    groups = lax.axis_size("dp")
    cores = groups // bands
    members = lax.axis_size("pre")
    core = lax.axis_index("dp") % cores
    band = lax.axis_index("dp") // cores
    plane = lax.axis_index("pre")
    tokens = inputs.shape[0]
    ahead = 1 - 2 * core
    spot = jnp.where(band % 2 == 0, band // 2, bands - 1 - band // 2)

    ring = list(range(0, bands, 2)) + list(range(bands - 1, 0, -2))

    def swap_core(array):
        return lax.ppermute(array, "dp", [(g, g ^ 1) for g in range(groups)])

    def swap_plane(array):
        return lax.ppermute(array, "pre", [(c, members - 1 - c) for c in range(members)])

    def deal(array, hop):
        pairs = [
            (
                (k * cores + c) * members + m,
                ((k ^ OFFSETS[m][hop]) * cores + c) * members + m,
            )
            for k in range(bands)
            for c in range(cores)
            for m in range(members)
        ]
        return lax.ppermute(array, ("dp", "pre"), pairs)

    hops = range(len(OFFSETS[0]))
    bands_out = [band ^ jnp.where(plane == 0, OFFSETS[0][hop], OFFSETS[1][hop]) for hop in hops]
    own_band, *packed = call(
        pack_kernel,
        [jax.ShapeDtypeStruct((tokens, BLOCK), inputs.dtype)] * len(hops)
        + [jax.ShapeDtypeStruct((tokens // 2, BLOCK), inputs.dtype)],
        [],
        jnp.stack([plane * (tokens // 2), band] + bands_out).astype(jnp.int32),
        inputs,
    )
    def exchange(array, offset):
        pairs = [
            (k * cores + c, (k ^ offset) * cores + c) for k in range(bands) for c in range(cores)
        ]
        return lax.ppermute(array, "dp", pairs)

    outputs = jnp.dot(inputs, weight, preferred_element_type=jnp.float32).astype(jnp.bfloat16)
    far_cot, outputs = lax.optimization_barrier((exchange(cotangent, 4), outputs))
    near = [deal(piece, hop) for hop, piece in zip(hops, packed)]
    pair = jnp.concatenate([cotangent, far_cot])
    cots = [pair] + [exchange(pair, offset) for offset in (1, 2, 3)]
    far = [swap_plane(piece) for piece in near]
    (partial_tile,) = call(
        tile_kernel,
        [jax.ShapeDtypeStruct((BLOCK, BLOCK), jnp.float32)],
        [pltpu.VMEM((bands * tokens, BLOCK), inputs.dtype)] * 2,
        jnp.stack([plane, band]).astype(jnp.int32),
        own_band,
        *near,
        *far,
        *cots,
    )
    other_partial = swap_core(partial_tile)
    side = jnp.stack([core, plane]).astype(jnp.int32)
    tile_half, root = call(
        newton_kernel,
        [
            jax.ShapeDtypeStruct((BLOCK, BLOCK), jnp.bfloat16),
            jax.ShapeDtypeStruct((BLOCK, BLOCK), jnp.bfloat16),
        ],
        [pltpu.VMEM((BLOCK, BLOCK), jnp.float32)],
        side,
        partial_tile,
        other_partial,
    )
    other_root = swap_core(root)
    rows = BLOCK // members // cores
    near_piece, next_piece, far_piece = call(
        update_kernel,
        [jax.ShapeDtypeStruct((rows, BLOCK), jnp.bfloat16)] * 3,
        [],
        side,
        root,
        other_root,
        tile_half,
    )

    def turn(array):
        pairs = [
            (ring[k] * cores + c, ring[(k + 1 - 2 * c) % bands] * cores + c)
            for k in range(bands)
            for c in range(cores)
        ]
        return lax.ppermute(array, "dp", pairs)

    half_way = bands // 2
    crossed = swap_plane(far_piece)
    heads = [near_piece, next_piece, crossed, swap_core(crossed)]
    columns = [jnp.zeros((bands, cores, rows, BLOCK), jnp.bfloat16)] * 2

    def put(chunk, piece, position, half):
        columns[chunk] = lax.dynamic_update_slice(
            columns[chunk], piece[None, None], (ring_band(position, bands), half, 0, 0)
        )

    for hop in range(half_way + 1):
        for k, head in enumerate(heads):
            chunk, half = k // 2, (core if k % 2 == 0 else 1 - core)
            if hop == half_way and k % 2 == 1:
                continue
            if hop > 0:
                heads[k] = head = turn(head)
                put(chunk, swap_core(head), spot + ahead * hop, 1 - half)
            put(chunk, head, spot - ahead * hop, half)
    former, latter = (column.reshape(bands, cores * rows, BLOCK) for column in columns)
    update = jnp.where(
        plane == 0,
        jnp.concatenate([former, latter], axis=-1),
        jnp.concatenate([latter, former], axis=-1),
    )
    return (outputs, update)


def solution(mesh):
    placed = (P("dp", None), P(None, "pre"), P("dp", "pre"))
    paired = mesh.shape["dp"] == 2 * D // BLOCK and mesh.shape["pre"] == CB == 2
    return jax.shard_map(
        on_device_paired if paired else on_device_general,
        mesh=mesh,
        in_specs=placed,
        out_specs=(P("dp", "pre"), P(None, "pre", None)),
        check_vma=False,
    )
```

```python
import math

import jax
import jax.numpy as jnp
from jax import lax
from jax.experimental import pallas as pl
from jax.experimental.pallas import tpu as pltpu
from jax.sharding import PartitionSpec as P

D = 4096
BLOCK = 512
CB = 2
ITERS = 3


DAMPING = 0.1
HIGH = lax.Precision.HIGHEST


def batch_dot(former, latter):
    return jnp.einsum(
        "sij,sjk->sik", former, latter, precision=HIGH, preferred_element_type=jnp.float32
    )


def on_device_general(inputs, weight, cotangent):
    groups = lax.axis_size("dp")
    members = lax.axis_size("pre")
    group_id = lax.axis_index("dp")
    member_id = lax.axis_index("pre")
    slab_rows = BLOCK // members
    blocks_all = D // BLOCK * CB
    rounds = max(1, blocks_all // groups)
    sharers = max(1, groups // blocks_all)
    col_width = BLOCK // sharers
    copy_id = group_id // blocks_all
    outputs = jnp.dot(inputs, weight, preferred_element_type=jnp.float32).astype(jnp.bfloat16)
    partial_value = lax.dot_general(
        inputs, cotangent, (((0,), (0,)), ((), ())), preferred_element_type=jnp.float32
    )
    owned_ids = (group_id + groups * jnp.arange(rounds, dtype=jnp.int32)) % blocks_all
    row_offsets = owned_ids // CB * BLOCK
    col_offsets = owned_ids % CB * BLOCK
    gradient = lax.psum(partial_value, "dp")
    row_bands = jax.vmap(lambda offset: lax.dynamic_slice_in_dim(gradient, offset, BLOCK, 0))(
        row_offsets
    )
    wide_band = lax.all_gather(row_bands, "pre", axis=2, tiled=True)
    tile_grad = jax.vmap(
        lambda row_band, offset: lax.dynamic_slice_in_dim(row_band, offset, BLOCK, 1)
    )(wide_band, col_offsets)
    first_row = member_id * slab_rows
    own_rows = lax.dynamic_slice_in_dim(tile_grad, first_row, slab_rows, 1)
    own_cols = lax.dynamic_slice_in_dim(tile_grad, first_row, slab_rows, 2)
    left_rows = jnp.einsum(
        "sij,skj->sik", own_rows, tile_grad, precision=HIGH, preferred_element_type=jnp.float32
    )
    right_rows = jnp.einsum(
        "sji,sjk->sik", own_cols, tile_grad, precision=HIGH, preferred_element_type=jnp.float32
    )
    stat_rows = jnp.stack([left_rows, right_rows], axis=1).reshape(rounds * 2, slab_rows, BLOCK)
    tile_energy = jnp.sum(tile_grad * tile_grad, axis=(1, 2))
    energy = jnp.stack([tile_energy, tile_energy], axis=1).reshape(rounds * 2)
    unit_rows = (jnp.arange(BLOCK)[None, :] == (first_row + jnp.arange(slab_rows))[:, None]).astype(
        jnp.float32
    )
    unit_eye = jnp.eye(BLOCK, dtype=jnp.float32)
    state_rows = stat_rows + (DAMPING * energy / BLOCK)[:, None, None] * unit_rows[None]
    root_rows = unit_rows[None]
    for iteration in range(ITERS):
        full_state = lax.all_gather(state_rows, "pre", axis=1, tiled=True)
        if iteration == 0:
            frob_norm = jnp.sqrt(jnp.sum(full_state * full_state, axis=(1, 2)))
            full_state = full_state / frob_norm[:, None, None]
            state_rows = state_rows / frob_norm[:, None, None]
            root_rows = unit_rows[None] * (frob_norm ** (-0.25))[:, None, None]
        factor = (5.0 * unit_eye - full_state) * 0.25
        square = batch_dot(factor, factor)
        square_rows = lax.dynamic_slice_in_dim(square, first_row, slab_rows, 1)
        fourth_rows = batch_dot(square_rows, square)
        state_rows = batch_dot(fourth_rows, full_state)
        root_rows = batch_dot(root_rows, factor)
    root_half = root_rows.astype(jnp.bfloat16).reshape(rounds, 2, slab_rows, BLOCK)
    right_full = lax.all_gather(root_half[:, 1], "pre", axis=1, tiled=True)
    right_cols = lax.dynamic_slice_in_dim(right_full, copy_id * col_width, col_width, 2)
    tile_half = tile_grad.astype(jnp.bfloat16)
    half_prod = jnp.einsum(
        "sij,sjk->sik", root_half[:, 0], tile_half, preferred_element_type=jnp.float32
    ).astype(jnp.bfloat16)
    piece_rows = jnp.einsum(
        "sij,sjk->sik", half_prod, right_cols, preferred_element_type=jnp.float32
    )
    piece_rows = (piece_rows * math.sqrt(BLOCK)).astype(jnp.bfloat16)
    collected = lax.all_gather(piece_rows[None], "dp", axis=0, tiled=True)
    if sharers == 1:
        ordered = jnp.swapaxes(collected, 0, 1).reshape(blocks_all, slab_rows, BLOCK)
    else:
        ordered = (
            collected[:, 0]
            .reshape(sharers, blocks_all, slab_rows, col_width)
            .transpose(1, 2, 0, 3)
            .reshape(blocks_all, slab_rows, BLOCK)
        )
    update = (
        ordered.reshape(D // BLOCK, CB, slab_rows, BLOCK)
        .transpose(0, 2, 1, 3)
        .reshape(D // BLOCK, slab_rows, CB * BLOCK)
    )
    return (outputs, update)


def contract(former, latter, former_dim, latter_dim):
    return lax.dot_general(
        former,
        latter,
        (((former_dim,), (latter_dim,)), ((), ())),
        preferred_element_type=jnp.float32,
    )


def product(former, latter):
    return contract(former.astype(jnp.bfloat16), latter.astype(jnp.bfloat16), 1, 0)


def total(array):
    return jnp.sum(jnp.sum(array, axis=0, keepdims=True), axis=1, keepdims=True)


def newton_step(states):
    excesses = [product(m, m) * (1.0 / 16.0) - 0.625 * m for m in states]
    growths = [3.125 * e + product(e, e) for e in excesses]
    return [(625.0 / 256.0) * m + product(m, g) for m, g in zip(states, growths)]


def inverse_roots(tile):
    tile_half = tile.astype(jnp.bfloat16)
    order = tile.shape[0]
    row_ids = lax.broadcasted_iota(jnp.int32, (order, order), 0)
    col_ids = lax.broadcasted_iota(jnp.int32, (order, order), 1)
    on_diagonal = row_ids == col_ids
    damp = (DAMPING / order) * total(tile * tile)
    stats = [contract(tile_half, tile_half, 1, 1), contract(tile_half, tile_half, 0, 0)]
    stats = [jnp.where(on_diagonal, stat + damp, stat) for stat in stats]
    norms = [jnp.sqrt(total(stat * stat)) for stat in stats]
    firsts = [stat / norm for stat, norm in zip(stats, norms)]
    seconds = newton_step(firsts)
    thirds = newton_step(seconds)
    crosses = [
        product(m, n) * (1.0 / 16.0) - (5.0 / 16.0) * (m + n) for m, n in zip(firsts, seconds)
    ]
    roots = []
    for cross, third, norm in zip(crosses, thirds, norms):
        root = 1.25 * cross - 0.25 * product(cross, third) - (25.0 / 64.0) * third
        root = jnp.where(on_diagonal, root + 125.0 / 64.0, root)
        roots.append((root / jnp.sqrt(jnp.sqrt(norm))).astype(jnp.bfloat16))
    return roots


def update_kernel(side_ref, mine_ref, other_ref, near_ref, next_ref, far_ref, left_ref):
    tile = mine_ref[...] + other_ref[...]
    tile_half = tile.astype(jnp.bfloat16)
    left_ref[...], right = inverse_roots(tile)
    rows = near_ref.shape[0]
    core, plane = side_ref[0], side_ref[1]
    for out_ref, part in (
        (near_ref, 2 * plane + core),
        (next_ref, 2 * plane + 1 - core),
        (far_ref, 2 * (1 - plane) + core),
    ):
        left = left_ref[pl.ds(pl.multiple_of(part * rows, rows), rows), :]
        half = contract(left, tile_half, 1, 0).astype(jnp.bfloat16)
        piece = contract(half, right, 1, 0) * math.sqrt(BLOCK)
        out_ref[...] = piece.astype(jnp.bfloat16)


OFFSETS = ((4, 7, 1, 2), (5, 6, 3, 2))


def pack_kernel(place_ref, inputs_ref, *piece_refs):
    for step, piece_ref in enumerate(piece_refs):
        rows = piece_ref.shape[0]
        last = step == len(piece_refs) - 1
        first_row = pl.multiple_of(place_ref[0], rows) if last else 0
        first_col = pl.multiple_of(place_ref[1 + step] * BLOCK, BLOCK)
        piece_ref[...] = inputs_ref[pl.ds(first_row, rows), pl.ds(first_col, BLOCK)]


def ring_band(position, bands):
    position = (position + 2 * bands) % bands
    return jnp.where(position < bands // 2, 2 * position, 2 * (bands - 1 - position) + 1)


def tile_kernel(place_ref, own_ref, *refs):
    hops = len(OFFSETS[0])
    near_refs, far_refs = refs[:hops], refs[hops : 2 * hops]
    cot_refs = refs[2 * hops : -3]
    partial_ref, band_ref, cot_ref = refs[-3:]
    plane, band = place_ref[0], place_ref[1]
    tokens = own_ref.shape[0]

    def put(to_ref, piece_ref, source, part):
        rows = piece_ref.shape[0]
        first_row = pl.multiple_of(source * tokens + part * rows, rows)
        to_ref[pl.ds(first_row, rows), :] = piece_ref[...]

    put(band_ref, own_ref, band, 0)
    for hop in range(hops):
        last = hop == hops - 1
        for piece_ref, member in ((near_refs[hop], plane), (far_refs[hop], 1 - plane)):
            offset = jnp.where(member == 0, OFFSETS[0][hop], OFFSETS[1][hop])
            put(band_ref, piece_ref, band ^ offset, member if last else 0)
    for offset, pair_ref in enumerate(cot_refs):
        for part, source in enumerate((band ^ offset, band ^ offset ^ 4)):
            put(cot_ref, pair_ref.at[pl.ds(part * tokens, tokens)], source, 0)
    partial_ref[...] = contract(band_ref[...], cot_ref[...], 0, 0)


def call(kernel, out_shapes, scratch_shapes, *operands):
    in_specs = [pl.BlockSpec(memory_space=pltpu.SMEM)]
    in_specs += [pl.BlockSpec(memory_space=pltpu.VMEM)] * (len(operands) - 1)
    return pl.pallas_call(
        kernel,
        out_shape=out_shapes,
        in_specs=in_specs,
        out_specs=[pl.BlockSpec(memory_space=pltpu.VMEM)] * len(out_shapes),
        scratch_shapes=scratch_shapes,
        compiler_params=pltpu.CompilerParams(vmem_limit_bytes=32 * 1024 * 1024),
    )(*operands)


def on_device_paired(inputs, weight, cotangent):
    bands = D // BLOCK
    groups = lax.axis_size("dp")
    cores = groups // bands
    members = lax.axis_size("pre")
    core = lax.axis_index("dp") % cores
    band = lax.axis_index("dp") // cores
    plane = lax.axis_index("pre")
    tokens = inputs.shape[0]
    ahead = 1 - 2 * core
    spot = jnp.where(band % 2 == 0, band // 2, bands - 1 - band // 2)

    ring = list(range(0, bands, 2)) + list(range(bands - 1, 0, -2))

    def swap_core(array):
        return lax.ppermute(array, "dp", [(g, g ^ 1) for g in range(groups)])

    def swap_plane(array):
        return lax.ppermute(array, "pre", [(c, members - 1 - c) for c in range(members)])

    def deal(array, hop):
        pairs = [
            (
                (k * cores + c) * members + m,
                ((k ^ OFFSETS[m][hop]) * cores + c) * members + m,
            )
            for k in range(bands)
            for c in range(cores)
            for m in range(members)
        ]
        return lax.ppermute(array, ("dp", "pre"), pairs)

    hops = range(len(OFFSETS[0]))
    bands_out = [band ^ jnp.where(plane == 0, OFFSETS[0][hop], OFFSETS[1][hop]) for hop in hops]
    own_band, *packed = call(
        pack_kernel,
        [jax.ShapeDtypeStruct((tokens, BLOCK), inputs.dtype)] * len(hops)
        + [jax.ShapeDtypeStruct((tokens // 2, BLOCK), inputs.dtype)],
        [],
        jnp.stack([plane * (tokens // 2), band] + bands_out).astype(jnp.int32),
        inputs,
    )
    def exchange(array, offset):
        pairs = [
            (k * cores + c, (k ^ offset) * cores + c) for k in range(bands) for c in range(cores)
        ]
        return lax.ppermute(array, "dp", pairs)

    outputs = jnp.dot(inputs, weight, preferred_element_type=jnp.float32).astype(jnp.bfloat16)
    far_cot, outputs = lax.optimization_barrier((exchange(cotangent, 4), outputs))
    near = [deal(piece, hop) for hop, piece in zip(hops, packed)]
    pair = jnp.concatenate([cotangent, far_cot])
    cots = [pair] + [exchange(pair, offset) for offset in (1, 2, 3)]
    far = [swap_plane(piece) for piece in near]
    (partial_tile,) = call(
        tile_kernel,
        [jax.ShapeDtypeStruct((BLOCK, BLOCK), jnp.float32)],
        [pltpu.VMEM((bands * tokens, BLOCK), inputs.dtype)] * 2,
        jnp.stack([plane, band]).astype(jnp.int32),
        own_band,
        *near,
        *far,
        *cots,
    )
    other_partial = swap_core(partial_tile)
    side = jnp.stack([core, plane]).astype(jnp.int32)
    rows = BLOCK // members // cores
    near_piece, next_piece, far_piece = call(
        update_kernel,
        [jax.ShapeDtypeStruct((rows, BLOCK), jnp.bfloat16)] * 3,
        [pltpu.VMEM((BLOCK, BLOCK), jnp.bfloat16)],
        side,
        partial_tile,
        other_partial,
    )

    def turn(array):
        pairs = [
            (ring[k] * cores + c, ring[(k + 1 - 2 * c) % bands] * cores + c)
            for k in range(bands)
            for c in range(cores)
        ]
        return lax.ppermute(array, "dp", pairs)

    half_way = bands // 2
    crossed = swap_plane(far_piece)
    heads = [near_piece, next_piece, crossed, swap_core(crossed)]
    columns = [jnp.zeros((bands, cores, rows, BLOCK), jnp.bfloat16)] * 2

    def put(chunk, piece, position, half):
        columns[chunk] = lax.dynamic_update_slice(
            columns[chunk], piece[None, None], (ring_band(position, bands), half, 0, 0)
        )

    for hop in range(half_way + 1):
        for k, head in enumerate(heads):
            chunk, half = k // 2, (core if k % 2 == 0 else 1 - core)
            if hop == half_way and k % 2 == 1:
                continue
            if hop > 0:
                heads[k] = head = turn(head)
                put(chunk, swap_core(head), spot + ahead * hop, 1 - half)
            put(chunk, head, spot - ahead * hop, half)
    former, latter = (column.reshape(bands, cores * rows, BLOCK) for column in columns)
    update = jnp.where(
        plane == 0,
        jnp.concatenate([former, latter], axis=-1),
        jnp.concatenate([latter, former], axis=-1),
    )
    return (outputs, update)


def solution(mesh):
    placed = (P("dp", None), P(None, "pre"), P("dp", "pre"))
    paired = mesh.shape["dp"] == 2 * D // BLOCK and mesh.shape["pre"] == CB == 2
    return jax.shard_map(
        on_device_paired if paired else on_device_general,
        mesh=mesh,
        in_specs=placed,
        out_specs=(P("dp", "pre"), P(None, "pre", None)),
        check_vma=False,
    )
```

```python
import math

import jax
import jax.numpy as jnp
from jax import lax
from jax.experimental import pallas as pl
from jax.experimental.pallas import tpu as pltpu
from jax.sharding import PartitionSpec as P

D = 4096
BLOCK = 512
CB = 2
ITERS = 3


DAMPING = 0.1
HIGH = lax.Precision.HIGHEST


def batch_dot(former, latter):
    return jnp.einsum(
        "sij,sjk->sik", former, latter, precision=HIGH, preferred_element_type=jnp.float32
    )


def on_device_general(inputs, weight, cotangent):
    groups = lax.axis_size("dp")
    members = lax.axis_size("pre")
    group_id = lax.axis_index("dp")
    member_id = lax.axis_index("pre")
    slab_rows = BLOCK // members
    blocks_all = D // BLOCK * CB
    rounds = max(1, blocks_all // groups)
    sharers = max(1, groups // blocks_all)
    col_width = BLOCK // sharers
    copy_id = group_id // blocks_all
    outputs = jnp.dot(inputs, weight, preferred_element_type=jnp.float32).astype(jnp.bfloat16)
    partial_value = lax.dot_general(
        inputs, cotangent, (((0,), (0,)), ((), ())), preferred_element_type=jnp.float32
    )
    owned_ids = (group_id + groups * jnp.arange(rounds, dtype=jnp.int32)) % blocks_all
    row_offsets = owned_ids // CB * BLOCK
    col_offsets = owned_ids % CB * BLOCK
    gradient = lax.psum(partial_value, "dp")
    row_bands = jax.vmap(lambda offset: lax.dynamic_slice_in_dim(gradient, offset, BLOCK, 0))(
        row_offsets
    )
    wide_band = lax.all_gather(row_bands, "pre", axis=2, tiled=True)
    tile_grad = jax.vmap(
        lambda row_band, offset: lax.dynamic_slice_in_dim(row_band, offset, BLOCK, 1)
    )(wide_band, col_offsets)
    first_row = member_id * slab_rows
    own_rows = lax.dynamic_slice_in_dim(tile_grad, first_row, slab_rows, 1)
    own_cols = lax.dynamic_slice_in_dim(tile_grad, first_row, slab_rows, 2)
    left_rows = jnp.einsum(
        "sij,skj->sik", own_rows, tile_grad, precision=HIGH, preferred_element_type=jnp.float32
    )
    right_rows = jnp.einsum(
        "sji,sjk->sik", own_cols, tile_grad, precision=HIGH, preferred_element_type=jnp.float32
    )
    stat_rows = jnp.stack([left_rows, right_rows], axis=1).reshape(rounds * 2, slab_rows, BLOCK)
    tile_energy = jnp.sum(tile_grad * tile_grad, axis=(1, 2))
    energy = jnp.stack([tile_energy, tile_energy], axis=1).reshape(rounds * 2)
    unit_rows = (jnp.arange(BLOCK)[None, :] == (first_row + jnp.arange(slab_rows))[:, None]).astype(
        jnp.float32
    )
    unit_eye = jnp.eye(BLOCK, dtype=jnp.float32)
    state_rows = stat_rows + (DAMPING * energy / BLOCK)[:, None, None] * unit_rows[None]
    root_rows = unit_rows[None]
    for iteration in range(ITERS):
        full_state = lax.all_gather(state_rows, "pre", axis=1, tiled=True)
        if iteration == 0:
            frob_norm = jnp.sqrt(jnp.sum(full_state * full_state, axis=(1, 2)))
            full_state = full_state / frob_norm[:, None, None]
            state_rows = state_rows / frob_norm[:, None, None]
            root_rows = unit_rows[None] * (frob_norm ** (-0.25))[:, None, None]
        factor = (5.0 * unit_eye - full_state) * 0.25
        square = batch_dot(factor, factor)
        square_rows = lax.dynamic_slice_in_dim(square, first_row, slab_rows, 1)
        fourth_rows = batch_dot(square_rows, square)
        state_rows = batch_dot(fourth_rows, full_state)
        root_rows = batch_dot(root_rows, factor)
    root_half = root_rows.astype(jnp.bfloat16).reshape(rounds, 2, slab_rows, BLOCK)
    right_full = lax.all_gather(root_half[:, 1], "pre", axis=1, tiled=True)
    right_cols = lax.dynamic_slice_in_dim(right_full, copy_id * col_width, col_width, 2)
    tile_half = tile_grad.astype(jnp.bfloat16)
    half_prod = jnp.einsum(
        "sij,sjk->sik", root_half[:, 0], tile_half, preferred_element_type=jnp.float32
    ).astype(jnp.bfloat16)
    piece_rows = jnp.einsum(
        "sij,sjk->sik", half_prod, right_cols, preferred_element_type=jnp.float32
    )
    piece_rows = (piece_rows * math.sqrt(BLOCK)).astype(jnp.bfloat16)
    collected = lax.all_gather(piece_rows[None], "dp", axis=0, tiled=True)
    if sharers == 1:
        ordered = jnp.swapaxes(collected, 0, 1).reshape(blocks_all, slab_rows, BLOCK)
    else:
        ordered = (
            collected[:, 0]
            .reshape(sharers, blocks_all, slab_rows, col_width)
            .transpose(1, 2, 0, 3)
            .reshape(blocks_all, slab_rows, BLOCK)
        )
    update = (
        ordered.reshape(D // BLOCK, CB, slab_rows, BLOCK)
        .transpose(0, 2, 1, 3)
        .reshape(D // BLOCK, slab_rows, CB * BLOCK)
    )
    return (outputs, update)


def contract(former, latter, former_dim, latter_dim):
    return lax.dot_general(
        former,
        latter,
        (((former_dim,), (latter_dim,)), ((), ())),
        preferred_element_type=jnp.float32,
    )


def product(former, latter):
    return contract(former.astype(jnp.bfloat16), latter.astype(jnp.bfloat16), 1, 0)


def total(array):
    return jnp.sum(jnp.sum(array, axis=0, keepdims=True), axis=1, keepdims=True)


def newton_step(states):
    excesses = [product(m, m) * (1.0 / 16.0) - 0.625 * m for m in states]
    growths = [3.125 * e + product(e, e) for e in excesses]
    return [(625.0 / 256.0) * m + product(m, g) for m, g in zip(states, growths)]


def inverse_roots(tile):
    tile_half = tile.astype(jnp.bfloat16)
    order = tile.shape[0]
    row_ids = lax.broadcasted_iota(jnp.int32, (order, order), 0)
    col_ids = lax.broadcasted_iota(jnp.int32, (order, order), 1)
    on_diagonal = row_ids == col_ids
    damp = (DAMPING / order) * total(tile * tile)
    stats = [contract(tile_half, tile_half, 1, 1), contract(tile_half, tile_half, 0, 0)]
    stats = [jnp.where(on_diagonal, stat + damp, stat) for stat in stats]
    norms = [jnp.sqrt(total(stat * stat)) for stat in stats]
    firsts = [stat / norm for stat, norm in zip(stats, norms)]
    seconds = newton_step(firsts)
    thirds = newton_step(seconds)
    crosses = [
        product(m, n) * (1.0 / 16.0) - (5.0 / 16.0) * (m + n) for m, n in zip(firsts, seconds)
    ]
    roots = []
    for cross, third, norm in zip(crosses, thirds, norms):
        root = 1.25 * cross - 0.25 * product(cross, third) - (25.0 / 64.0) * third
        root = jnp.where(on_diagonal, root + 125.0 / 64.0, root)
        roots.append((root / jnp.sqrt(jnp.sqrt(norm))).astype(jnp.bfloat16))
    return roots


def update_kernel(side_ref, mine_ref, other_ref, near_ref, next_ref, far_ref, left_ref):
    tile = mine_ref[...] + other_ref[...]
    tile_half = tile.astype(jnp.bfloat16)
    left_ref[...], right = inverse_roots(tile)
    rows = near_ref.shape[0]
    core, plane = side_ref[0], side_ref[1]
    for out_ref, part in (
        (near_ref, 2 * plane + core),
        (next_ref, 2 * plane + 1 - core),
        (far_ref, 2 * (1 - plane) + core),
    ):
        left = left_ref[pl.ds(pl.multiple_of(part * rows, rows), rows), :]
        half = contract(left, tile_half, 1, 0).astype(jnp.bfloat16)
        piece = contract(half, right, 1, 0) * math.sqrt(BLOCK)
        out_ref[...] = piece.astype(jnp.bfloat16)


OFFSETS = ((4, 7, 2), (5, 6, 3))
SHARED = 1


def pack_kernel(place_ref, inputs_ref, *piece_refs):
    for step, piece_ref in enumerate(piece_refs):
        first_col = pl.multiple_of(place_ref[step] * BLOCK, BLOCK)
        piece_ref[...] = inputs_ref[:, pl.ds(first_col, BLOCK)]


def ring_band(position, bands):
    position = (position + 2 * bands) % bands
    return jnp.where(position < bands // 2, 2 * position, 2 * (bands - 1 - position) + 1)


def tile_kernel(place_ref, own_ref, shared_ref, *refs):
    hops = len(OFFSETS[0])
    near_refs, far_refs = refs[:hops], refs[hops : 2 * hops]
    cot_refs = refs[2 * hops : -3]
    partial_ref, band_ref, cot_ref = refs[-3:]
    plane, band = place_ref[0], place_ref[1]
    tokens = own_ref.shape[0]

    def put(to_ref, piece_ref, source):
        first_row = pl.multiple_of(source * tokens, tokens)
        to_ref[pl.ds(first_row, tokens), :] = piece_ref[...]

    put(band_ref, own_ref, band)
    put(band_ref, shared_ref, band ^ SHARED)
    for hop in range(hops):
        for piece_ref, member in ((near_refs[hop], plane), (far_refs[hop], 1 - plane)):
            put(band_ref, piece_ref, band ^ jnp.where(member == 0, OFFSETS[0][hop], OFFSETS[1][hop]))
    for offset, pair_ref in enumerate(cot_refs):
        for part, source in enumerate((band ^ offset, band ^ offset ^ 4)):
            put(cot_ref, pair_ref.at[pl.ds(part * tokens, tokens)], source)
    partial_ref[...] = contract(band_ref[...], cot_ref[...], 0, 0)


def call(kernel, out_shapes, scratch_shapes, *operands):
    in_specs = [pl.BlockSpec(memory_space=pltpu.SMEM)]
    in_specs += [pl.BlockSpec(memory_space=pltpu.VMEM)] * (len(operands) - 1)
    return pl.pallas_call(
        kernel,
        out_shape=out_shapes,
        in_specs=in_specs,
        out_specs=[pl.BlockSpec(memory_space=pltpu.VMEM)] * len(out_shapes),
        scratch_shapes=scratch_shapes,
        compiler_params=pltpu.CompilerParams(vmem_limit_bytes=32 * 1024 * 1024),
    )(*operands)


def on_device_paired(inputs, weight, cotangent):
    bands = D // BLOCK
    groups = lax.axis_size("dp")
    cores = groups // bands
    members = lax.axis_size("pre")
    core = lax.axis_index("dp") % cores
    band = lax.axis_index("dp") // cores
    plane = lax.axis_index("pre")
    tokens = inputs.shape[0]
    ahead = 1 - 2 * core
    spot = jnp.where(band % 2 == 0, band // 2, bands - 1 - band // 2)

    ring = list(range(0, bands, 2)) + list(range(bands - 1, 0, -2))

    def swap_core(array):
        return lax.ppermute(array, "dp", [(g, g ^ 1) for g in range(groups)])

    def swap_plane(array):
        return lax.ppermute(array, "pre", [(c, members - 1 - c) for c in range(members)])

    def deal(array, hop):
        pairs = [
            (
                (k * cores + c) * members + m,
                ((k ^ OFFSETS[m][hop]) * cores + c) * members + m,
            )
            for k in range(bands)
            for c in range(cores)
            for m in range(members)
        ]
        return lax.ppermute(array, ("dp", "pre"), pairs)

    hops = range(len(OFFSETS[0]))
    bands_out = [band ^ jnp.where(plane == 0, OFFSETS[0][hop], OFFSETS[1][hop]) for hop in hops]
    *packed, own_band = call(
        pack_kernel,
        [jax.ShapeDtypeStruct((tokens, BLOCK), inputs.dtype)] * (len(hops) + 2),
        [],
        jnp.stack(bands_out + [band ^ SHARED, band]).astype(jnp.int32),
        inputs,
    )

    def exchange(array, offset):
        pairs = [
            (k * cores + c, (k ^ offset) * cores + c) for k in range(bands) for c in range(cores)
        ]
        return lax.ppermute(array, "dp", pairs)

    outputs = jnp.dot(inputs, weight, preferred_element_type=jnp.float32).astype(jnp.bfloat16)
    far_cot, outputs = lax.optimization_barrier((exchange(cotangent, 4), outputs))
    near = [deal(packed[hop], hop) for hop in hops]
    shared = exchange(packed[-1], SHARED)
    pair = jnp.concatenate([cotangent, far_cot])
    cots = [pair] + [exchange(pair, offset) for offset in (1, 2, 3)]
    far = [swap_plane(piece) for piece in near]
    (partial_tile,) = call(
        tile_kernel,
        [jax.ShapeDtypeStruct((BLOCK, BLOCK), jnp.float32)],
        [pltpu.VMEM((bands * tokens, BLOCK), inputs.dtype)] * 2,
        jnp.stack([plane, band]).astype(jnp.int32),
        own_band,
        shared,
        *near,
        *far,
        *cots,
    )
    other_partial = swap_core(partial_tile)
    side = jnp.stack([core, plane]).astype(jnp.int32)
    rows = BLOCK // members // cores
    near_piece, next_piece, far_piece = call(
        update_kernel,
        [jax.ShapeDtypeStruct((rows, BLOCK), jnp.bfloat16)] * 3,
        [pltpu.VMEM((BLOCK, BLOCK), jnp.bfloat16)],
        side,
        partial_tile,
        other_partial,
    )

    def turn(array):
        pairs = [
            (ring[k] * cores + c, ring[(k + 1 - 2 * c) % bands] * cores + c)
            for k in range(bands)
            for c in range(cores)
        ]
        return lax.ppermute(array, "dp", pairs)

    half_way = bands // 2
    crossed = swap_plane(far_piece)
    heads = [near_piece, next_piece, crossed, swap_core(crossed)]
    columns = [jnp.zeros((bands, cores, rows, BLOCK), jnp.bfloat16)] * 2

    def put(chunk, piece, position, half):
        columns[chunk] = lax.dynamic_update_slice(
            columns[chunk], piece[None, None], (ring_band(position, bands), half, 0, 0)
        )

    for hop in range(half_way + 1):
        for k, head in enumerate(heads):
            chunk, half = k // 2, (core if k % 2 == 0 else 1 - core)
            if hop == half_way and k % 2 == 1:
                continue
            if hop > 0:
                heads[k] = head = turn(head)
                put(chunk, swap_core(head), spot + ahead * hop, 1 - half)
            put(chunk, head, spot - ahead * hop, half)
    former, latter = (column.reshape(bands, cores * rows, BLOCK) for column in columns)
    update = jnp.where(
        plane == 0,
        jnp.concatenate([former, latter], axis=-1),
        jnp.concatenate([latter, former], axis=-1),
    )
    return (outputs, update)


def solution(mesh):
    placed = (P("dp", None), P(None, "pre"), P("dp", "pre"))
    paired = mesh.shape["dp"] == 2 * D // BLOCK and mesh.shape["pre"] == CB == 2
    return jax.shard_map(
        on_device_paired if paired else on_device_general,
        mesh=mesh,
        in_specs=placed,
        out_specs=(P("dp", "pre"), P(None, "pre", None)),
        check_vma=False,
    )
```

```python
import math

import jax
import jax.numpy as jnp
from jax import lax
from jax.experimental import pallas as pl
from jax.experimental.pallas import tpu as pltpu
from jax.sharding import PartitionSpec as P

D = 4096
BLOCK = 512
CB = 2
ITERS = 3


DAMPING = 0.1
HIGH = lax.Precision.HIGHEST


def batch_dot(former, latter):
    return jnp.einsum(
        "sij,sjk->sik", former, latter, precision=HIGH, preferred_element_type=jnp.float32
    )


def on_device_general(inputs, weight, cotangent):
    groups = lax.axis_size("dp")
    members = lax.axis_size("pre")
    group_id = lax.axis_index("dp")
    member_id = lax.axis_index("pre")
    slab_rows = BLOCK // members
    blocks_all = D // BLOCK * CB
    rounds = max(1, blocks_all // groups)
    sharers = max(1, groups // blocks_all)
    col_width = BLOCK // sharers
    copy_id = group_id // blocks_all
    outputs = jnp.dot(inputs, weight, preferred_element_type=jnp.float32).astype(jnp.bfloat16)
    partial_value = lax.dot_general(
        inputs, cotangent, (((0,), (0,)), ((), ())), preferred_element_type=jnp.float32
    )
    owned_ids = (group_id + groups * jnp.arange(rounds, dtype=jnp.int32)) % blocks_all
    row_offsets = owned_ids // CB * BLOCK
    col_offsets = owned_ids % CB * BLOCK
    gradient = lax.psum(partial_value, "dp")
    row_bands = jax.vmap(lambda offset: lax.dynamic_slice_in_dim(gradient, offset, BLOCK, 0))(
        row_offsets
    )
    wide_band = lax.all_gather(row_bands, "pre", axis=2, tiled=True)
    tile_grad = jax.vmap(
        lambda row_band, offset: lax.dynamic_slice_in_dim(row_band, offset, BLOCK, 1)
    )(wide_band, col_offsets)
    first_row = member_id * slab_rows
    own_rows = lax.dynamic_slice_in_dim(tile_grad, first_row, slab_rows, 1)
    own_cols = lax.dynamic_slice_in_dim(tile_grad, first_row, slab_rows, 2)
    left_rows = jnp.einsum(
        "sij,skj->sik", own_rows, tile_grad, precision=HIGH, preferred_element_type=jnp.float32
    )
    right_rows = jnp.einsum(
        "sji,sjk->sik", own_cols, tile_grad, precision=HIGH, preferred_element_type=jnp.float32
    )
    stat_rows = jnp.stack([left_rows, right_rows], axis=1).reshape(rounds * 2, slab_rows, BLOCK)
    tile_energy = jnp.sum(tile_grad * tile_grad, axis=(1, 2))
    energy = jnp.stack([tile_energy, tile_energy], axis=1).reshape(rounds * 2)
    unit_rows = (jnp.arange(BLOCK)[None, :] == (first_row + jnp.arange(slab_rows))[:, None]).astype(
        jnp.float32
    )
    unit_eye = jnp.eye(BLOCK, dtype=jnp.float32)
    state_rows = stat_rows + (DAMPING * energy / BLOCK)[:, None, None] * unit_rows[None]
    root_rows = unit_rows[None]
    for iteration in range(ITERS):
        full_state = lax.all_gather(state_rows, "pre", axis=1, tiled=True)
        if iteration == 0:
            frob_norm = jnp.sqrt(jnp.sum(full_state * full_state, axis=(1, 2)))
            full_state = full_state / frob_norm[:, None, None]
            state_rows = state_rows / frob_norm[:, None, None]
            root_rows = unit_rows[None] * (frob_norm ** (-0.25))[:, None, None]
        factor = (5.0 * unit_eye - full_state) * 0.25
        square = batch_dot(factor, factor)
        square_rows = lax.dynamic_slice_in_dim(square, first_row, slab_rows, 1)
        fourth_rows = batch_dot(square_rows, square)
        state_rows = batch_dot(fourth_rows, full_state)
        root_rows = batch_dot(root_rows, factor)
    root_half = root_rows.astype(jnp.bfloat16).reshape(rounds, 2, slab_rows, BLOCK)
    right_full = lax.all_gather(root_half[:, 1], "pre", axis=1, tiled=True)
    right_cols = lax.dynamic_slice_in_dim(right_full, copy_id * col_width, col_width, 2)
    tile_half = tile_grad.astype(jnp.bfloat16)
    half_prod = jnp.einsum(
        "sij,sjk->sik", root_half[:, 0], tile_half, preferred_element_type=jnp.float32
    ).astype(jnp.bfloat16)
    piece_rows = jnp.einsum(
        "sij,sjk->sik", half_prod, right_cols, preferred_element_type=jnp.float32
    )
    piece_rows = (piece_rows * math.sqrt(BLOCK)).astype(jnp.bfloat16)
    collected = lax.all_gather(piece_rows[None], "dp", axis=0, tiled=True)
    if sharers == 1:
        ordered = jnp.swapaxes(collected, 0, 1).reshape(blocks_all, slab_rows, BLOCK)
    else:
        ordered = (
            collected[:, 0]
            .reshape(sharers, blocks_all, slab_rows, col_width)
            .transpose(1, 2, 0, 3)
            .reshape(blocks_all, slab_rows, BLOCK)
        )
    update = (
        ordered.reshape(D // BLOCK, CB, slab_rows, BLOCK)
        .transpose(0, 2, 1, 3)
        .reshape(D // BLOCK, slab_rows, CB * BLOCK)
    )
    return (outputs, update)


def contract(former, latter, former_dim, latter_dim):
    return lax.dot_general(
        former,
        latter,
        (((former_dim,), (latter_dim,)), ((), ())),
        preferred_element_type=jnp.float32,
    )


def product(former, latter):
    return contract(former.astype(jnp.bfloat16), latter.astype(jnp.bfloat16), 1, 0)


def total(array):
    return jnp.sum(jnp.sum(array, axis=0, keepdims=True), axis=1, keepdims=True)


def newton_step(states):
    excesses = [product(m, m) * (1.0 / 16.0) - 0.625 * m for m in states]
    growths = [3.125 * e + product(e, e) for e in excesses]
    return [(625.0 / 256.0) * m + product(m, g) for m, g in zip(states, growths)]


def inverse_roots(tile):
    tile_half = tile.astype(jnp.bfloat16)
    order = tile.shape[0]
    row_ids = lax.broadcasted_iota(jnp.int32, (order, order), 0)
    col_ids = lax.broadcasted_iota(jnp.int32, (order, order), 1)
    on_diagonal = row_ids == col_ids
    damp = (DAMPING / order) * total(tile * tile)
    stats = [contract(tile_half, tile_half, 1, 1), contract(tile_half, tile_half, 0, 0)]
    stats = [jnp.where(on_diagonal, stat + damp, stat) for stat in stats]
    norms = [jnp.sqrt(total(stat * stat)) for stat in stats]
    firsts = [stat / norm for stat, norm in zip(stats, norms)]
    seconds = newton_step(firsts)
    thirds = newton_step(seconds)
    crosses = [
        product(m, n) * (1.0 / 16.0) - (5.0 / 16.0) * (m + n) for m, n in zip(firsts, seconds)
    ]
    roots = []
    for cross, third, norm in zip(crosses, thirds, norms):
        root = 1.25 * cross - 0.25 * product(cross, third) - (25.0 / 64.0) * third
        root = jnp.where(on_diagonal, root + 125.0 / 64.0, root)
        roots.append((root / jnp.sqrt(jnp.sqrt(norm))).astype(jnp.bfloat16))
    return roots


def update_kernel(side_ref, mine_ref, other_ref, near_ref, next_ref, far_ref, left_ref):
    tile = mine_ref[...] + other_ref[...]
    tile_half = tile.astype(jnp.bfloat16)
    left_ref[...], right = inverse_roots(tile)
    rows = near_ref.shape[0]
    core, plane = side_ref[0], side_ref[1]
    for out_ref, part in (
        (near_ref, 2 * plane + core),
        (next_ref, 2 * plane + 1 - core),
        (far_ref, 2 * (1 - plane) + core),
    ):
        left = left_ref[pl.ds(pl.multiple_of(part * rows, rows), rows), :]
        half = contract(left, tile_half, 1, 0).astype(jnp.bfloat16)
        piece = contract(half, right, 1, 0) * math.sqrt(BLOCK)
        out_ref[...] = piece.astype(jnp.bfloat16)


OFFSETS = ((4, 7, 2), (5, 6, 3))
SHARED = 1


def pack_kernel(place_ref, inputs_ref, *piece_refs):
    for step, piece_ref in enumerate(piece_refs):
        first_col = pl.multiple_of(place_ref[step] * BLOCK, BLOCK)
        piece_ref[...] = inputs_ref[:, pl.ds(first_col, BLOCK)]


def ring_band(position, bands):
    position = (position + 2 * bands) % bands
    return jnp.where(position < bands // 2, 2 * position, 2 * (bands - 1 - position) + 1)


def tile_kernel(place_ref, own_ref, shared_ref, *refs):
    hops = len(OFFSETS[0])
    near_refs, far_refs = refs[:hops], refs[hops : 2 * hops]
    cot_refs = refs[2 * hops : -3]
    partial_ref, band_ref, cot_ref = refs[-3:]
    plane, band = place_ref[0], place_ref[1]
    tokens = own_ref.shape[0]

    def put(to_ref, piece_ref, source):
        first_row = pl.multiple_of(source * tokens, tokens)
        to_ref[pl.ds(first_row, tokens), :] = piece_ref[...]

    put(band_ref, own_ref, band)
    put(band_ref, shared_ref, band ^ SHARED)
    for hop in range(hops):
        for piece_ref, member in ((near_refs[hop], plane), (far_refs[hop], 1 - plane)):
            put(band_ref, piece_ref, band ^ jnp.where(member == 0, OFFSETS[0][hop], OFFSETS[1][hop]))
    for offset, pair_ref in enumerate(cot_refs):
        for part, source in enumerate((band ^ offset, band ^ offset ^ 4)):
            put(cot_ref, pair_ref.at[pl.ds(part * tokens, tokens)], source)
    partial_ref[...] = contract(band_ref[...], cot_ref[...], 0, 0)


def call(kernel, out_shapes, scratch_shapes, *operands):
    in_specs = [pl.BlockSpec(memory_space=pltpu.SMEM)]
    in_specs += [pl.BlockSpec(memory_space=pltpu.VMEM)] * (len(operands) - 1)
    return pl.pallas_call(
        kernel,
        out_shape=out_shapes,
        in_specs=in_specs,
        out_specs=[pl.BlockSpec(memory_space=pltpu.VMEM)] * len(out_shapes),
        scratch_shapes=scratch_shapes,
        compiler_params=pltpu.CompilerParams(vmem_limit_bytes=32 * 1024 * 1024),
    )(*operands)


def on_device_paired(inputs, weight, cotangent):
    bands = D // BLOCK
    groups = lax.axis_size("dp")
    cores = groups // bands
    members = lax.axis_size("pre")
    core = lax.axis_index("dp") % cores
    band = lax.axis_index("dp") // cores
    plane = lax.axis_index("pre")
    tokens = inputs.shape[0]
    ahead = 1 - 2 * core
    spot = jnp.where(band % 2 == 0, band // 2, bands - 1 - band // 2)

    ring = list(range(0, bands, 2)) + list(range(bands - 1, 0, -2))

    def swap_core(array):
        return lax.ppermute(array, "dp", [(g, g ^ 1) for g in range(groups)])

    def swap_plane(array):
        return lax.ppermute(array, "pre", [(c, members - 1 - c) for c in range(members)])

    def deal(array, hop):
        pairs = [
            (
                (k * cores + c) * members + m,
                ((k ^ OFFSETS[m][hop]) * cores + c) * members + m,
            )
            for k in range(bands)
            for c in range(cores)
            for m in range(members)
        ]
        return lax.ppermute(array, ("dp", "pre"), pairs)

    hops = range(len(OFFSETS[0]))
    bands_out = [band ^ jnp.where(plane == 0, OFFSETS[0][hop], OFFSETS[1][hop]) for hop in hops]
    *packed, own_band = call(
        pack_kernel,
        [jax.ShapeDtypeStruct((tokens, BLOCK), inputs.dtype)] * (len(hops) + 2),
        [],
        jnp.stack(bands_out + [band ^ SHARED, band]).astype(jnp.int32),
        inputs,
    )

    def exchange(array, offset):
        pairs = [
            (k * cores + c, (k ^ offset) * cores + c) for k in range(bands) for c in range(cores)
        ]
        return lax.ppermute(array, "dp", pairs)

    far_cot = exchange(cotangent, 4)
    near = [deal(packed[hop], hop) for hop in hops]
    shared = exchange(packed[-1], SHARED)
    pair = jnp.concatenate([cotangent, far_cot])
    cots = [pair] + [exchange(pair, offset) for offset in (1, 2, 3)]
    far = [swap_plane(piece) for piece in near]
    outputs = jnp.dot(inputs, weight, preferred_element_type=jnp.float32).astype(jnp.bfloat16)
    own_band, outputs = lax.optimization_barrier((own_band, outputs))
    (partial_tile,) = call(
        tile_kernel,
        [jax.ShapeDtypeStruct((BLOCK, BLOCK), jnp.float32)],
        [pltpu.VMEM((bands * tokens, BLOCK), inputs.dtype)] * 2,
        jnp.stack([plane, band]).astype(jnp.int32),
        own_band,
        shared,
        *near,
        *far,
        *cots,
    )
    other_partial = swap_core(partial_tile)
    side = jnp.stack([core, plane]).astype(jnp.int32)
    rows = BLOCK // members // cores
    near_piece, next_piece, far_piece = call(
        update_kernel,
        [jax.ShapeDtypeStruct((rows, BLOCK), jnp.bfloat16)] * 3,
        [pltpu.VMEM((BLOCK, BLOCK), jnp.bfloat16)],
        side,
        partial_tile,
        other_partial,
    )

    def turn(array):
        pairs = [
            (ring[k] * cores + c, ring[(k + 1 - 2 * c) % bands] * cores + c)
            for k in range(bands)
            for c in range(cores)
        ]
        return lax.ppermute(array, "dp", pairs)

    half_way = bands // 2
    crossed = swap_plane(far_piece)
    heads = [near_piece[None], crossed[None], jnp.stack([next_piece, swap_core(crossed)])]
    chunks = [(0,), (1,), (0, 1)]
    halves = [core, core, 1 - core]
    columns = [jnp.zeros((bands, cores, rows, BLOCK), jnp.bfloat16)] * 2

    def put(parts, pieces, position, half):
        for chunk, piece in zip(parts, pieces):
            columns[chunk] = lax.dynamic_update_slice(
                columns[chunk], piece[None, None], (ring_band(position, bands), half, 0, 0)
            )

    for hop in range(half_way + 1):
        for k, head in enumerate(heads):
            if hop == half_way and k == 2:
                continue
            if hop > 0:
                heads[k] = head = turn(head)
                put(chunks[k], swap_core(head), spot + ahead * hop, 1 - halves[k])
            put(chunks[k], head, spot - ahead * hop, halves[k])
    former, latter = (column.reshape(bands, cores * rows, BLOCK) for column in columns)
    update = jnp.where(
        plane == 0,
        jnp.concatenate([former, latter], axis=-1),
        jnp.concatenate([latter, former], axis=-1),
    )
    return (outputs, update)


def solution(mesh):
    placed = (P("dp", None), P(None, "pre"), P("dp", "pre"))
    paired = mesh.shape["dp"] == 2 * D // BLOCK and mesh.shape["pre"] == CB == 2
    return jax.shard_map(
        on_device_paired if paired else on_device_general,
        mesh=mesh,
        in_specs=placed,
        out_specs=(P("dp", "pre"), P(None, "pre", None)),
        check_vma=False,
    )
```

```python
import math

import jax
import jax.numpy as jnp
from jax import lax
from jax.experimental import pallas as pl
from jax.experimental.pallas import tpu as pltpu
from jax.sharding import PartitionSpec as P

D = 4096
BLOCK = 512
CB = 2
ITERS = 3


DAMPING = 0.1
HIGH = lax.Precision.HIGHEST


def batch_dot(former, latter):
    return jnp.einsum(
        "sij,sjk->sik", former, latter, precision=HIGH, preferred_element_type=jnp.float32
    )


def on_device_general(inputs, weight, cotangent):
    groups = lax.axis_size("dp")
    members = lax.axis_size("pre")
    group_id = lax.axis_index("dp")
    member_id = lax.axis_index("pre")
    slab_rows = BLOCK // members
    blocks_all = D // BLOCK * CB
    rounds = max(1, blocks_all // groups)
    sharers = max(1, groups // blocks_all)
    col_width = BLOCK // sharers
    copy_id = group_id // blocks_all
    outputs = jnp.dot(inputs, weight, preferred_element_type=jnp.float32).astype(jnp.bfloat16)
    partial_value = lax.dot_general(
        inputs, cotangent, (((0,), (0,)), ((), ())), preferred_element_type=jnp.float32
    )
    owned_ids = (group_id + groups * jnp.arange(rounds, dtype=jnp.int32)) % blocks_all
    row_offsets = owned_ids // CB * BLOCK
    col_offsets = owned_ids % CB * BLOCK
    gradient = lax.psum(partial_value, "dp")
    row_bands = jax.vmap(lambda offset: lax.dynamic_slice_in_dim(gradient, offset, BLOCK, 0))(
        row_offsets
    )
    wide_band = lax.all_gather(row_bands, "pre", axis=2, tiled=True)
    tile_grad = jax.vmap(
        lambda row_band, offset: lax.dynamic_slice_in_dim(row_band, offset, BLOCK, 1)
    )(wide_band, col_offsets)
    first_row = member_id * slab_rows
    own_rows = lax.dynamic_slice_in_dim(tile_grad, first_row, slab_rows, 1)
    own_cols = lax.dynamic_slice_in_dim(tile_grad, first_row, slab_rows, 2)
    left_rows = jnp.einsum(
        "sij,skj->sik", own_rows, tile_grad, precision=HIGH, preferred_element_type=jnp.float32
    )
    right_rows = jnp.einsum(
        "sji,sjk->sik", own_cols, tile_grad, precision=HIGH, preferred_element_type=jnp.float32
    )
    stat_rows = jnp.stack([left_rows, right_rows], axis=1).reshape(rounds * 2, slab_rows, BLOCK)
    tile_energy = jnp.sum(tile_grad * tile_grad, axis=(1, 2))
    energy = jnp.stack([tile_energy, tile_energy], axis=1).reshape(rounds * 2)
    unit_rows = (jnp.arange(BLOCK)[None, :] == (first_row + jnp.arange(slab_rows))[:, None]).astype(
        jnp.float32
    )
    unit_eye = jnp.eye(BLOCK, dtype=jnp.float32)
    state_rows = stat_rows + (DAMPING * energy / BLOCK)[:, None, None] * unit_rows[None]
    root_rows = unit_rows[None]
    for iteration in range(ITERS):
        full_state = lax.all_gather(state_rows, "pre", axis=1, tiled=True)
        if iteration == 0:
            frob_norm = jnp.sqrt(jnp.sum(full_state * full_state, axis=(1, 2)))
            full_state = full_state / frob_norm[:, None, None]
            state_rows = state_rows / frob_norm[:, None, None]
            root_rows = unit_rows[None] * (frob_norm ** (-0.25))[:, None, None]
        factor = (5.0 * unit_eye - full_state) * 0.25
        square = batch_dot(factor, factor)
        square_rows = lax.dynamic_slice_in_dim(square, first_row, slab_rows, 1)
        fourth_rows = batch_dot(square_rows, square)
        state_rows = batch_dot(fourth_rows, full_state)
        root_rows = batch_dot(root_rows, factor)
    root_half = root_rows.astype(jnp.bfloat16).reshape(rounds, 2, slab_rows, BLOCK)
    right_full = lax.all_gather(root_half[:, 1], "pre", axis=1, tiled=True)
    right_cols = lax.dynamic_slice_in_dim(right_full, copy_id * col_width, col_width, 2)
    tile_half = tile_grad.astype(jnp.bfloat16)
    half_prod = jnp.einsum(
        "sij,sjk->sik", root_half[:, 0], tile_half, preferred_element_type=jnp.float32
    ).astype(jnp.bfloat16)
    piece_rows = jnp.einsum(
        "sij,sjk->sik", half_prod, right_cols, preferred_element_type=jnp.float32
    )
    piece_rows = (piece_rows * math.sqrt(BLOCK)).astype(jnp.bfloat16)
    collected = lax.all_gather(piece_rows[None], "dp", axis=0, tiled=True)
    if sharers == 1:
        ordered = jnp.swapaxes(collected, 0, 1).reshape(blocks_all, slab_rows, BLOCK)
    else:
        ordered = (
            collected[:, 0]
            .reshape(sharers, blocks_all, slab_rows, col_width)
            .transpose(1, 2, 0, 3)
            .reshape(blocks_all, slab_rows, BLOCK)
        )
    update = (
        ordered.reshape(D // BLOCK, CB, slab_rows, BLOCK)
        .transpose(0, 2, 1, 3)
        .reshape(D // BLOCK, slab_rows, CB * BLOCK)
    )
    return (outputs, update)


def contract(former, latter, former_dim, latter_dim):
    return lax.dot_general(
        former,
        latter,
        (((former_dim,), (latter_dim,)), ((), ())),
        preferred_element_type=jnp.float32,
    )


def product(former, latter):
    return contract(former.astype(jnp.bfloat16), latter.astype(jnp.bfloat16), 1, 0)


def total(array):
    return jnp.sum(jnp.sum(array, axis=0, keepdims=True), axis=1, keepdims=True)


def newton_step(states):
    excesses = [product(m, m) * (1.0 / 16.0) - 0.625 * m for m in states]
    growths = [3.125 * e + product(e, e) for e in excesses]
    return [(625.0 / 256.0) * m + product(m, g) for m, g in zip(states, growths)]


def inverse_roots(tile):
    tile_half = tile.astype(jnp.bfloat16)
    order = tile.shape[0]
    row_ids = lax.broadcasted_iota(jnp.int32, (order, order), 0)
    col_ids = lax.broadcasted_iota(jnp.int32, (order, order), 1)
    on_diagonal = row_ids == col_ids
    damp = (DAMPING / order) * total(tile * tile)
    stats = [contract(tile_half, tile_half, 1, 1), contract(tile_half, tile_half, 0, 0)]
    stats = [jnp.where(on_diagonal, stat + damp, stat) for stat in stats]
    norms = [jnp.sqrt(total(stat * stat)) for stat in stats]
    firsts = [stat / norm for stat, norm in zip(stats, norms)]
    seconds = newton_step(firsts)
    thirds = newton_step(seconds)
    crosses = [
        product(m, n) * (1.0 / 16.0) - (5.0 / 16.0) * (m + n) for m, n in zip(firsts, seconds)
    ]
    roots = []
    for cross, third, norm in zip(crosses, thirds, norms):
        root = 1.25 * cross - 0.25 * product(cross, third) - (25.0 / 64.0) * third
        root = jnp.where(on_diagonal, root + 125.0 / 64.0, root)
        roots.append((root / jnp.sqrt(jnp.sqrt(norm))).astype(jnp.bfloat16))
    return roots


def update_kernel(side_ref, mine_ref, other_ref, near_ref, next_ref, far_ref, left_ref):
    tile = mine_ref[...] + other_ref[...]
    tile_half = tile.astype(jnp.bfloat16)
    left_ref[...], right = inverse_roots(tile)
    rows = near_ref.shape[0]
    core, plane = side_ref[0], side_ref[1]
    for out_ref, part in (
        (near_ref, 2 * plane + core),
        (next_ref, 2 * plane + 1 - core),
        (far_ref, 2 * (1 - plane) + core),
    ):
        left = left_ref[pl.ds(pl.multiple_of(part * rows, rows), rows), :]
        half = contract(left, tile_half, 1, 0).astype(jnp.bfloat16)
        piece = contract(half, right, 1, 0) * math.sqrt(BLOCK)
        out_ref[...] = piece.astype(jnp.bfloat16)


OFFSETS = ((4, 7, 2), (5, 6, 3))
SHARED = 1


def pack_kernel(place_ref, inputs_ref, *piece_refs):
    for step, piece_ref in enumerate(piece_refs):
        first_col = pl.multiple_of(place_ref[step] * BLOCK, BLOCK)
        piece_ref[...] = inputs_ref[:, pl.ds(first_col, BLOCK)]


def ring_band(position, bands):
    position = (position + 2 * bands) % bands
    return jnp.where(position < bands // 2, 2 * position, 2 * (bands - 1 - position) + 1)


def tile_kernel(place_ref, own_ref, shared_ref, *refs):
    hops = len(OFFSETS[0])
    near_refs, far_refs = refs[:hops], refs[hops : 2 * hops]
    cot_refs = refs[2 * hops : -3]
    partial_ref, band_ref, cot_ref = refs[-3:]
    plane, band = place_ref[0], place_ref[1]
    tokens = own_ref.shape[0]

    def put(to_ref, piece_ref, source):
        first_row = pl.multiple_of(source * tokens, tokens)
        to_ref[pl.ds(first_row, tokens), :] = piece_ref[...]

    put(band_ref, own_ref, band)
    put(band_ref, shared_ref, band ^ SHARED)
    for hop in range(hops):
        for piece_ref, member in ((near_refs[hop], plane), (far_refs[hop], 1 - plane)):
            put(band_ref, piece_ref, band ^ jnp.where(member == 0, OFFSETS[0][hop], OFFSETS[1][hop]))
    for offset, pair_ref in enumerate(cot_refs):
        for part, source in enumerate((band ^ offset, band ^ offset ^ 4)):
            put(cot_ref, pair_ref.at[pl.ds(part * tokens, tokens)], source)
    partial_ref[...] = contract(band_ref[...], cot_ref[...], 0, 0)


def call(kernel, out_shapes, scratch_shapes, *operands):
    in_specs = [pl.BlockSpec(memory_space=pltpu.SMEM)]
    in_specs += [pl.BlockSpec(memory_space=pltpu.VMEM)] * (len(operands) - 1)
    return pl.pallas_call(
        kernel,
        out_shape=out_shapes,
        in_specs=in_specs,
        out_specs=[pl.BlockSpec(memory_space=pltpu.VMEM)] * len(out_shapes),
        scratch_shapes=scratch_shapes,
        compiler_params=pltpu.CompilerParams(vmem_limit_bytes=32 * 1024 * 1024),
    )(*operands)


def on_device_paired(inputs, weight, cotangent):
    bands = D // BLOCK
    groups = lax.axis_size("dp")
    cores = groups // bands
    members = lax.axis_size("pre")
    core = lax.axis_index("dp") % cores
    band = lax.axis_index("dp") // cores
    plane = lax.axis_index("pre")
    tokens = inputs.shape[0]
    ahead = 1 - 2 * core
    spot = jnp.where(band % 2 == 0, band // 2, bands - 1 - band // 2)

    ring = list(range(0, bands, 2)) + list(range(bands - 1, 0, -2))

    def swap_core(array):
        return lax.ppermute(array, "dp", [(g, g ^ 1) for g in range(groups)])

    def swap_plane(array):
        return lax.ppermute(array, "pre", [(c, members - 1 - c) for c in range(members)])

    def deal(array, hop):
        pairs = [
            (
                (k * cores + c) * members + m,
                ((k ^ OFFSETS[m][hop]) * cores + c) * members + m,
            )
            for k in range(bands)
            for c in range(cores)
            for m in range(members)
        ]
        return lax.ppermute(array, ("dp", "pre"), pairs)

    hops = range(len(OFFSETS[0]))
    bands_out = [band ^ jnp.where(plane == 0, OFFSETS[0][hop], OFFSETS[1][hop]) for hop in hops]
    *packed, own_band = call(
        pack_kernel,
        [jax.ShapeDtypeStruct((tokens, BLOCK), inputs.dtype)] * (len(hops) + 2),
        [],
        jnp.stack(bands_out + [band ^ SHARED, band]).astype(jnp.int32),
        inputs,
    )

    def exchange(array, offset):
        pairs = [
            (k * cores + c, (k ^ offset) * cores + c) for k in range(bands) for c in range(cores)
        ]
        return lax.ppermute(array, "dp", pairs)

    def project(columns):
        out = jnp.dot(inputs, weight[:, columns], preferred_element_type=jnp.float32)
        return out.astype(jnp.bfloat16)

    head_columns = weight.shape[1] // 4
    far_cot, head_outputs = lax.optimization_barrier(
        (exchange(cotangent, 4), project(slice(0, head_columns)))
    )
    near = [deal(packed[hop], hop) for hop in hops]
    shared = exchange(packed[-1], SHARED)
    pair = jnp.concatenate([cotangent, far_cot])
    cots = [pair] + [exchange(pair, offset) for offset in (1, 2, 3)]
    far = [swap_plane(piece) for piece in near]
    rows = BLOCK // members // cores
    columns = [jnp.zeros((bands, cores, rows, BLOCK), jnp.bfloat16) for _ in range(2)]
    own_band, tail_outputs, *columns = lax.optimization_barrier(
        (own_band, project(slice(head_columns, None)), *columns)
    )
    outputs = jnp.concatenate([head_outputs, tail_outputs], axis=1)
    (partial_tile,) = call(
        tile_kernel,
        [jax.ShapeDtypeStruct((BLOCK, BLOCK), jnp.float32)],
        [pltpu.VMEM((bands * tokens, BLOCK), inputs.dtype)] * 2,
        jnp.stack([plane, band]).astype(jnp.int32),
        own_band,
        shared,
        *near,
        *far,
        *cots,
    )
    other_partial = swap_core(partial_tile)
    side = jnp.stack([core, plane]).astype(jnp.int32)
    near_piece, next_piece, far_piece = call(
        update_kernel,
        [jax.ShapeDtypeStruct((rows, BLOCK), jnp.bfloat16)] * 3,
        [pltpu.VMEM((BLOCK, BLOCK), jnp.bfloat16)],
        side,
        partial_tile,
        other_partial,
    )

    def turn(array):
        pairs = [
            (ring[k] * cores + c, ring[(k + 1 - 2 * c) % bands] * cores + c)
            for k in range(bands)
            for c in range(cores)
        ]
        return lax.ppermute(array, "dp", pairs)

    half_way = bands // 2
    crossed = swap_plane(far_piece)
    heads = [near_piece, next_piece, crossed, swap_core(crossed)]

    def put(chunk, piece, position, half):
        columns[chunk] = lax.dynamic_update_slice(
            columns[chunk], piece[None, None], (ring_band(position, bands), half, 0, 0)
        )

    for hop in range(half_way + 1):
        for k, head in enumerate(heads):
            chunk, half = k // 2, (core if k % 2 == 0 else 1 - core)
            if hop == half_way and k % 2 == 1:
                continue
            if hop > 0:
                heads[k] = head = turn(head)
                put(chunk, swap_core(head), spot + ahead * hop, 1 - half)
            put(chunk, head, spot - ahead * hop, half)
    former, latter = (column.reshape(bands, cores * rows, BLOCK) for column in columns)
    update = jnp.where(
        plane == 0,
        jnp.concatenate([former, latter], axis=-1),
        jnp.concatenate([latter, former], axis=-1),
    )
    return (outputs, update)


def solution(mesh):
    placed = (P("dp", None), P(None, "pre"), P("dp", "pre"))
    paired = mesh.shape["dp"] == 2 * D // BLOCK and mesh.shape["pre"] == CB == 2
    return jax.shard_map(
        on_device_paired if paired else on_device_general,
        mesh=mesh,
        in_specs=placed,
        out_specs=(P("dp", "pre"), P(None, "pre", None)),
        check_vma=False,
    )
```

```python
import math

import jax
import jax.numpy as jnp
from jax import lax
from jax.experimental import pallas as pl
from jax.experimental.pallas import tpu as pltpu
from jax.sharding import PartitionSpec as P

D = 4096
BLOCK = 512
CB = 2
ITERS = 3


DAMPING = 0.1
HIGH = lax.Precision.HIGHEST


def batch_dot(former, latter):
    return jnp.einsum(
        "sij,sjk->sik", former, latter, precision=HIGH, preferred_element_type=jnp.float32
    )


def on_device_general(inputs, weight, cotangent):
    groups = lax.axis_size("dp")
    members = lax.axis_size("pre")
    group_id = lax.axis_index("dp")
    member_id = lax.axis_index("pre")
    slab_rows = BLOCK // members
    blocks_all = D // BLOCK * CB
    rounds = max(1, blocks_all // groups)
    sharers = max(1, groups // blocks_all)
    col_width = BLOCK // sharers
    copy_id = group_id // blocks_all
    outputs = jnp.dot(inputs, weight, preferred_element_type=jnp.float32).astype(jnp.bfloat16)
    partial_value = lax.dot_general(
        inputs, cotangent, (((0,), (0,)), ((), ())), preferred_element_type=jnp.float32
    )
    owned_ids = (group_id + groups * jnp.arange(rounds, dtype=jnp.int32)) % blocks_all
    row_offsets = owned_ids // CB * BLOCK
    col_offsets = owned_ids % CB * BLOCK
    gradient = lax.psum(partial_value, "dp")
    row_bands = jax.vmap(lambda offset: lax.dynamic_slice_in_dim(gradient, offset, BLOCK, 0))(
        row_offsets
    )
    wide_band = lax.all_gather(row_bands, "pre", axis=2, tiled=True)
    tile_grad = jax.vmap(
        lambda row_band, offset: lax.dynamic_slice_in_dim(row_band, offset, BLOCK, 1)
    )(wide_band, col_offsets)
    first_row = member_id * slab_rows
    own_rows = lax.dynamic_slice_in_dim(tile_grad, first_row, slab_rows, 1)
    own_cols = lax.dynamic_slice_in_dim(tile_grad, first_row, slab_rows, 2)
    left_rows = jnp.einsum(
        "sij,skj->sik", own_rows, tile_grad, precision=HIGH, preferred_element_type=jnp.float32
    )
    right_rows = jnp.einsum(
        "sji,sjk->sik", own_cols, tile_grad, precision=HIGH, preferred_element_type=jnp.float32
    )
    stat_rows = jnp.stack([left_rows, right_rows], axis=1).reshape(rounds * 2, slab_rows, BLOCK)
    tile_energy = jnp.sum(tile_grad * tile_grad, axis=(1, 2))
    energy = jnp.stack([tile_energy, tile_energy], axis=1).reshape(rounds * 2)
    unit_rows = (jnp.arange(BLOCK)[None, :] == (first_row + jnp.arange(slab_rows))[:, None]).astype(
        jnp.float32
    )
    unit_eye = jnp.eye(BLOCK, dtype=jnp.float32)
    state_rows = stat_rows + (DAMPING * energy / BLOCK)[:, None, None] * unit_rows[None]
    root_rows = unit_rows[None]
    for iteration in range(ITERS):
        full_state = lax.all_gather(state_rows, "pre", axis=1, tiled=True)
        if iteration == 0:
            frob_norm = jnp.sqrt(jnp.sum(full_state * full_state, axis=(1, 2)))
            full_state = full_state / frob_norm[:, None, None]
            state_rows = state_rows / frob_norm[:, None, None]
            root_rows = unit_rows[None] * (frob_norm ** (-0.25))[:, None, None]
        factor = (5.0 * unit_eye - full_state) * 0.25
        square = batch_dot(factor, factor)
        square_rows = lax.dynamic_slice_in_dim(square, first_row, slab_rows, 1)
        fourth_rows = batch_dot(square_rows, square)
        state_rows = batch_dot(fourth_rows, full_state)
        root_rows = batch_dot(root_rows, factor)
    root_half = root_rows.astype(jnp.bfloat16).reshape(rounds, 2, slab_rows, BLOCK)
    right_full = lax.all_gather(root_half[:, 1], "pre", axis=1, tiled=True)
    right_cols = lax.dynamic_slice_in_dim(right_full, copy_id * col_width, col_width, 2)
    tile_half = tile_grad.astype(jnp.bfloat16)
    half_prod = jnp.einsum(
        "sij,sjk->sik", root_half[:, 0], tile_half, preferred_element_type=jnp.float32
    ).astype(jnp.bfloat16)
    piece_rows = jnp.einsum(
        "sij,sjk->sik", half_prod, right_cols, preferred_element_type=jnp.float32
    )
    piece_rows = (piece_rows * math.sqrt(BLOCK)).astype(jnp.bfloat16)
    collected = lax.all_gather(piece_rows[None], "dp", axis=0, tiled=True)
    if sharers == 1:
        ordered = jnp.swapaxes(collected, 0, 1).reshape(blocks_all, slab_rows, BLOCK)
    else:
        ordered = (
            collected[:, 0]
            .reshape(sharers, blocks_all, slab_rows, col_width)
            .transpose(1, 2, 0, 3)
            .reshape(blocks_all, slab_rows, BLOCK)
        )
    update = (
        ordered.reshape(D // BLOCK, CB, slab_rows, BLOCK)
        .transpose(0, 2, 1, 3)
        .reshape(D // BLOCK, slab_rows, CB * BLOCK)
    )
    return (outputs, update)


def contract(former, latter, former_dim, latter_dim):
    return lax.dot_general(
        former,
        latter,
        (((former_dim,), (latter_dim,)), ((), ())),
        preferred_element_type=jnp.float32,
    )


def product(former, latter):
    return contract(former.astype(jnp.bfloat16), latter.astype(jnp.bfloat16), 1, 0)


def total(array):
    return jnp.sum(jnp.sum(array, axis=0, keepdims=True), axis=1, keepdims=True)


def newton_step(states):
    excesses = [product(m, m) * (1.0 / 16.0) - 0.625 * m for m in states]
    growths = [3.125 * e + product(e, e) for e in excesses]
    return [(625.0 / 256.0) * m + product(m, g) for m, g in zip(states, growths)]


def inverse_roots(tile):
    tile_half = tile.astype(jnp.bfloat16)
    order = tile.shape[0]
    row_ids = lax.broadcasted_iota(jnp.int32, (order, order), 0)
    col_ids = lax.broadcasted_iota(jnp.int32, (order, order), 1)
    on_diagonal = row_ids == col_ids
    damp = (DAMPING / order) * total(tile * tile)
    stats = [contract(tile_half, tile_half, 1, 1), contract(tile_half, tile_half, 0, 0)]
    stats = [jnp.where(on_diagonal, stat + damp, stat) for stat in stats]
    norms = [jnp.sqrt(total(stat * stat)) for stat in stats]
    firsts = [stat / norm for stat, norm in zip(stats, norms)]
    seconds = newton_step(firsts)
    thirds = newton_step(seconds)
    crosses = [
        product(m, n) * (1.0 / 16.0) - (5.0 / 16.0) * (m + n) for m, n in zip(firsts, seconds)
    ]
    roots = []
    for cross, third, norm in zip(crosses, thirds, norms):
        root = 1.25 * cross - 0.25 * product(cross, third) - (25.0 / 64.0) * third
        root = jnp.where(on_diagonal, root + 125.0 / 64.0, root)
        roots.append((root / jnp.sqrt(jnp.sqrt(norm))).astype(jnp.bfloat16))
    return roots


def update_kernel(side_ref, mine_ref, other_ref, near_ref, next_ref, far_ref, left_ref):
    tile = mine_ref[...] + other_ref[...]
    tile_half = tile.astype(jnp.bfloat16)
    left_ref[...], right = inverse_roots(tile)
    rows = near_ref.shape[0]
    core, plane = side_ref[0], side_ref[1]
    for out_ref, part in (
        (near_ref, 2 * plane + core),
        (next_ref, 2 * plane + 1 - core),
        (far_ref, 2 * (1 - plane) + core),
    ):
        left = left_ref[pl.ds(pl.multiple_of(part * rows, rows), rows), :]
        half = contract(left, tile_half, 1, 0).astype(jnp.bfloat16)
        piece = contract(half, right, 1, 0) * math.sqrt(BLOCK)
        out_ref[...] = piece.astype(jnp.bfloat16)


OFFSETS = ((4, 7, 2), (5, 6, 3))
SHARED = 1


def pack_kernel(place_ref, inputs_ref, *piece_refs):
    for step, piece_ref in enumerate(piece_refs):
        first_col = pl.multiple_of(place_ref[step] * BLOCK, BLOCK)
        piece_ref[...] = inputs_ref[:, pl.ds(first_col, BLOCK)]


def ring_band(position, bands):
    position = (position + 2 * bands) % bands
    return jnp.where(position < bands // 2, 2 * position, 2 * (bands - 1 - position) + 1)


def tile_kernel(place_ref, own_ref, shared_ref, *refs):
    hops = len(OFFSETS[0])
    near_refs, far_refs = refs[:hops], refs[hops : 2 * hops]
    cot_refs = refs[2 * hops : -3]
    partial_ref, band_ref, cot_ref = refs[-3:]
    plane, band = place_ref[0], place_ref[1]
    tokens = own_ref.shape[0]

    def put(to_ref, piece_ref, source):
        first_row = pl.multiple_of(source * tokens, tokens)
        to_ref[pl.ds(first_row, tokens), :] = piece_ref[...]

    put(band_ref, own_ref, band)
    put(band_ref, shared_ref, band ^ SHARED)
    for hop in range(hops):
        for piece_ref, member in ((near_refs[hop], plane), (far_refs[hop], 1 - plane)):
            put(band_ref, piece_ref, band ^ jnp.where(member == 0, OFFSETS[0][hop], OFFSETS[1][hop]))
    for offset, pair_ref in enumerate(cot_refs):
        for part, source in enumerate((band ^ offset, band ^ offset ^ 4)):
            put(cot_ref, pair_ref.at[pl.ds(part * tokens, tokens)], source)
    partial_ref[...] = contract(band_ref[...], cot_ref[...], 0, 0)


def call(kernel, out_shapes, scratch_shapes, *operands):
    in_specs = [pl.BlockSpec(memory_space=pltpu.SMEM)]
    in_specs += [pl.BlockSpec(memory_space=pltpu.VMEM)] * (len(operands) - 1)
    return pl.pallas_call(
        kernel,
        out_shape=out_shapes,
        in_specs=in_specs,
        out_specs=[pl.BlockSpec(memory_space=pltpu.VMEM)] * len(out_shapes),
        scratch_shapes=scratch_shapes,
        compiler_params=pltpu.CompilerParams(vmem_limit_bytes=32 * 1024 * 1024),
    )(*operands)


def on_device_paired(inputs, weight, cotangent):
    bands = D // BLOCK
    groups = lax.axis_size("dp")
    cores = groups // bands
    members = lax.axis_size("pre")
    core = lax.axis_index("dp") % cores
    band = lax.axis_index("dp") // cores
    plane = lax.axis_index("pre")
    tokens = inputs.shape[0]
    ahead = 1 - 2 * core
    spot = jnp.where(band % 2 == 0, band // 2, bands - 1 - band // 2)

    ring = list(range(0, bands, 2)) + list(range(bands - 1, 0, -2))

    def swap_core(array):
        return lax.ppermute(array, "dp", [(g, g ^ 1) for g in range(groups)])

    def swap_plane(array):
        return lax.ppermute(array, "pre", [(c, members - 1 - c) for c in range(members)])

    def deal(array, hop):
        pairs = [
            (
                (k * cores + c) * members + m,
                ((k ^ OFFSETS[m][hop]) * cores + c) * members + m,
            )
            for k in range(bands)
            for c in range(cores)
            for m in range(members)
        ]
        return lax.ppermute(array, ("dp", "pre"), pairs)

    hops = range(len(OFFSETS[0]))
    bands_out = [band ^ jnp.where(plane == 0, OFFSETS[0][hop], OFFSETS[1][hop]) for hop in hops]
    *packed, own_band = call(
        pack_kernel,
        [jax.ShapeDtypeStruct((tokens, BLOCK), inputs.dtype)] * (len(hops) + 2),
        [],
        jnp.stack(bands_out + [band ^ SHARED, band]).astype(jnp.int32),
        inputs,
    )

    def exchange(array, offset):
        pairs = [
            (k * cores + c, (k ^ offset) * cores + c) for k in range(bands) for c in range(cores)
        ]
        return lax.ppermute(array, "dp", pairs)

    outputs = jnp.dot(inputs, weight, preferred_element_type=jnp.float32).astype(jnp.bfloat16)
    far_cot, outputs = lax.optimization_barrier((exchange(cotangent, 4), outputs))
    near = [deal(packed[hop], hop) for hop in hops]
    shared = exchange(packed[-1], SHARED)
    pair = jnp.concatenate([cotangent, far_cot])
    cots = [pair] + [exchange(pair, offset) for offset in (1, 2, 3)]
    far = [swap_plane(piece) for piece in near]
    (partial_tile,) = call(
        tile_kernel,
        [jax.ShapeDtypeStruct((BLOCK, BLOCK), jnp.float32)],
        [pltpu.VMEM((bands * tokens, BLOCK), inputs.dtype)] * 2,
        jnp.stack([plane, band]).astype(jnp.int32),
        own_band,
        shared,
        *near,
        *far,
        *cots,
    )
    other_partial = swap_core(partial_tile)
    side = jnp.stack([core, plane]).astype(jnp.int32)
    rows = BLOCK // members // cores
    near_piece, next_piece, far_piece = call(
        update_kernel,
        [jax.ShapeDtypeStruct((rows, BLOCK), jnp.bfloat16)] * 3,
        [pltpu.VMEM((BLOCK, BLOCK), jnp.bfloat16)],
        side,
        partial_tile,
        other_partial,
    )

    def turn(array):
        pairs = [
            (ring[k] * cores + c, ring[(k + 1 - 2 * c) % bands] * cores + c)
            for k in range(bands)
            for c in range(cores)
        ]
        return lax.ppermute(array, "dp", pairs)

    half_way = bands // 2
    crossed = swap_plane(far_piece)
    heads = [near_piece, next_piece, crossed, swap_core(crossed)]
    columns = [jnp.zeros((bands, cores, rows, BLOCK), jnp.bfloat16)] * 2

    def put(chunk, piece, position, half):
        columns[chunk] = lax.dynamic_update_slice(
            columns[chunk], piece[None, None], (ring_band(position, bands), half, 0, 0)
        )

    def join(own, other):
        return jnp.where(
            plane == 0,
            jnp.concatenate([own, other], axis=-1),
            jnp.concatenate([other, own], axis=-1),
        )

    for hop in range(half_way):
        for k, head in enumerate(heads):
            chunk, half = k // 2, (core if k % 2 == 0 else 1 - core)
            if hop > 0:
                heads[k] = head = turn(head)
                put(chunk, swap_core(head), spot + ahead * hop, 1 - half)
            put(chunk, head, spot - ahead * hop, half)
    update = join(*(column.reshape(bands, cores * rows, BLOCK) for column in columns))
    opposite = []
    for head in heads[::2]:
        mine = turn(head)
        other = swap_core(mine)
        opposite.append(
            jnp.where(core == 0, jnp.concatenate([mine, other]), jnp.concatenate([other, mine]))
        )
    update = lax.dynamic_update_slice(
        update, join(*opposite)[None], (ring_band(spot + half_way, bands), 0, 0)
    )
    return (outputs, update)


def solution(mesh):
    placed = (P("dp", None), P(None, "pre"), P("dp", "pre"))
    paired = mesh.shape["dp"] == 2 * D // BLOCK and mesh.shape["pre"] == CB == 2
    return jax.shard_map(
        on_device_paired if paired else on_device_general,
        mesh=mesh,
        in_specs=placed,
        out_specs=(P("dp", "pre"), P(None, "pre", None)),
        check_vma=False,
    )
```

```python
import math

import jax
import jax.numpy as jnp
from jax import lax
from jax.experimental import pallas as pl
from jax.experimental.pallas import tpu as pltpu
from jax.sharding import PartitionSpec as P

D = 4096
BLOCK = 512
CB = 2
ITERS = 3


DAMPING = 0.1
HIGH = lax.Precision.HIGHEST


def batch_dot(former, latter):
    return jnp.einsum(
        "sij,sjk->sik", former, latter, precision=HIGH, preferred_element_type=jnp.float32
    )


def on_device_general(inputs, weight, cotangent):
    groups = lax.axis_size("dp")
    members = lax.axis_size("pre")
    group_id = lax.axis_index("dp")
    member_id = lax.axis_index("pre")
    slab_rows = BLOCK // members
    blocks_all = D // BLOCK * CB
    rounds = max(1, blocks_all // groups)
    sharers = max(1, groups // blocks_all)
    col_width = BLOCK // sharers
    copy_id = group_id // blocks_all
    outputs = jnp.dot(inputs, weight, preferred_element_type=jnp.float32).astype(jnp.bfloat16)
    partial_value = lax.dot_general(
        inputs, cotangent, (((0,), (0,)), ((), ())), preferred_element_type=jnp.float32
    )
    owned_ids = (group_id + groups * jnp.arange(rounds, dtype=jnp.int32)) % blocks_all
    row_offsets = owned_ids // CB * BLOCK
    col_offsets = owned_ids % CB * BLOCK
    gradient = lax.psum(partial_value, "dp")
    row_bands = jax.vmap(lambda offset: lax.dynamic_slice_in_dim(gradient, offset, BLOCK, 0))(
        row_offsets
    )
    wide_band = lax.all_gather(row_bands, "pre", axis=2, tiled=True)
    tile_grad = jax.vmap(
        lambda row_band, offset: lax.dynamic_slice_in_dim(row_band, offset, BLOCK, 1)
    )(wide_band, col_offsets)
    first_row = member_id * slab_rows
    own_rows = lax.dynamic_slice_in_dim(tile_grad, first_row, slab_rows, 1)
    own_cols = lax.dynamic_slice_in_dim(tile_grad, first_row, slab_rows, 2)
    left_rows = jnp.einsum(
        "sij,skj->sik", own_rows, tile_grad, precision=HIGH, preferred_element_type=jnp.float32
    )
    right_rows = jnp.einsum(
        "sji,sjk->sik", own_cols, tile_grad, precision=HIGH, preferred_element_type=jnp.float32
    )
    stat_rows = jnp.stack([left_rows, right_rows], axis=1).reshape(rounds * 2, slab_rows, BLOCK)
    tile_energy = jnp.sum(tile_grad * tile_grad, axis=(1, 2))
    energy = jnp.stack([tile_energy, tile_energy], axis=1).reshape(rounds * 2)
    unit_rows = (jnp.arange(BLOCK)[None, :] == (first_row + jnp.arange(slab_rows))[:, None]).astype(
        jnp.float32
    )
    unit_eye = jnp.eye(BLOCK, dtype=jnp.float32)
    state_rows = stat_rows + (DAMPING * energy / BLOCK)[:, None, None] * unit_rows[None]
    root_rows = unit_rows[None]
    for iteration in range(ITERS):
        full_state = lax.all_gather(state_rows, "pre", axis=1, tiled=True)
        if iteration == 0:
            frob_norm = jnp.sqrt(jnp.sum(full_state * full_state, axis=(1, 2)))
            full_state = full_state / frob_norm[:, None, None]
            state_rows = state_rows / frob_norm[:, None, None]
            root_rows = unit_rows[None] * (frob_norm ** (-0.25))[:, None, None]
        factor = (5.0 * unit_eye - full_state) * 0.25
        square = batch_dot(factor, factor)
        square_rows = lax.dynamic_slice_in_dim(square, first_row, slab_rows, 1)
        fourth_rows = batch_dot(square_rows, square)
        state_rows = batch_dot(fourth_rows, full_state)
        root_rows = batch_dot(root_rows, factor)
    root_half = root_rows.astype(jnp.bfloat16).reshape(rounds, 2, slab_rows, BLOCK)
    right_full = lax.all_gather(root_half[:, 1], "pre", axis=1, tiled=True)
    right_cols = lax.dynamic_slice_in_dim(right_full, copy_id * col_width, col_width, 2)
    tile_half = tile_grad.astype(jnp.bfloat16)
    half_prod = jnp.einsum(
        "sij,sjk->sik", root_half[:, 0], tile_half, preferred_element_type=jnp.float32
    ).astype(jnp.bfloat16)
    piece_rows = jnp.einsum(
        "sij,sjk->sik", half_prod, right_cols, preferred_element_type=jnp.float32
    )
    piece_rows = (piece_rows * math.sqrt(BLOCK)).astype(jnp.bfloat16)
    collected = lax.all_gather(piece_rows[None], "dp", axis=0, tiled=True)
    if sharers == 1:
        ordered = jnp.swapaxes(collected, 0, 1).reshape(blocks_all, slab_rows, BLOCK)
    else:
        ordered = (
            collected[:, 0]
            .reshape(sharers, blocks_all, slab_rows, col_width)
            .transpose(1, 2, 0, 3)
            .reshape(blocks_all, slab_rows, BLOCK)
        )
    update = (
        ordered.reshape(D // BLOCK, CB, slab_rows, BLOCK)
        .transpose(0, 2, 1, 3)
        .reshape(D // BLOCK, slab_rows, CB * BLOCK)
    )
    return (outputs, update)


def contract(former, latter, former_dim, latter_dim):
    return lax.dot_general(
        former,
        latter,
        (((former_dim,), (latter_dim,)), ((), ())),
        preferred_element_type=jnp.float32,
    )


def product(former, latter):
    return contract(former.astype(jnp.bfloat16), latter.astype(jnp.bfloat16), 1, 0)


def total(array):
    return jnp.sum(jnp.sum(array, axis=0, keepdims=True), axis=1, keepdims=True)


def newton_step(states):
    excesses = [product(m, m) * (1.0 / 16.0) - 0.625 * m for m in states]
    growths = [3.125 * e + product(e, e) for e in excesses]
    return [(625.0 / 256.0) * m + product(m, g) for m, g in zip(states, growths)]


def inverse_roots(tile):
    tile_half = tile.astype(jnp.bfloat16)
    order = tile.shape[0]
    row_ids = lax.broadcasted_iota(jnp.int32, (order, order), 0)
    col_ids = lax.broadcasted_iota(jnp.int32, (order, order), 1)
    on_diagonal = row_ids == col_ids
    damp = (DAMPING / order) * total(tile * tile)
    stats = [contract(tile_half, tile_half, 1, 1), contract(tile_half, tile_half, 0, 0)]
    stats = [jnp.where(on_diagonal, stat + damp, stat) for stat in stats]
    norms = [jnp.sqrt(total(stat * stat)) for stat in stats]
    firsts = [stat * (1.0 / norm) for stat, norm in zip(stats, norms)]
    seconds = newton_step(firsts)
    thirds = newton_step(seconds)
    crosses = [
        product(m, n) * (1.0 / 16.0) - (5.0 / 16.0) * (m + n) for m, n in zip(firsts, seconds)
    ]
    roots = []
    for cross, third, norm in zip(crosses, thirds, norms):
        root = 1.25 * cross - 0.25 * product(cross, third) - (25.0 / 64.0) * third
        root = jnp.where(on_diagonal, root + 125.0 / 64.0, root)
        scale = 1.0 / jnp.sqrt(jnp.sqrt(norm))
        roots.append((root * scale).astype(jnp.bfloat16))
    return roots


def update_kernel(side_ref, mine_ref, other_ref, near_ref, next_ref, far_ref, left_ref):
    tile = mine_ref[...] + other_ref[...]
    tile_half = tile.astype(jnp.bfloat16)
    left_ref[...], right = inverse_roots(tile)
    rows = near_ref.shape[0]
    core, plane = side_ref[0], side_ref[1]
    for out_ref, part in (
        (near_ref, 2 * plane + core),
        (next_ref, 2 * plane + 1 - core),
        (far_ref, 2 * (1 - plane) + core),
    ):
        left = left_ref[pl.ds(pl.multiple_of(part * rows, rows), rows), :]
        half = contract(left, tile_half, 1, 0).astype(jnp.bfloat16)
        piece = contract(half, right, 1, 0) * math.sqrt(BLOCK)
        out_ref[...] = piece.astype(jnp.bfloat16)


OFFSETS = ((4, 7, 2), (5, 6, 3))
SHARED = 1


def pack_kernel(place_ref, inputs_ref, *piece_refs):
    for step, piece_ref in enumerate(piece_refs):
        first_col = pl.multiple_of(place_ref[step] * BLOCK, BLOCK)
        piece_ref[...] = inputs_ref[:, pl.ds(first_col, BLOCK)]


def ring_band(position, bands):
    position = (position + 2 * bands) % bands
    return jnp.where(position < bands // 2, 2 * position, 2 * (bands - 1 - position) + 1)


def tile_kernel(place_ref, own_ref, shared_ref, *refs):
    hops = len(OFFSETS[0])
    near_refs, far_refs = refs[:hops], refs[hops : 2 * hops]
    cot_refs = refs[2 * hops : -3]
    partial_ref, band_ref, cot_ref = refs[-3:]
    plane, band = place_ref[0], place_ref[1]
    tokens = own_ref.shape[0]

    def put(to_ref, piece_ref, source):
        first_row = pl.multiple_of(source * tokens, tokens)
        to_ref[pl.ds(first_row, tokens), :] = piece_ref[...]

    put(band_ref, own_ref, band)
    put(band_ref, shared_ref, band ^ SHARED)
    for hop in range(hops):
        for piece_ref, member in ((near_refs[hop], plane), (far_refs[hop], 1 - plane)):
            put(band_ref, piece_ref, band ^ jnp.where(member == 0, OFFSETS[0][hop], OFFSETS[1][hop]))
    for offset, pair_ref in enumerate(cot_refs):
        for part, source in enumerate((band ^ offset, band ^ offset ^ 4)):
            put(cot_ref, pair_ref.at[pl.ds(part * tokens, tokens)], source)
    partial_ref[...] = contract(band_ref[...], cot_ref[...], 0, 0)


def call(kernel, out_shapes, scratch_shapes, *operands):
    in_specs = [pl.BlockSpec(memory_space=pltpu.SMEM)]
    in_specs += [pl.BlockSpec(memory_space=pltpu.VMEM)] * (len(operands) - 1)
    return pl.pallas_call(
        kernel,
        out_shape=out_shapes,
        in_specs=in_specs,
        out_specs=[pl.BlockSpec(memory_space=pltpu.VMEM)] * len(out_shapes),
        scratch_shapes=scratch_shapes,
        compiler_params=pltpu.CompilerParams(vmem_limit_bytes=32 * 1024 * 1024),
    )(*operands)


def on_device_paired(inputs, weight, cotangent):
    bands = D // BLOCK
    groups = lax.axis_size("dp")
    cores = groups // bands
    members = lax.axis_size("pre")
    core = lax.axis_index("dp") % cores
    band = lax.axis_index("dp") // cores
    plane = lax.axis_index("pre")
    tokens = inputs.shape[0]
    ahead = 1 - 2 * core
    spot = jnp.where(band % 2 == 0, band // 2, bands - 1 - band // 2)

    ring = list(range(0, bands, 2)) + list(range(bands - 1, 0, -2))

    def swap_core(array):
        return lax.ppermute(array, "dp", [(g, g ^ 1) for g in range(groups)])

    def swap_plane(array):
        return lax.ppermute(array, "pre", [(c, members - 1 - c) for c in range(members)])

    def deal(array, hop):
        pairs = [
            (
                (k * cores + c) * members + m,
                ((k ^ OFFSETS[m][hop]) * cores + c) * members + m,
            )
            for k in range(bands)
            for c in range(cores)
            for m in range(members)
        ]
        return lax.ppermute(array, ("dp", "pre"), pairs)

    hops = range(len(OFFSETS[0]))
    bands_out = [band ^ jnp.where(plane == 0, OFFSETS[0][hop], OFFSETS[1][hop]) for hop in hops]
    *packed, own_band = call(
        pack_kernel,
        [jax.ShapeDtypeStruct((tokens, BLOCK), inputs.dtype)] * (len(hops) + 2),
        [],
        jnp.stack(bands_out + [band ^ SHARED, band]).astype(jnp.int32),
        inputs,
    )

    def exchange(array, offset):
        pairs = [
            (k * cores + c, (k ^ offset) * cores + c) for k in range(bands) for c in range(cores)
        ]
        return lax.ppermute(array, "dp", pairs)

    outputs = jnp.dot(inputs, weight, preferred_element_type=jnp.float32).astype(jnp.bfloat16)
    far_cot, outputs = lax.optimization_barrier((exchange(cotangent, 4), outputs))
    near = [deal(packed[hop], hop) for hop in hops]
    shared = exchange(packed[-1], SHARED)
    pair = jnp.concatenate([cotangent, far_cot])
    cots = [pair] + [exchange(pair, offset) for offset in (1, 2, 3)]
    far = [swap_plane(piece) for piece in near]
    (partial_tile,) = call(
        tile_kernel,
        [jax.ShapeDtypeStruct((BLOCK, BLOCK), jnp.float32)],
        [pltpu.VMEM((bands * tokens, BLOCK), inputs.dtype)] * 2,
        jnp.stack([plane, band]).astype(jnp.int32),
        own_band,
        shared,
        *near,
        *far,
        *cots,
    )
    other_partial = swap_core(partial_tile)
    side = jnp.stack([core, plane]).astype(jnp.int32)
    rows = BLOCK // members // cores
    near_piece, next_piece, far_piece = call(
        update_kernel,
        [jax.ShapeDtypeStruct((rows, BLOCK), jnp.bfloat16)] * 3,
        [pltpu.VMEM((BLOCK, BLOCK), jnp.bfloat16)],
        side,
        partial_tile,
        other_partial,
    )

    def turn(array):
        pairs = [
            (ring[k] * cores + c, ring[(k + 1 - 2 * c) % bands] * cores + c)
            for k in range(bands)
            for c in range(cores)
        ]
        return lax.ppermute(array, "dp", pairs)

    half_way = bands // 2
    crossed = swap_plane(far_piece)
    heads = [crossed, swap_core(crossed), near_piece, next_piece]
    columns = [jnp.zeros((bands, cores, rows, BLOCK), jnp.bfloat16)] * 2

    def put(chunk, piece, position, half):
        columns[chunk] = lax.dynamic_update_slice(
            columns[chunk], piece[None, None], (ring_band(position, bands), half, 0, 0)
        )

    for hop in range(half_way + 1):
        for k, head in enumerate(heads):
            chunk, half = k // 2, (core if k % 2 == 0 else 1 - core)
            if hop == half_way and k % 2 == 1:
                continue
            if hop > 0:
                heads[k] = head = turn(head)
                put(chunk, swap_core(head), spot + ahead * hop, 1 - half)
            put(chunk, head, spot - ahead * hop, half)
    latter, former = (column.reshape(bands, cores * rows, BLOCK) for column in columns)
    update = jnp.where(
        plane == 0,
        jnp.concatenate([former, latter], axis=-1),
        jnp.concatenate([latter, former], axis=-1),
    )
    return (outputs, update)


def solution(mesh):
    placed = (P("dp", None), P(None, "pre"), P("dp", "pre"))
    paired = mesh.shape["dp"] == 2 * D // BLOCK and mesh.shape["pre"] == CB == 2
    return jax.shard_map(
        on_device_paired if paired else on_device_general,
        mesh=mesh,
        in_specs=placed,
        out_specs=(P("dp", "pre"), P(None, "pre", None)),
        check_vma=False,
    )
```

```python
import math

import jax
import jax.numpy as jnp
from jax import lax
from jax.experimental import pallas as pl
from jax.experimental.pallas import tpu as pltpu
from jax.sharding import PartitionSpec as P

D = 4096
BLOCK = 512
CB = 2
ITERS = 3


DAMPING = 0.1
HIGH = lax.Precision.HIGHEST


def batch_dot(former, latter):
    return jnp.einsum(
        "sij,sjk->sik", former, latter, precision=HIGH, preferred_element_type=jnp.float32
    )


def on_device_general(inputs, weight, cotangent):
    groups = lax.axis_size("dp")
    members = lax.axis_size("pre")
    group_id = lax.axis_index("dp")
    member_id = lax.axis_index("pre")
    slab_rows = BLOCK // members
    blocks_all = D // BLOCK * CB
    rounds = max(1, blocks_all // groups)
    sharers = max(1, groups // blocks_all)
    col_width = BLOCK // sharers
    copy_id = group_id // blocks_all
    outputs = jnp.dot(inputs, weight, preferred_element_type=jnp.float32).astype(jnp.bfloat16)
    partial_value = lax.dot_general(
        inputs, cotangent, (((0,), (0,)), ((), ())), preferred_element_type=jnp.float32
    )
    owned_ids = (group_id + groups * jnp.arange(rounds, dtype=jnp.int32)) % blocks_all
    row_offsets = owned_ids // CB * BLOCK
    col_offsets = owned_ids % CB * BLOCK
    gradient = lax.psum(partial_value, "dp")
    row_bands = jax.vmap(lambda offset: lax.dynamic_slice_in_dim(gradient, offset, BLOCK, 0))(
        row_offsets
    )
    wide_band = lax.all_gather(row_bands, "pre", axis=2, tiled=True)
    tile_grad = jax.vmap(
        lambda row_band, offset: lax.dynamic_slice_in_dim(row_band, offset, BLOCK, 1)
    )(wide_band, col_offsets)
    first_row = member_id * slab_rows
    own_rows = lax.dynamic_slice_in_dim(tile_grad, first_row, slab_rows, 1)
    own_cols = lax.dynamic_slice_in_dim(tile_grad, first_row, slab_rows, 2)
    left_rows = jnp.einsum(
        "sij,skj->sik", own_rows, tile_grad, precision=HIGH, preferred_element_type=jnp.float32
    )
    right_rows = jnp.einsum(
        "sji,sjk->sik", own_cols, tile_grad, precision=HIGH, preferred_element_type=jnp.float32
    )
    stat_rows = jnp.stack([left_rows, right_rows], axis=1).reshape(rounds * 2, slab_rows, BLOCK)
    tile_energy = jnp.sum(tile_grad * tile_grad, axis=(1, 2))
    energy = jnp.stack([tile_energy, tile_energy], axis=1).reshape(rounds * 2)
    unit_rows = (jnp.arange(BLOCK)[None, :] == (first_row + jnp.arange(slab_rows))[:, None]).astype(
        jnp.float32
    )
    unit_eye = jnp.eye(BLOCK, dtype=jnp.float32)
    state_rows = stat_rows + (DAMPING * energy / BLOCK)[:, None, None] * unit_rows[None]
    root_rows = unit_rows[None]
    for iteration in range(ITERS):
        full_state = lax.all_gather(state_rows, "pre", axis=1, tiled=True)
        if iteration == 0:
            frob_norm = jnp.sqrt(jnp.sum(full_state * full_state, axis=(1, 2)))
            full_state = full_state / frob_norm[:, None, None]
            state_rows = state_rows / frob_norm[:, None, None]
            root_rows = unit_rows[None] * (frob_norm ** (-0.25))[:, None, None]
        factor = (5.0 * unit_eye - full_state) * 0.25
        square = batch_dot(factor, factor)
        square_rows = lax.dynamic_slice_in_dim(square, first_row, slab_rows, 1)
        fourth_rows = batch_dot(square_rows, square)
        state_rows = batch_dot(fourth_rows, full_state)
        root_rows = batch_dot(root_rows, factor)
    root_half = root_rows.astype(jnp.bfloat16).reshape(rounds, 2, slab_rows, BLOCK)
    right_full = lax.all_gather(root_half[:, 1], "pre", axis=1, tiled=True)
    right_cols = lax.dynamic_slice_in_dim(right_full, copy_id * col_width, col_width, 2)
    tile_half = tile_grad.astype(jnp.bfloat16)
    half_prod = jnp.einsum(
        "sij,sjk->sik", root_half[:, 0], tile_half, preferred_element_type=jnp.float32
    ).astype(jnp.bfloat16)
    piece_rows = jnp.einsum(
        "sij,sjk->sik", half_prod, right_cols, preferred_element_type=jnp.float32
    )
    piece_rows = (piece_rows * math.sqrt(BLOCK)).astype(jnp.bfloat16)
    collected = lax.all_gather(piece_rows[None], "dp", axis=0, tiled=True)
    if sharers == 1:
        ordered = jnp.swapaxes(collected, 0, 1).reshape(blocks_all, slab_rows, BLOCK)
    else:
        ordered = (
            collected[:, 0]
            .reshape(sharers, blocks_all, slab_rows, col_width)
            .transpose(1, 2, 0, 3)
            .reshape(blocks_all, slab_rows, BLOCK)
        )
    update = (
        ordered.reshape(D // BLOCK, CB, slab_rows, BLOCK)
        .transpose(0, 2, 1, 3)
        .reshape(D // BLOCK, slab_rows, CB * BLOCK)
    )
    return (outputs, update)


def contract(former, latter, former_dim, latter_dim):
    return lax.dot_general(
        former,
        latter,
        (((former_dim,), (latter_dim,)), ((), ())),
        preferred_element_type=jnp.float32,
    )


def product(former, latter):
    return contract(former.astype(jnp.bfloat16), latter.astype(jnp.bfloat16), 1, 0)


def total(array):
    return jnp.sum(jnp.sum(array, axis=0, keepdims=True), axis=1, keepdims=True)


def newton_step(states):
    excesses = [product(m, m) * (1.0 / 16.0) - 0.625 * m for m in states]
    growths = [3.125 * e + product(e, e) for e in excesses]
    return [(625.0 / 256.0) * m + product(m, g) for m, g in zip(states, growths)]


def inverse_roots(tile):
    tile_half = tile.astype(jnp.bfloat16)
    order = tile.shape[0]
    row_ids = lax.broadcasted_iota(jnp.int32, (order, order), 0)
    col_ids = lax.broadcasted_iota(jnp.int32, (order, order), 1)
    on_diagonal = row_ids == col_ids
    damp = (DAMPING / order) * total(tile * tile)
    stats = [contract(tile_half, tile_half, 1, 1), contract(tile_half, tile_half, 0, 0)]
    stats = [jnp.where(on_diagonal, stat + damp, stat) for stat in stats]
    norms = [jnp.sqrt(total(stat * stat)) for stat in stats]
    firsts = [stat * (1.0 / norm) for stat, norm in zip(stats, norms)]
    seconds = newton_step(firsts)
    thirds = newton_step(seconds)
    crosses = [
        product(m, n) * (1.0 / 16.0) - (5.0 / 16.0) * (m + n) for m, n in zip(firsts, seconds)
    ]
    roots = []
    for cross, third, norm in zip(crosses, thirds, norms):
        root = 1.25 * cross - 0.25 * product(cross, third) - (25.0 / 64.0) * third
        root = jnp.where(on_diagonal, root + 125.0 / 64.0, root)
        scale = 1.0 / jnp.sqrt(jnp.sqrt(norm))
        roots.append((root * scale).astype(jnp.bfloat16))
    return roots


def update_kernel(side_ref, mine_ref, other_ref, near_ref, next_ref, far_ref, left_ref):
    tile = mine_ref[...] + other_ref[...]
    tile_half = tile.astype(jnp.bfloat16)
    left_ref[...], right = inverse_roots(tile)
    rows = near_ref.shape[0]
    core, plane = side_ref[0], side_ref[1]
    for out_ref, part in (
        (near_ref, 2 * plane + core),
        (next_ref, 2 * plane + 1 - core),
        (far_ref, 2 * (1 - plane) + core),
    ):
        left = left_ref[pl.ds(pl.multiple_of(part * rows, rows), rows), :]
        half = contract(left, tile_half, 1, 0).astype(jnp.bfloat16)
        piece = contract(half, right, 1, 0) * math.sqrt(BLOCK)
        out_ref[...] = piece.astype(jnp.bfloat16)


OFFSETS = ((4, 7, 2), (5, 6, 3))
SHARED = 1
PAIR_OFFSETS = (0, 3, 2, 1)


def pack_kernel(place_ref, inputs_ref, *piece_refs):
    for step, piece_ref in enumerate(piece_refs):
        first_col = pl.multiple_of(place_ref[step] * BLOCK, BLOCK)
        piece_ref[...] = inputs_ref[:, pl.ds(first_col, BLOCK)]


def ring_band(position, bands):
    position = (position + 2 * bands) % bands
    return jnp.where(position < bands // 2, 2 * position, 2 * (bands - 1 - position) + 1)


def tile_kernel(place_ref, own_ref, shared_ref, *refs):
    hops = len(OFFSETS[0])
    near_refs, far_refs = refs[:hops], refs[hops : 2 * hops]
    cot_refs = refs[2 * hops : -3]
    partial_ref, band_ref, cot_ref = refs[-3:]
    plane, band = place_ref[0], place_ref[1]
    tokens = own_ref.shape[0]

    def put(to_ref, piece_ref, source):
        first_row = pl.multiple_of(source * tokens, tokens)
        to_ref[pl.ds(first_row, tokens), :] = piece_ref[...]

    put(band_ref, own_ref, band)
    put(band_ref, shared_ref, band ^ SHARED)
    for hop in range(hops):
        for piece_ref, member in ((near_refs[hop], plane), (far_refs[hop], 1 - plane)):
            put(band_ref, piece_ref, band ^ jnp.where(member == 0, OFFSETS[0][hop], OFFSETS[1][hop]))
    for offset, pair_ref in zip(PAIR_OFFSETS, cot_refs):
        for part, source in enumerate((band ^ offset, band ^ offset ^ 4)):
            put(cot_ref, pair_ref.at[pl.ds(part * tokens, tokens)], source)
    partial_ref[...] = contract(band_ref[...], cot_ref[...], 0, 0)


def call(kernel, out_shapes, scratch_shapes, *operands):
    in_specs = [pl.BlockSpec(memory_space=pltpu.SMEM)]
    in_specs += [pl.BlockSpec(memory_space=pltpu.VMEM)] * (len(operands) - 1)
    return pl.pallas_call(
        kernel,
        out_shape=out_shapes,
        in_specs=in_specs,
        out_specs=[pl.BlockSpec(memory_space=pltpu.VMEM)] * len(out_shapes),
        scratch_shapes=scratch_shapes,
        compiler_params=pltpu.CompilerParams(vmem_limit_bytes=32 * 1024 * 1024),
    )(*operands)


def on_device_paired(inputs, weight, cotangent):
    bands = D // BLOCK
    groups = lax.axis_size("dp")
    cores = groups // bands
    members = lax.axis_size("pre")
    core = lax.axis_index("dp") % cores
    band = lax.axis_index("dp") // cores
    plane = lax.axis_index("pre")
    tokens = inputs.shape[0]
    ahead = 1 - 2 * core
    spot = jnp.where(band % 2 == 0, band // 2, bands - 1 - band // 2)

    ring = list(range(0, bands, 2)) + list(range(bands - 1, 0, -2))

    def swap_core(array):
        return lax.ppermute(array, "dp", [(g, g ^ 1) for g in range(groups)])

    def swap_plane(array):
        return lax.ppermute(array, "pre", [(c, members - 1 - c) for c in range(members)])

    def deal(array, hop):
        pairs = [
            (
                (k * cores + c) * members + m,
                ((k ^ OFFSETS[m][hop]) * cores + c) * members + m,
            )
            for k in range(bands)
            for c in range(cores)
            for m in range(members)
        ]
        return lax.ppermute(array, ("dp", "pre"), pairs)

    hops = range(len(OFFSETS[0]))
    bands_out = [band ^ jnp.where(plane == 0, OFFSETS[0][hop], OFFSETS[1][hop]) for hop in hops]
    *packed, own_band = call(
        pack_kernel,
        [jax.ShapeDtypeStruct((tokens, BLOCK), inputs.dtype)] * (len(hops) + 2),
        [],
        jnp.stack(bands_out + [band ^ SHARED, band]).astype(jnp.int32),
        inputs,
    )

    def exchange(array, offset):
        pairs = [
            (k * cores + c, (k ^ offset) * cores + c) for k in range(bands) for c in range(cores)
        ]
        return lax.ppermute(array, "dp", pairs)

    outputs = jnp.dot(inputs, weight, preferred_element_type=jnp.float32).astype(jnp.bfloat16)
    far_cot, outputs = lax.optimization_barrier((exchange(cotangent, 4), outputs))
    near = [deal(packed[hop], hop) for hop in hops]
    shared = exchange(packed[-1], SHARED)
    pair = jnp.concatenate([cotangent, far_cot])
    cots = [pair] + [exchange(pair, offset) for offset in PAIR_OFFSETS[1:]]
    far = [swap_plane(piece) for piece in near]
    (partial_tile,) = call(
        tile_kernel,
        [jax.ShapeDtypeStruct((BLOCK, BLOCK), jnp.float32)],
        [pltpu.VMEM((bands * tokens, BLOCK), inputs.dtype)] * 2,
        jnp.stack([plane, band]).astype(jnp.int32),
        own_band,
        shared,
        *near,
        *far,
        *cots,
    )
    other_partial = swap_core(partial_tile)
    side = jnp.stack([core, plane]).astype(jnp.int32)
    rows = BLOCK // members // cores
    near_piece, next_piece, far_piece = call(
        update_kernel,
        [jax.ShapeDtypeStruct((rows, BLOCK), jnp.bfloat16)] * 3,
        [pltpu.VMEM((BLOCK, BLOCK), jnp.bfloat16)],
        side,
        partial_tile,
        other_partial,
    )

    def turn(array):
        pairs = [
            (ring[k] * cores + c, ring[(k + 1 - 2 * c) % bands] * cores + c)
            for k in range(bands)
            for c in range(cores)
        ]
        return lax.ppermute(array, "dp", pairs)

    half_way = bands // 2
    crossed = swap_plane(far_piece)
    heads = [crossed, swap_core(crossed), near_piece, next_piece]
    columns = [jnp.zeros((bands, cores, rows, BLOCK), jnp.bfloat16)] * 2

    def put(chunk, piece, position, half):
        columns[chunk] = lax.dynamic_update_slice(
            columns[chunk], piece[None, None], (ring_band(position, bands), half, 0, 0)
        )

    for hop in range(half_way + 1):
        for k, head in enumerate(heads):
            chunk, half = k // 2, (core if k % 2 == 0 else 1 - core)
            if hop == half_way and k % 2 == 1:
                continue
            if hop > 0:
                heads[k] = head = turn(head)
                put(chunk, swap_core(head), spot + ahead * hop, 1 - half)
            put(chunk, head, spot - ahead * hop, half)
    latter, former = (column.reshape(bands, cores * rows, BLOCK) for column in columns)
    update = jnp.where(
        plane == 0,
        jnp.concatenate([former, latter], axis=-1),
        jnp.concatenate([latter, former], axis=-1),
    )
    return (outputs, update)


def solution(mesh):
    placed = (P("dp", None), P(None, "pre"), P("dp", "pre"))
    paired = mesh.shape["dp"] == 2 * D // BLOCK and mesh.shape["pre"] == CB == 2
    return jax.shard_map(
        on_device_paired if paired else on_device_general,
        mesh=mesh,
        in_specs=placed,
        out_specs=(P("dp", "pre"), P(None, "pre", None)),
        check_vma=False,
    )
```

```python
import math

import jax
import jax.numpy as jnp
from jax import lax
from jax.experimental import pallas as pl
from jax.experimental.pallas import tpu as pltpu
from jax.sharding import PartitionSpec as P

D = 4096
BLOCK = 512
CB = 2
ITERS = 3


DAMPING = 0.1
HIGH = lax.Precision.HIGHEST


def batch_dot(former, latter):
    return jnp.einsum(
        "sij,sjk->sik", former, latter, precision=HIGH, preferred_element_type=jnp.float32
    )


def on_device_general(inputs, weight, cotangent):
    groups = lax.axis_size("dp")
    members = lax.axis_size("pre")
    group_id = lax.axis_index("dp")
    member_id = lax.axis_index("pre")
    slab_rows = BLOCK // members
    blocks_all = D // BLOCK * CB
    rounds = max(1, blocks_all // groups)
    sharers = max(1, groups // blocks_all)
    col_width = BLOCK // sharers
    copy_id = group_id // blocks_all
    outputs = jnp.dot(inputs, weight, preferred_element_type=jnp.float32).astype(jnp.bfloat16)
    partial_value = lax.dot_general(
        inputs, cotangent, (((0,), (0,)), ((), ())), preferred_element_type=jnp.float32
    )
    owned_ids = (group_id + groups * jnp.arange(rounds, dtype=jnp.int32)) % blocks_all
    row_offsets = owned_ids // CB * BLOCK
    col_offsets = owned_ids % CB * BLOCK
    gradient = lax.psum(partial_value, "dp")
    row_bands = jax.vmap(lambda offset: lax.dynamic_slice_in_dim(gradient, offset, BLOCK, 0))(
        row_offsets
    )
    wide_band = lax.all_gather(row_bands, "pre", axis=2, tiled=True)
    tile_grad = jax.vmap(
        lambda row_band, offset: lax.dynamic_slice_in_dim(row_band, offset, BLOCK, 1)
    )(wide_band, col_offsets)
    first_row = member_id * slab_rows
    own_rows = lax.dynamic_slice_in_dim(tile_grad, first_row, slab_rows, 1)
    own_cols = lax.dynamic_slice_in_dim(tile_grad, first_row, slab_rows, 2)
    left_rows = jnp.einsum(
        "sij,skj->sik", own_rows, tile_grad, precision=HIGH, preferred_element_type=jnp.float32
    )
    right_rows = jnp.einsum(
        "sji,sjk->sik", own_cols, tile_grad, precision=HIGH, preferred_element_type=jnp.float32
    )
    stat_rows = jnp.stack([left_rows, right_rows], axis=1).reshape(rounds * 2, slab_rows, BLOCK)
    tile_energy = jnp.sum(tile_grad * tile_grad, axis=(1, 2))
    energy = jnp.stack([tile_energy, tile_energy], axis=1).reshape(rounds * 2)
    unit_rows = (jnp.arange(BLOCK)[None, :] == (first_row + jnp.arange(slab_rows))[:, None]).astype(
        jnp.float32
    )
    unit_eye = jnp.eye(BLOCK, dtype=jnp.float32)
    state_rows = stat_rows + (DAMPING * energy / BLOCK)[:, None, None] * unit_rows[None]
    root_rows = unit_rows[None]
    for iteration in range(ITERS):
        full_state = lax.all_gather(state_rows, "pre", axis=1, tiled=True)
        if iteration == 0:
            frob_norm = jnp.sqrt(jnp.sum(full_state * full_state, axis=(1, 2)))
            full_state = full_state / frob_norm[:, None, None]
            state_rows = state_rows / frob_norm[:, None, None]
            root_rows = unit_rows[None] * (frob_norm ** (-0.25))[:, None, None]
        factor = (5.0 * unit_eye - full_state) * 0.25
        square = batch_dot(factor, factor)
        square_rows = lax.dynamic_slice_in_dim(square, first_row, slab_rows, 1)
        fourth_rows = batch_dot(square_rows, square)
        state_rows = batch_dot(fourth_rows, full_state)
        root_rows = batch_dot(root_rows, factor)
    root_half = root_rows.astype(jnp.bfloat16).reshape(rounds, 2, slab_rows, BLOCK)
    right_full = lax.all_gather(root_half[:, 1], "pre", axis=1, tiled=True)
    right_cols = lax.dynamic_slice_in_dim(right_full, copy_id * col_width, col_width, 2)
    tile_half = tile_grad.astype(jnp.bfloat16)
    half_prod = jnp.einsum(
        "sij,sjk->sik", root_half[:, 0], tile_half, preferred_element_type=jnp.float32
    ).astype(jnp.bfloat16)
    piece_rows = jnp.einsum(
        "sij,sjk->sik", half_prod, right_cols, preferred_element_type=jnp.float32
    )
    piece_rows = (piece_rows * math.sqrt(BLOCK)).astype(jnp.bfloat16)
    collected = lax.all_gather(piece_rows[None], "dp", axis=0, tiled=True)
    if sharers == 1:
        ordered = jnp.swapaxes(collected, 0, 1).reshape(blocks_all, slab_rows, BLOCK)
    else:
        ordered = (
            collected[:, 0]
            .reshape(sharers, blocks_all, slab_rows, col_width)
            .transpose(1, 2, 0, 3)
            .reshape(blocks_all, slab_rows, BLOCK)
        )
    update = (
        ordered.reshape(D // BLOCK, CB, slab_rows, BLOCK)
        .transpose(0, 2, 1, 3)
        .reshape(D // BLOCK, slab_rows, CB * BLOCK)
    )
    return (outputs, update)


def contract(former, latter, former_dim, latter_dim):
    return lax.dot_general(
        former,
        latter,
        (((former_dim,), (latter_dim,)), ((), ())),
        preferred_element_type=jnp.float32,
    )


def product(former, latter):
    return contract(former.astype(jnp.bfloat16), latter.astype(jnp.bfloat16), 1, 0)


def total(array):
    return jnp.sum(jnp.sum(array, axis=0, keepdims=True), axis=1, keepdims=True)


def newton_step(states):
    excesses = [product(m, m) * (1.0 / 16.0) - 0.625 * m for m in states]
    growths = [3.125 * e + product(e, e) for e in excesses]
    return [(625.0 / 256.0) * m + product(m, g) for m, g in zip(states, growths)]


def inverse_roots(tile):
    tile_half = tile.astype(jnp.bfloat16)
    order = tile.shape[0]
    row_ids = lax.broadcasted_iota(jnp.int32, (order, order), 0)
    col_ids = lax.broadcasted_iota(jnp.int32, (order, order), 1)
    on_diagonal = row_ids == col_ids
    damp = (DAMPING / order) * total(tile * tile)
    stats = [contract(tile_half, tile_half, 1, 1), contract(tile_half, tile_half, 0, 0)]
    stats = [jnp.where(on_diagonal, stat + damp, stat) for stat in stats]
    norms = [jnp.sqrt(total(stat * stat)) for stat in stats]
    firsts = [stat * (1.0 / norm) for stat, norm in zip(stats, norms)]
    seconds = newton_step(firsts)
    thirds = newton_step(seconds)
    crosses = [
        product(m, n) * (1.0 / 16.0) - (5.0 / 16.0) * (m + n) for m, n in zip(firsts, seconds)
    ]
    roots = []
    for cross, third, norm in zip(crosses, thirds, norms):
        root = 1.25 * cross - 0.25 * product(cross, third) - (25.0 / 64.0) * third
        root = jnp.where(on_diagonal, root + 125.0 / 64.0, root)
        scale = 1.0 / jnp.sqrt(jnp.sqrt(norm))
        roots.append((root * scale).astype(jnp.bfloat16))
    return roots


def update_kernel(side_ref, mine_ref, other_ref, near_ref, next_ref, far_ref, left_ref):
    tile = mine_ref[...] + other_ref[...]
    tile_half = tile.astype(jnp.bfloat16)
    left_ref[...], right = inverse_roots(tile)
    rows = near_ref.shape[0]
    core, plane = side_ref[0], side_ref[1]
    for out_ref, part in (
        (near_ref, 2 * plane + core),
        (next_ref, 2 * plane + 1 - core),
        (far_ref, 2 * (1 - plane) + core),
    ):
        left = left_ref[pl.ds(pl.multiple_of(part * rows, rows), rows), :]
        half = contract(left, tile_half, 1, 0).astype(jnp.bfloat16)
        piece = contract(half, right, 1, 0) * math.sqrt(BLOCK)
        out_ref[...] = piece.astype(jnp.bfloat16)


OFFSETS = ((4, 7, 2), (5, 6, 3))
SHARED = 1


def pack_kernel(place_ref, inputs_ref, *piece_refs):
    for step, piece_ref in enumerate(piece_refs):
        first_col = pl.multiple_of(place_ref[step] * BLOCK, BLOCK)
        piece_ref[...] = inputs_ref[:, pl.ds(first_col, BLOCK)]


def ring_band(position, bands):
    position = (position + 2 * bands) % bands
    return jnp.where(position < bands // 2, 2 * position, 2 * (bands - 1 - position) + 1)


def tile_kernel(place_ref, own_ref, shared_ref, *refs):
    hops = len(OFFSETS[0])
    near_refs, far_refs = refs[:hops], refs[hops : 2 * hops]
    cot_refs = refs[2 * hops : -3]
    partial_ref, band_ref, cot_ref = refs[-3:]
    plane, band = place_ref[0], place_ref[1]
    tokens = own_ref.shape[0]

    def put(to_ref, piece_ref, source):
        first_row = pl.multiple_of(source * tokens, tokens)
        to_ref[pl.ds(first_row, tokens), :] = piece_ref[...]

    put(band_ref, own_ref, band)
    put(band_ref, shared_ref, band ^ SHARED)
    for hop in range(hops):
        for piece_ref, member in ((near_refs[hop], plane), (far_refs[hop], 1 - plane)):
            put(band_ref, piece_ref, band ^ jnp.where(member == 0, OFFSETS[0][hop], OFFSETS[1][hop]))
    for offset, pair_ref in enumerate(cot_refs):
        for part, source in enumerate((band ^ offset, band ^ offset ^ 4)):
            put(cot_ref, pair_ref.at[pl.ds(part * tokens, tokens)], source)
    partial_ref[...] = contract(band_ref[...], cot_ref[...], 0, 0)


def call(kernel, out_shapes, scratch_shapes, *operands):
    in_specs = [pl.BlockSpec(memory_space=pltpu.SMEM)]
    in_specs += [pl.BlockSpec(memory_space=pltpu.VMEM)] * (len(operands) - 1)
    return pl.pallas_call(
        kernel,
        out_shape=out_shapes,
        in_specs=in_specs,
        out_specs=[pl.BlockSpec(memory_space=pltpu.VMEM)] * len(out_shapes),
        scratch_shapes=scratch_shapes,
        compiler_params=pltpu.CompilerParams(vmem_limit_bytes=32 * 1024 * 1024),
    )(*operands)


def on_device_paired(inputs, weight, cotangent):
    bands = D // BLOCK
    groups = lax.axis_size("dp")
    cores = groups // bands
    members = lax.axis_size("pre")
    core = lax.axis_index("dp") % cores
    band = lax.axis_index("dp") // cores
    plane = lax.axis_index("pre")
    tokens = inputs.shape[0]
    ahead = 1 - 2 * core
    spot = jnp.where(band % 2 == 0, band // 2, bands - 1 - band // 2)

    ring = list(range(0, bands, 2)) + list(range(bands - 1, 0, -2))

    def swap_core(array):
        return lax.ppermute(array, "dp", [(g, g ^ 1) for g in range(groups)])

    def swap_plane(array):
        return lax.ppermute(array, "pre", [(c, members - 1 - c) for c in range(members)])

    def deal(array, hop):
        pairs = [
            (
                (k * cores + c) * members + m,
                ((k ^ OFFSETS[m][hop]) * cores + c) * members + m,
            )
            for k in range(bands)
            for c in range(cores)
            for m in range(members)
        ]
        return lax.ppermute(array, ("dp", "pre"), pairs)

    hops = range(len(OFFSETS[0]))
    bands_out = [band ^ jnp.where(plane == 0, OFFSETS[0][hop], OFFSETS[1][hop]) for hop in hops]
    *packed, own_band = call(
        pack_kernel,
        [jax.ShapeDtypeStruct((tokens, BLOCK), inputs.dtype)] * (len(hops) + 2),
        [],
        jnp.stack(bands_out + [band ^ SHARED, band]).astype(jnp.int32),
        inputs,
    )

    def exchange(array, offset):
        pairs = [
            (k * cores + c, (k ^ offset) * cores + c) for k in range(bands) for c in range(cores)
        ]
        return lax.ppermute(array, "dp", pairs)

    outputs = jnp.dot(inputs, weight, preferred_element_type=jnp.float32).astype(jnp.bfloat16)
    far_cot, outputs, shared = lax.optimization_barrier(
        (exchange(cotangent, 4), outputs, exchange(packed[-1], SHARED))
    )
    near = [deal(packed[hop], hop) for hop in hops]
    pair = jnp.concatenate([cotangent, far_cot])
    cots = [pair] + [exchange(pair, offset) for offset in (1, 2, 3)]
    far = [swap_plane(piece) for piece in near]
    (partial_tile,) = call(
        tile_kernel,
        [jax.ShapeDtypeStruct((BLOCK, BLOCK), jnp.float32)],
        [pltpu.VMEM((bands * tokens, BLOCK), inputs.dtype)] * 2,
        jnp.stack([plane, band]).astype(jnp.int32),
        own_band,
        shared,
        *near,
        *far,
        *cots,
    )
    other_partial = swap_core(partial_tile)
    side = jnp.stack([core, plane]).astype(jnp.int32)
    rows = BLOCK // members // cores
    near_piece, next_piece, far_piece = call(
        update_kernel,
        [jax.ShapeDtypeStruct((rows, BLOCK), jnp.bfloat16)] * 3,
        [pltpu.VMEM((BLOCK, BLOCK), jnp.bfloat16)],
        side,
        partial_tile,
        other_partial,
    )

    def turn(array):
        pairs = [
            (ring[k] * cores + c, ring[(k + 1 - 2 * c) % bands] * cores + c)
            for k in range(bands)
            for c in range(cores)
        ]
        return lax.ppermute(array, "dp", pairs)

    half_way = bands // 2
    crossed = swap_plane(far_piece)
    heads = [crossed, swap_core(crossed), near_piece, next_piece]
    columns = [jnp.zeros((bands, cores, rows, BLOCK), jnp.bfloat16)] * 2

    def put(chunk, piece, position, half):
        columns[chunk] = lax.dynamic_update_slice(
            columns[chunk], piece[None, None], (ring_band(position, bands), half, 0, 0)
        )

    for hop in range(half_way + 1):
        for k, head in enumerate(heads):
            chunk, half = k // 2, (core if k % 2 == 0 else 1 - core)
            if hop == half_way and k % 2 == 1:
                continue
            if hop > 0:
                heads[k] = head = turn(head)
                put(chunk, swap_core(head), spot + ahead * hop, 1 - half)
            put(chunk, head, spot - ahead * hop, half)
    latter, former = (column.reshape(bands, cores * rows, BLOCK) for column in columns)
    update = jnp.where(
        plane == 0,
        jnp.concatenate([former, latter], axis=-1),
        jnp.concatenate([latter, former], axis=-1),
    )
    return (outputs, update)


def solution(mesh):
    placed = (P("dp", None), P(None, "pre"), P("dp", "pre"))
    paired = mesh.shape["dp"] == 2 * D // BLOCK and mesh.shape["pre"] == CB == 2
    return jax.shard_map(
        on_device_paired if paired else on_device_general,
        mesh=mesh,
        in_specs=placed,
        out_specs=(P("dp", "pre"), P(None, "pre", None)),
        check_vma=False,
    )
```

```python
import math

import jax
import jax.numpy as jnp
from jax import lax
from jax.experimental import pallas as pl
from jax.experimental.pallas import tpu as pltpu
from jax.sharding import PartitionSpec as P

D = 4096
BLOCK = 512
CB = 2
ITERS = 3


DAMPING = 0.1
HIGH = lax.Precision.HIGHEST


def batch_dot(former, latter):
    return jnp.einsum(
        "sij,sjk->sik", former, latter, precision=HIGH, preferred_element_type=jnp.float32
    )


def on_device_general(inputs, weight, cotangent):
    groups = lax.axis_size("dp")
    members = lax.axis_size("pre")
    group_id = lax.axis_index("dp")
    member_id = lax.axis_index("pre")
    slab_rows = BLOCK // members
    blocks_all = D // BLOCK * CB
    rounds = max(1, blocks_all // groups)
    sharers = max(1, groups // blocks_all)
    col_width = BLOCK // sharers
    copy_id = group_id // blocks_all
    outputs = jnp.dot(inputs, weight, preferred_element_type=jnp.float32).astype(jnp.bfloat16)
    partial_value = lax.dot_general(
        inputs, cotangent, (((0,), (0,)), ((), ())), preferred_element_type=jnp.float32
    )
    owned_ids = (group_id + groups * jnp.arange(rounds, dtype=jnp.int32)) % blocks_all
    row_offsets = owned_ids // CB * BLOCK
    col_offsets = owned_ids % CB * BLOCK
    gradient = lax.psum(partial_value, "dp")
    row_bands = jax.vmap(lambda offset: lax.dynamic_slice_in_dim(gradient, offset, BLOCK, 0))(
        row_offsets
    )
    wide_band = lax.all_gather(row_bands, "pre", axis=2, tiled=True)
    tile_grad = jax.vmap(
        lambda row_band, offset: lax.dynamic_slice_in_dim(row_band, offset, BLOCK, 1)
    )(wide_band, col_offsets)
    first_row = member_id * slab_rows
    own_rows = lax.dynamic_slice_in_dim(tile_grad, first_row, slab_rows, 1)
    own_cols = lax.dynamic_slice_in_dim(tile_grad, first_row, slab_rows, 2)
    left_rows = jnp.einsum(
        "sij,skj->sik", own_rows, tile_grad, precision=HIGH, preferred_element_type=jnp.float32
    )
    right_rows = jnp.einsum(
        "sji,sjk->sik", own_cols, tile_grad, precision=HIGH, preferred_element_type=jnp.float32
    )
    stat_rows = jnp.stack([left_rows, right_rows], axis=1).reshape(rounds * 2, slab_rows, BLOCK)
    tile_energy = jnp.sum(tile_grad * tile_grad, axis=(1, 2))
    energy = jnp.stack([tile_energy, tile_energy], axis=1).reshape(rounds * 2)
    unit_rows = (jnp.arange(BLOCK)[None, :] == (first_row + jnp.arange(slab_rows))[:, None]).astype(
        jnp.float32
    )
    unit_eye = jnp.eye(BLOCK, dtype=jnp.float32)
    state_rows = stat_rows + (DAMPING * energy / BLOCK)[:, None, None] * unit_rows[None]
    root_rows = unit_rows[None]
    for iteration in range(ITERS):
        full_state = lax.all_gather(state_rows, "pre", axis=1, tiled=True)
        if iteration == 0:
            frob_norm = jnp.sqrt(jnp.sum(full_state * full_state, axis=(1, 2)))
            full_state = full_state / frob_norm[:, None, None]
            state_rows = state_rows / frob_norm[:, None, None]
            root_rows = unit_rows[None] * (frob_norm ** (-0.25))[:, None, None]
        factor = (5.0 * unit_eye - full_state) * 0.25
        square = batch_dot(factor, factor)
        square_rows = lax.dynamic_slice_in_dim(square, first_row, slab_rows, 1)
        fourth_rows = batch_dot(square_rows, square)
        state_rows = batch_dot(fourth_rows, full_state)
        root_rows = batch_dot(root_rows, factor)
    root_half = root_rows.astype(jnp.bfloat16).reshape(rounds, 2, slab_rows, BLOCK)
    right_full = lax.all_gather(root_half[:, 1], "pre", axis=1, tiled=True)
    right_cols = lax.dynamic_slice_in_dim(right_full, copy_id * col_width, col_width, 2)
    tile_half = tile_grad.astype(jnp.bfloat16)
    half_prod = jnp.einsum(
        "sij,sjk->sik", root_half[:, 0], tile_half, preferred_element_type=jnp.float32
    ).astype(jnp.bfloat16)
    piece_rows = jnp.einsum(
        "sij,sjk->sik", half_prod, right_cols, preferred_element_type=jnp.float32
    )
    piece_rows = (piece_rows * math.sqrt(BLOCK)).astype(jnp.bfloat16)
    collected = lax.all_gather(piece_rows[None], "dp", axis=0, tiled=True)
    if sharers == 1:
        ordered = jnp.swapaxes(collected, 0, 1).reshape(blocks_all, slab_rows, BLOCK)
    else:
        ordered = (
            collected[:, 0]
            .reshape(sharers, blocks_all, slab_rows, col_width)
            .transpose(1, 2, 0, 3)
            .reshape(blocks_all, slab_rows, BLOCK)
        )
    update = (
        ordered.reshape(D // BLOCK, CB, slab_rows, BLOCK)
        .transpose(0, 2, 1, 3)
        .reshape(D // BLOCK, slab_rows, CB * BLOCK)
    )
    return (outputs, update)


def contract(former, latter, former_dim, latter_dim):
    return lax.dot_general(
        former,
        latter,
        (((former_dim,), (latter_dim,)), ((), ())),
        preferred_element_type=jnp.float32,
    )


def product(former, latter):
    return contract(former.astype(jnp.bfloat16), latter.astype(jnp.bfloat16), 1, 0)


def total(array):
    return jnp.sum(jnp.sum(array, axis=0, keepdims=True), axis=1, keepdims=True)


def newton_step(states):
    excesses = [product(m, m) * (1.0 / 16.0) - 0.625 * m for m in states]
    growths = [3.125 * e + product(e, e) for e in excesses]
    return [(625.0 / 256.0) * m + product(m, g) for m, g in zip(states, growths)]


def inverse_roots(tile):
    tile_half = tile.astype(jnp.bfloat16)
    order = tile.shape[0]
    row_ids = lax.broadcasted_iota(jnp.int32, (order, order), 0)
    col_ids = lax.broadcasted_iota(jnp.int32, (order, order), 1)
    on_diagonal = row_ids == col_ids
    damp = (DAMPING / order) * total(tile * tile)
    stats = [contract(tile_half, tile_half, 1, 1), contract(tile_half, tile_half, 0, 0)]
    stats = [jnp.where(on_diagonal, stat + damp, stat) for stat in stats]
    norms = [jnp.sqrt(total(stat * stat)) for stat in stats]
    firsts = [stat * (1.0 / norm) for stat, norm in zip(stats, norms)]
    seconds = newton_step(firsts)
    thirds = newton_step(seconds)
    crosses = [
        product(m, n) * (1.0 / 16.0) - (5.0 / 16.0) * (m + n) for m, n in zip(firsts, seconds)
    ]
    roots = []
    for cross, third, norm in zip(crosses, thirds, norms):
        root = 1.25 * cross - 0.25 * product(cross, third) - (25.0 / 64.0) * third
        root = jnp.where(on_diagonal, root + 125.0 / 64.0, root)
        scale = 1.0 / jnp.sqrt(jnp.sqrt(norm))
        roots.append((root * scale).astype(jnp.bfloat16))
    return roots


def update_kernel(place_ref, mine_ref, other_ref, near_ref, next_ref, far_ref, left_ref):
    tile = mine_ref[...] + other_ref[...]
    tile_half = tile.astype(jnp.bfloat16)
    left_ref[...], right = inverse_roots(tile)
    rows = near_ref.shape[0]
    core, plane = place_ref[0], place_ref[1]
    for out_ref, part in (
        (near_ref, 2 * plane + core),
        (next_ref, 2 * plane + 1 - core),
        (far_ref, 2 * (1 - plane) + core),
    ):
        left = left_ref[pl.ds(pl.multiple_of(part * rows, rows), rows), :]
        half = contract(left, tile_half, 1, 0).astype(jnp.bfloat16)
        piece = contract(half, right, 1, 0) * math.sqrt(BLOCK)
        out_ref[...] = piece.astype(jnp.bfloat16)


OFFSETS = ((4, 7, 2), (5, 6, 3))
SHARED = 1


def pack_kernel(place_ref, inputs_ref, *piece_refs):
    for step, piece_ref in enumerate(piece_refs):
        first_col = pl.multiple_of(place_ref[step] * BLOCK, BLOCK)
        piece_ref[...] = inputs_ref[:, pl.ds(first_col, BLOCK)]


def ring_band(position, bands):
    position = (position + 2 * bands) % bands
    return jnp.where(position < bands // 2, 2 * position, 2 * (bands - 1 - position) + 1)


def tile_kernel(place_ref, own_ref, *refs):
    hops = len(OFFSETS[0])
    near_refs, far_refs = refs[:hops], refs[hops : 2 * hops]
    shared_ref = refs[2 * hops]
    cot_refs = refs[2 * hops + 1 : -3]
    partial_ref, band_ref, cot_ref = refs[-3:]
    plane, band = place_ref[1], place_ref[2]
    tokens = own_ref.shape[0]

    def put(to_ref, piece_ref, source):
        first_row = pl.multiple_of(source * tokens, tokens)
        to_ref[pl.ds(first_row, tokens), :] = piece_ref[...]

    put(band_ref, own_ref, band)
    put(band_ref, shared_ref, band ^ SHARED)
    for hop in range(hops):
        for piece_ref, member in ((near_refs[hop], plane), (far_refs[hop], 1 - plane)):
            put(band_ref, piece_ref, band ^ jnp.where(member == 0, OFFSETS[0][hop], OFFSETS[1][hop]))
    for offset, pair_ref in enumerate(cot_refs):
        for part, source in enumerate((band ^ offset, band ^ offset ^ 4)):
            put(cot_ref, pair_ref.at[pl.ds(part * tokens, tokens)], source)
    partial_ref[...] = contract(band_ref[...], cot_ref[...], 0, 0)


def call(kernel, out_shapes, scratch_shapes, *operands):
    in_specs = [pl.BlockSpec(memory_space=pltpu.SMEM)]
    in_specs += [pl.BlockSpec(memory_space=pltpu.VMEM)] * (len(operands) - 1)
    return pl.pallas_call(
        kernel,
        out_shape=out_shapes,
        in_specs=in_specs,
        out_specs=[pl.BlockSpec(memory_space=pltpu.VMEM)] * len(out_shapes),
        scratch_shapes=scratch_shapes,
        compiler_params=pltpu.CompilerParams(vmem_limit_bytes=32 * 1024 * 1024),
    )(*operands)


def on_device_paired(inputs, weight, cotangent):
    bands = D // BLOCK
    groups = lax.axis_size("dp")
    cores = groups // bands
    members = lax.axis_size("pre")
    core = lax.axis_index("dp") % cores
    band = lax.axis_index("dp") // cores
    plane = lax.axis_index("pre")
    tokens = inputs.shape[0]
    ahead = 1 - 2 * core
    spot = jnp.where(band % 2 == 0, band // 2, bands - 1 - band // 2)

    ring = list(range(0, bands, 2)) + list(range(bands - 1, 0, -2))

    def swap_core(array):
        return lax.ppermute(array, "dp", [(g, g ^ 1) for g in range(groups)])

    def swap_plane(array):
        return lax.ppermute(array, "pre", [(c, members - 1 - c) for c in range(members)])

    def deal(array, hop):
        pairs = [
            (
                (k * cores + c) * members + m,
                ((k ^ OFFSETS[m][hop]) * cores + c) * members + m,
            )
            for k in range(bands)
            for c in range(cores)
            for m in range(members)
        ]
        return lax.ppermute(array, ("dp", "pre"), pairs)

    hops = range(len(OFFSETS[0]))
    bands_out = [band ^ jnp.where(plane == 0, OFFSETS[0][hop], OFFSETS[1][hop]) for hop in hops]
    *packed, own_band = call(
        pack_kernel,
        [jax.ShapeDtypeStruct((tokens, BLOCK), inputs.dtype)] * (len(hops) + 2),
        [],
        jnp.stack(bands_out + [band ^ SHARED, band]).astype(jnp.int32),
        inputs,
    )

    def exchange(array, offset):
        pairs = [
            (k * cores + c, (k ^ offset) * cores + c) for k in range(bands) for c in range(cores)
        ]
        return lax.ppermute(array, "dp", pairs)

    outputs = jnp.dot(inputs, weight, preferred_element_type=jnp.float32).astype(jnp.bfloat16)
    far_cot, outputs = lax.optimization_barrier((exchange(cotangent, 4), outputs))
    near = [deal(packed[hop], hop) for hop in hops]
    shared = exchange(packed[-1], SHARED)
    pair = jnp.concatenate([cotangent, far_cot])
    cots = [pair] + [exchange(pair, offset) for offset in (1, 2, 3)]
    far = [swap_plane(piece) for piece in near]
    place = jnp.stack([core, plane, band]).astype(jnp.int32)
    (partial_tile,) = call(
        tile_kernel,
        [jax.ShapeDtypeStruct((BLOCK, BLOCK), jnp.float32)],
        [pltpu.VMEM((bands * tokens, BLOCK), inputs.dtype)] * 2,
        place,
        own_band,
        *near,
        *far,
        shared,
        *cots,
    )
    other_partial = swap_core(partial_tile)
    rows = BLOCK // members // cores
    near_piece, next_piece, far_piece = call(
        update_kernel,
        [jax.ShapeDtypeStruct((rows, BLOCK), jnp.bfloat16)] * 3,
        [pltpu.VMEM((BLOCK, BLOCK), jnp.bfloat16)],
        place,
        partial_tile,
        other_partial,
    )

    def turn(array):
        pairs = [
            (ring[k] * cores + c, ring[(k + 1 - 2 * c) % bands] * cores + c)
            for k in range(bands)
            for c in range(cores)
        ]
        return lax.ppermute(array, "dp", pairs)

    half_way = bands // 2
    crossed = swap_plane(far_piece)
    heads = [crossed, swap_core(crossed), near_piece, next_piece]
    columns = [jnp.zeros((bands, cores, rows, BLOCK), jnp.bfloat16)] * 2

    def put(chunk, piece, position, half):
        columns[chunk] = lax.dynamic_update_slice(
            columns[chunk], piece[None, None], (ring_band(position, bands), half, 0, 0)
        )

    for hop in range(half_way + 1):
        for k, head in enumerate(heads):
            chunk, half = k // 2, (core if k % 2 == 0 else 1 - core)
            if hop == half_way and k % 2 == 1:
                continue
            if hop > 0:
                heads[k] = head = turn(head)
                put(chunk, swap_core(head), spot + ahead * hop, 1 - half)
            put(chunk, head, spot - ahead * hop, half)
    latter, former = (column.reshape(bands, cores * rows, BLOCK) for column in columns)
    update = jnp.where(
        plane == 0,
        jnp.concatenate([former, latter], axis=-1),
        jnp.concatenate([latter, former], axis=-1),
    )
    return (outputs, update)


def solution(mesh):
    placed = (P("dp", None), P(None, "pre"), P("dp", "pre"))
    paired = mesh.shape["dp"] == 2 * D // BLOCK and mesh.shape["pre"] == CB == 2
    return jax.shard_map(
        on_device_paired if paired else on_device_general,
        mesh=mesh,
        in_specs=placed,
        out_specs=(P("dp", "pre"), P(None, "pre", None)),
        check_vma=False,
    )
```

```python
import math

import jax
import jax.numpy as jnp
from jax import lax
from jax.experimental import pallas as pl
from jax.experimental.pallas import tpu as pltpu
from jax.sharding import PartitionSpec as P

D = 4096
BLOCK = 512
CB = 2
ITERS = 3


DAMPING = 0.1
HIGH = lax.Precision.HIGHEST


def batch_dot(former, latter):
    return jnp.einsum(
        "sij,sjk->sik", former, latter, precision=HIGH, preferred_element_type=jnp.float32
    )


def on_device_general(inputs, weight, cotangent):
    groups = lax.axis_size("dp")
    members = lax.axis_size("pre")
    group_id = lax.axis_index("dp")
    member_id = lax.axis_index("pre")
    slab_rows = BLOCK // members
    blocks_all = D // BLOCK * CB
    rounds = max(1, blocks_all // groups)
    sharers = max(1, groups // blocks_all)
    col_width = BLOCK // sharers
    copy_id = group_id // blocks_all
    outputs = jnp.dot(inputs, weight, preferred_element_type=jnp.float32).astype(jnp.bfloat16)
    partial_value = lax.dot_general(
        inputs, cotangent, (((0,), (0,)), ((), ())), preferred_element_type=jnp.float32
    )
    owned_ids = (group_id + groups * jnp.arange(rounds, dtype=jnp.int32)) % blocks_all
    row_offsets = owned_ids // CB * BLOCK
    col_offsets = owned_ids % CB * BLOCK
    gradient = lax.psum(partial_value, "dp")
    row_bands = jax.vmap(lambda offset: lax.dynamic_slice_in_dim(gradient, offset, BLOCK, 0))(
        row_offsets
    )
    wide_band = lax.all_gather(row_bands, "pre", axis=2, tiled=True)
    tile_grad = jax.vmap(
        lambda row_band, offset: lax.dynamic_slice_in_dim(row_band, offset, BLOCK, 1)
    )(wide_band, col_offsets)
    first_row = member_id * slab_rows
    own_rows = lax.dynamic_slice_in_dim(tile_grad, first_row, slab_rows, 1)
    own_cols = lax.dynamic_slice_in_dim(tile_grad, first_row, slab_rows, 2)
    left_rows = jnp.einsum(
        "sij,skj->sik", own_rows, tile_grad, precision=HIGH, preferred_element_type=jnp.float32
    )
    right_rows = jnp.einsum(
        "sji,sjk->sik", own_cols, tile_grad, precision=HIGH, preferred_element_type=jnp.float32
    )
    stat_rows = jnp.stack([left_rows, right_rows], axis=1).reshape(rounds * 2, slab_rows, BLOCK)
    tile_energy = jnp.sum(tile_grad * tile_grad, axis=(1, 2))
    energy = jnp.stack([tile_energy, tile_energy], axis=1).reshape(rounds * 2)
    unit_rows = (jnp.arange(BLOCK)[None, :] == (first_row + jnp.arange(slab_rows))[:, None]).astype(
        jnp.float32
    )
    unit_eye = jnp.eye(BLOCK, dtype=jnp.float32)
    state_rows = stat_rows + (DAMPING * energy / BLOCK)[:, None, None] * unit_rows[None]
    root_rows = unit_rows[None]
    for iteration in range(ITERS):
        full_state = lax.all_gather(state_rows, "pre", axis=1, tiled=True)
        if iteration == 0:
            frob_norm = jnp.sqrt(jnp.sum(full_state * full_state, axis=(1, 2)))
            full_state = full_state / frob_norm[:, None, None]
            state_rows = state_rows / frob_norm[:, None, None]
            root_rows = unit_rows[None] * (frob_norm ** (-0.25))[:, None, None]
        factor = (5.0 * unit_eye - full_state) * 0.25
        square = batch_dot(factor, factor)
        square_rows = lax.dynamic_slice_in_dim(square, first_row, slab_rows, 1)
        fourth_rows = batch_dot(square_rows, square)
        state_rows = batch_dot(fourth_rows, full_state)
        root_rows = batch_dot(root_rows, factor)
    root_half = root_rows.astype(jnp.bfloat16).reshape(rounds, 2, slab_rows, BLOCK)
    right_full = lax.all_gather(root_half[:, 1], "pre", axis=1, tiled=True)
    right_cols = lax.dynamic_slice_in_dim(right_full, copy_id * col_width, col_width, 2)
    tile_half = tile_grad.astype(jnp.bfloat16)
    half_prod = jnp.einsum(
        "sij,sjk->sik", root_half[:, 0], tile_half, preferred_element_type=jnp.float32
    ).astype(jnp.bfloat16)
    piece_rows = jnp.einsum(
        "sij,sjk->sik", half_prod, right_cols, preferred_element_type=jnp.float32
    )
    piece_rows = (piece_rows * math.sqrt(BLOCK)).astype(jnp.bfloat16)
    collected = lax.all_gather(piece_rows[None], "dp", axis=0, tiled=True)
    if sharers == 1:
        ordered = jnp.swapaxes(collected, 0, 1).reshape(blocks_all, slab_rows, BLOCK)
    else:
        ordered = (
            collected[:, 0]
            .reshape(sharers, blocks_all, slab_rows, col_width)
            .transpose(1, 2, 0, 3)
            .reshape(blocks_all, slab_rows, BLOCK)
        )
    update = (
        ordered.reshape(D // BLOCK, CB, slab_rows, BLOCK)
        .transpose(0, 2, 1, 3)
        .reshape(D // BLOCK, slab_rows, CB * BLOCK)
    )
    return (outputs, update)


def contract(former, latter, former_dim, latter_dim):
    return lax.dot_general(
        former,
        latter,
        (((former_dim,), (latter_dim,)), ((), ())),
        preferred_element_type=jnp.float32,
    )


def product(former, latter):
    return contract(former.astype(jnp.bfloat16), latter.astype(jnp.bfloat16), 1, 0)


def total(array):
    return jnp.sum(jnp.sum(array, axis=0, keepdims=True), axis=1, keepdims=True)


def newton_step(states):
    excesses = [product(m, m) * (1.0 / 16.0) - 0.625 * m for m in states]
    growths = [3.125 * e + product(e, e) for e in excesses]
    return [(625.0 / 256.0) * m + product(m, g) for m, g in zip(states, growths)]


def inverse_roots(tile):
    tile_half = tile.astype(jnp.bfloat16)
    order = tile.shape[0]
    row_ids = lax.broadcasted_iota(jnp.int32, (order, order), 0)
    col_ids = lax.broadcasted_iota(jnp.int32, (order, order), 1)
    on_diagonal = row_ids == col_ids
    damp = (DAMPING / order) * total(tile * tile)
    stats = [contract(tile_half, tile_half, 1, 1), contract(tile_half, tile_half, 0, 0)]
    stats = [jnp.where(on_diagonal, stat + damp, stat) for stat in stats]
    norms = [jnp.sqrt(total(stat * stat)) for stat in stats]
    firsts = [stat * (1.0 / norm) for stat, norm in zip(stats, norms)]
    seconds = newton_step(firsts)
    thirds = newton_step(seconds)
    crosses = [
        product(m, n) * (1.0 / 16.0) - (5.0 / 16.0) * (m + n) for m, n in zip(firsts, seconds)
    ]
    roots = []
    for cross, third, norm in zip(crosses, thirds, norms):
        root = 1.25 * cross - 0.25 * product(cross, third) - (25.0 / 64.0) * third
        root = jnp.where(on_diagonal, root + 125.0 / 64.0, root)
        scale = 1.0 / jnp.sqrt(jnp.sqrt(norm))
        roots.append((root * scale).astype(jnp.bfloat16))
    return roots


def update_kernel(side_ref, mine_ref, other_ref, near_ref, next_ref, far_ref, left_ref):
    tile = mine_ref[...] + other_ref[...]
    tile_half = tile.astype(jnp.bfloat16)
    left_ref[...], right = inverse_roots(tile)
    rows = near_ref.shape[0]
    core, plane = side_ref[0], side_ref[1]
    parts = (2 * plane + core, 2 * plane + 1 - core, 2 * (1 - plane) + core)
    left = jnp.concatenate(
        [left_ref[pl.ds(pl.multiple_of(part * rows, rows), rows), :] for part in parts]
    )
    half = contract(left, tile_half, 1, 0).astype(jnp.bfloat16)
    pieces = (contract(half, right, 1, 0) * math.sqrt(BLOCK)).astype(jnp.bfloat16)
    for number, out_ref in enumerate((near_ref, next_ref, far_ref)):
        out_ref[...] = pieces[number * rows : (number + 1) * rows]


OFFSETS = ((4, 7, 2), (5, 6, 3))
SHARED = 1


def pack_kernel(place_ref, inputs_ref, *piece_refs):
    for step, piece_ref in enumerate(piece_refs):
        first_col = pl.multiple_of(place_ref[step] * BLOCK, BLOCK)
        piece_ref[...] = inputs_ref[:, pl.ds(first_col, BLOCK)]


def ring_band(position, bands):
    position = (position + 2 * bands) % bands
    return jnp.where(position < bands // 2, 2 * position, 2 * (bands - 1 - position) + 1)


def tile_kernel(place_ref, own_ref, shared_ref, *refs):
    hops = len(OFFSETS[0])
    near_refs, far_refs = refs[:hops], refs[hops : 2 * hops]
    cot_refs = refs[2 * hops : -3]
    partial_ref, band_ref, cot_ref = refs[-3:]
    plane, band = place_ref[0], place_ref[1]
    tokens = own_ref.shape[0]

    def put(to_ref, piece_ref, source):
        first_row = pl.multiple_of(source * tokens, tokens)
        to_ref[pl.ds(first_row, tokens), :] = piece_ref[...]

    put(band_ref, own_ref, band)
    put(band_ref, shared_ref, band ^ SHARED)
    for hop in range(hops):
        for piece_ref, member in ((near_refs[hop], plane), (far_refs[hop], 1 - plane)):
            put(band_ref, piece_ref, band ^ jnp.where(member == 0, OFFSETS[0][hop], OFFSETS[1][hop]))
    for offset, pair_ref in enumerate(cot_refs):
        for part, source in enumerate((band ^ offset, band ^ offset ^ 4)):
            put(cot_ref, pair_ref.at[pl.ds(part * tokens, tokens)], source)
    partial_ref[...] = contract(band_ref[...], cot_ref[...], 0, 0)


def call(kernel, out_shapes, scratch_shapes, *operands):
    in_specs = [pl.BlockSpec(memory_space=pltpu.SMEM)]
    in_specs += [pl.BlockSpec(memory_space=pltpu.VMEM)] * (len(operands) - 1)
    return pl.pallas_call(
        kernel,
        out_shape=out_shapes,
        in_specs=in_specs,
        out_specs=[pl.BlockSpec(memory_space=pltpu.VMEM)] * len(out_shapes),
        scratch_shapes=scratch_shapes,
        compiler_params=pltpu.CompilerParams(vmem_limit_bytes=32 * 1024 * 1024),
    )(*operands)


def on_device_paired(inputs, weight, cotangent):
    bands = D // BLOCK
    groups = lax.axis_size("dp")
    cores = groups // bands
    members = lax.axis_size("pre")
    core = lax.axis_index("dp") % cores
    band = lax.axis_index("dp") // cores
    plane = lax.axis_index("pre")
    tokens = inputs.shape[0]
    ahead = 1 - 2 * core
    spot = jnp.where(band % 2 == 0, band // 2, bands - 1 - band // 2)

    ring = list(range(0, bands, 2)) + list(range(bands - 1, 0, -2))

    def swap_core(array):
        return lax.ppermute(array, "dp", [(g, g ^ 1) for g in range(groups)])

    def swap_plane(array):
        return lax.ppermute(array, "pre", [(c, members - 1 - c) for c in range(members)])

    def deal(array, hop):
        pairs = [
            (
                (k * cores + c) * members + m,
                ((k ^ OFFSETS[m][hop]) * cores + c) * members + m,
            )
            for k in range(bands)
            for c in range(cores)
            for m in range(members)
        ]
        return lax.ppermute(array, ("dp", "pre"), pairs)

    hops = range(len(OFFSETS[0]))
    bands_out = [band ^ jnp.where(plane == 0, OFFSETS[0][hop], OFFSETS[1][hop]) for hop in hops]
    *packed, own_band = call(
        pack_kernel,
        [jax.ShapeDtypeStruct((tokens, BLOCK), inputs.dtype)] * (len(hops) + 2),
        [],
        jnp.stack(bands_out + [band ^ SHARED, band]).astype(jnp.int32),
        inputs,
    )

    def exchange(array, offset):
        pairs = [
            (k * cores + c, (k ^ offset) * cores + c) for k in range(bands) for c in range(cores)
        ]
        return lax.ppermute(array, "dp", pairs)

    outputs = jnp.dot(inputs, weight, preferred_element_type=jnp.float32).astype(jnp.bfloat16)
    far_cot, outputs = lax.optimization_barrier((exchange(cotangent, 4), outputs))
    near = [deal(packed[hop], hop) for hop in hops]
    shared = exchange(packed[-1], SHARED)
    pair = jnp.concatenate([cotangent, far_cot])
    cots = [pair] + [exchange(pair, offset) for offset in (1, 2, 3)]
    far = [swap_plane(piece) for piece in near]
    (partial_tile,) = call(
        tile_kernel,
        [jax.ShapeDtypeStruct((BLOCK, BLOCK), jnp.float32)],
        [pltpu.VMEM((bands * tokens, BLOCK), inputs.dtype)] * 2,
        jnp.stack([plane, band]).astype(jnp.int32),
        own_band,
        shared,
        *near,
        *far,
        *cots,
    )
    other_partial = swap_core(partial_tile)
    side = jnp.stack([core, plane]).astype(jnp.int32)
    rows = BLOCK // members // cores
    near_piece, next_piece, far_piece = call(
        update_kernel,
        [jax.ShapeDtypeStruct((rows, BLOCK), jnp.bfloat16)] * 3,
        [pltpu.VMEM((BLOCK, BLOCK), jnp.bfloat16)],
        side,
        partial_tile,
        other_partial,
    )

    def turn(array):
        pairs = [
            (ring[k] * cores + c, ring[(k + 1 - 2 * c) % bands] * cores + c)
            for k in range(bands)
            for c in range(cores)
        ]
        return lax.ppermute(array, "dp", pairs)

    half_way = bands // 2
    crossed = swap_plane(far_piece)
    heads = [crossed, swap_core(crossed), near_piece, next_piece]
    columns = [jnp.zeros((bands, cores, rows, BLOCK), jnp.bfloat16)] * 2

    def put(chunk, piece, position, half):
        columns[chunk] = lax.dynamic_update_slice(
            columns[chunk], piece[None, None], (ring_band(position, bands), half, 0, 0)
        )

    for hop in range(half_way + 1):
        for k, head in enumerate(heads):
            chunk, half = k // 2, (core if k % 2 == 0 else 1 - core)
            if hop == half_way and k % 2 == 1:
                continue
            if hop > 0:
                heads[k] = head = turn(head)
                put(chunk, swap_core(head), spot + ahead * hop, 1 - half)
            put(chunk, head, spot - ahead * hop, half)
    latter, former = (column.reshape(bands, cores * rows, BLOCK) for column in columns)
    update = jnp.where(
        plane == 0,
        jnp.concatenate([former, latter], axis=-1),
        jnp.concatenate([latter, former], axis=-1),
    )
    return (outputs, update)


def solution(mesh):
    placed = (P("dp", None), P(None, "pre"), P("dp", "pre"))
    paired = mesh.shape["dp"] == 2 * D // BLOCK and mesh.shape["pre"] == CB == 2
    return jax.shard_map(
        on_device_paired if paired else on_device_general,
        mesh=mesh,
        in_specs=placed,
        out_specs=(P("dp", "pre"), P(None, "pre", None)),
        check_vma=False,
    )
```

```python
import math

import jax
import jax.numpy as jnp
from jax import lax
from jax.experimental import pallas as pl
from jax.experimental.pallas import tpu as pltpu
from jax.sharding import PartitionSpec as P

D = 4096
BLOCK = 512
CB = 2
ITERS = 3


DAMPING = 0.1
HIGH = lax.Precision.HIGHEST


def batch_dot(former, latter):
    return jnp.einsum(
        "sij,sjk->sik", former, latter, precision=HIGH, preferred_element_type=jnp.float32
    )


def on_device_general(inputs, weight, cotangent):
    groups = lax.axis_size("dp")
    members = lax.axis_size("pre")
    group_id = lax.axis_index("dp")
    member_id = lax.axis_index("pre")
    slab_rows = BLOCK // members
    blocks_all = D // BLOCK * CB
    rounds = max(1, blocks_all // groups)
    sharers = max(1, groups // blocks_all)
    col_width = BLOCK // sharers
    copy_id = group_id // blocks_all
    outputs = jnp.dot(inputs, weight, preferred_element_type=jnp.float32).astype(jnp.bfloat16)
    partial_value = lax.dot_general(
        inputs, cotangent, (((0,), (0,)), ((), ())), preferred_element_type=jnp.float32
    )
    owned_ids = (group_id + groups * jnp.arange(rounds, dtype=jnp.int32)) % blocks_all
    row_offsets = owned_ids // CB * BLOCK
    col_offsets = owned_ids % CB * BLOCK
    gradient = lax.psum(partial_value, "dp")
    row_bands = jax.vmap(lambda offset: lax.dynamic_slice_in_dim(gradient, offset, BLOCK, 0))(
        row_offsets
    )
    wide_band = lax.all_gather(row_bands, "pre", axis=2, tiled=True)
    tile_grad = jax.vmap(
        lambda row_band, offset: lax.dynamic_slice_in_dim(row_band, offset, BLOCK, 1)
    )(wide_band, col_offsets)
    first_row = member_id * slab_rows
    own_rows = lax.dynamic_slice_in_dim(tile_grad, first_row, slab_rows, 1)
    own_cols = lax.dynamic_slice_in_dim(tile_grad, first_row, slab_rows, 2)
    left_rows = jnp.einsum(
        "sij,skj->sik", own_rows, tile_grad, precision=HIGH, preferred_element_type=jnp.float32
    )
    right_rows = jnp.einsum(
        "sji,sjk->sik", own_cols, tile_grad, precision=HIGH, preferred_element_type=jnp.float32
    )
    stat_rows = jnp.stack([left_rows, right_rows], axis=1).reshape(rounds * 2, slab_rows, BLOCK)
    tile_energy = jnp.sum(tile_grad * tile_grad, axis=(1, 2))
    energy = jnp.stack([tile_energy, tile_energy], axis=1).reshape(rounds * 2)
    unit_rows = (jnp.arange(BLOCK)[None, :] == (first_row + jnp.arange(slab_rows))[:, None]).astype(
        jnp.float32
    )
    unit_eye = jnp.eye(BLOCK, dtype=jnp.float32)
    state_rows = stat_rows + (DAMPING * energy / BLOCK)[:, None, None] * unit_rows[None]
    root_rows = unit_rows[None]
    for iteration in range(ITERS):
        full_state = lax.all_gather(state_rows, "pre", axis=1, tiled=True)
        if iteration == 0:
            frob_norm = jnp.sqrt(jnp.sum(full_state * full_state, axis=(1, 2)))
            full_state = full_state / frob_norm[:, None, None]
            state_rows = state_rows / frob_norm[:, None, None]
            root_rows = unit_rows[None] * (frob_norm ** (-0.25))[:, None, None]
        factor = (5.0 * unit_eye - full_state) * 0.25
        square = batch_dot(factor, factor)
        square_rows = lax.dynamic_slice_in_dim(square, first_row, slab_rows, 1)
        fourth_rows = batch_dot(square_rows, square)
        state_rows = batch_dot(fourth_rows, full_state)
        root_rows = batch_dot(root_rows, factor)
    root_half = root_rows.astype(jnp.bfloat16).reshape(rounds, 2, slab_rows, BLOCK)
    right_full = lax.all_gather(root_half[:, 1], "pre", axis=1, tiled=True)
    right_cols = lax.dynamic_slice_in_dim(right_full, copy_id * col_width, col_width, 2)
    tile_half = tile_grad.astype(jnp.bfloat16)
    half_prod = jnp.einsum(
        "sij,sjk->sik", root_half[:, 0], tile_half, preferred_element_type=jnp.float32
    ).astype(jnp.bfloat16)
    piece_rows = jnp.einsum(
        "sij,sjk->sik", half_prod, right_cols, preferred_element_type=jnp.float32
    )
    piece_rows = (piece_rows * math.sqrt(BLOCK)).astype(jnp.bfloat16)
    collected = lax.all_gather(piece_rows[None], "dp", axis=0, tiled=True)
    if sharers == 1:
        ordered = jnp.swapaxes(collected, 0, 1).reshape(blocks_all, slab_rows, BLOCK)
    else:
        ordered = (
            collected[:, 0]
            .reshape(sharers, blocks_all, slab_rows, col_width)
            .transpose(1, 2, 0, 3)
            .reshape(blocks_all, slab_rows, BLOCK)
        )
    update = (
        ordered.reshape(D // BLOCK, CB, slab_rows, BLOCK)
        .transpose(0, 2, 1, 3)
        .reshape(D // BLOCK, slab_rows, CB * BLOCK)
    )
    return (outputs, update)


def contract(former, latter, former_dim, latter_dim):
    return lax.dot_general(
        former,
        latter,
        (((former_dim,), (latter_dim,)), ((), ())),
        preferred_element_type=jnp.float32,
    )


def product(former, latter):
    return contract(former.astype(jnp.bfloat16), latter.astype(jnp.bfloat16), 1, 0)


def total(array):
    return jnp.sum(jnp.sum(array, axis=0, keepdims=True), axis=1, keepdims=True)


def newton_step(states):
    excesses = [product(m, m) * (1.0 / 16.0) - 0.625 * m for m in states]
    growths = [3.125 * e + product(e, e) for e in excesses]
    return [(625.0 / 256.0) * m + product(m, g) for m, g in zip(states, growths)]


def inverse_roots(tile):
    tile_half = tile.astype(jnp.bfloat16)
    order = tile.shape[0]
    row_ids = lax.broadcasted_iota(jnp.int32, (order, order), 0)
    col_ids = lax.broadcasted_iota(jnp.int32, (order, order), 1)
    on_diagonal = row_ids == col_ids
    damp = (DAMPING / order) * total(tile * tile)
    stats = [contract(tile_half, tile_half, 1, 1), contract(tile_half, tile_half, 0, 0)]
    stats = [jnp.where(on_diagonal, stat + damp, stat) for stat in stats]
    norms = [jnp.sqrt(total(stat * stat)) for stat in stats]
    firsts = [stat * (1.0 / norm) for stat, norm in zip(stats, norms)]
    seconds = newton_step(firsts)
    thirds = newton_step(seconds)
    crosses = [
        product(m, n) * (1.0 / 16.0) - (5.0 / 16.0) * (m + n) for m, n in zip(firsts, seconds)
    ]
    roots = []
    for cross, third, norm in zip(crosses, thirds, norms):
        root = 1.25 * cross - 0.25 * product(cross, third) - (25.0 / 64.0) * third
        root = jnp.where(on_diagonal, root + 125.0 / 64.0, root)
        scale = 1.0 / jnp.sqrt(jnp.sqrt(norm))
        roots.append((root * scale).astype(jnp.bfloat16))
    return roots


def update_kernel(side_ref, mine_ref, other_ref, near_ref, next_ref, far_ref, left_ref):
    tile = mine_ref[...] + other_ref[...]
    tile_half = tile.astype(jnp.bfloat16)
    left_ref[...], right = inverse_roots(tile)
    rows = near_ref.shape[0]
    core, plane = side_ref[0], side_ref[1]
    parts = (2 * plane + core, 2 * plane + 1 - core, 2 * (1 - plane) + core)
    left = jnp.concatenate(
        [left_ref[pl.ds(pl.multiple_of(part * rows, rows), rows), :] for part in parts]
    )
    half = contract(left, tile_half, 1, 0).astype(jnp.bfloat16)
    pieces = (contract(half, right, 1, 0) * math.sqrt(BLOCK)).astype(jnp.bfloat16)
    for number, out_ref in enumerate((near_ref, next_ref, far_ref)):
        out_ref[...] = pieces[number * rows : (number + 1) * rows]


OFFSETS = ((4, 7, 2), (5, 6, 3))
SHARED = 1
PAIR_OFFSETS = (0, 2, 1, 3)


def pack_kernel(place_ref, inputs_ref, *piece_refs):
    for step, piece_ref in enumerate(piece_refs):
        first_col = pl.multiple_of(place_ref[step] * BLOCK, BLOCK)
        piece_ref[...] = inputs_ref[:, pl.ds(first_col, BLOCK)]


def ring_band(position, bands):
    position = (position + 2 * bands) % bands
    return jnp.where(position < bands // 2, 2 * position, 2 * (bands - 1 - position) + 1)


def tile_kernel(place_ref, own_ref, shared_ref, *refs):
    hops = len(OFFSETS[0])
    near_refs, far_refs = refs[:hops], refs[hops : 2 * hops]
    cot_refs = refs[2 * hops : -3]
    partial_ref, band_ref, cot_ref = refs[-3:]
    plane, band = place_ref[0], place_ref[1]
    tokens = own_ref.shape[0]

    def put(to_ref, piece_ref, source):
        first_row = pl.multiple_of(source * tokens, tokens)
        to_ref[pl.ds(first_row, tokens), :] = piece_ref[...]

    put(band_ref, own_ref, band)
    put(band_ref, shared_ref, band ^ SHARED)
    for hop in range(hops):
        for piece_ref, member in ((near_refs[hop], plane), (far_refs[hop], 1 - plane)):
            put(band_ref, piece_ref, band ^ jnp.where(member == 0, OFFSETS[0][hop], OFFSETS[1][hop]))
    for offset, pair_ref in zip(PAIR_OFFSETS, cot_refs):
        for part, source in enumerate((band ^ offset, band ^ offset ^ 4)):
            put(cot_ref, pair_ref.at[pl.ds(part * tokens, tokens)], source)
    partial_ref[...] = contract(band_ref[...], cot_ref[...], 0, 0)


def call(kernel, out_shapes, scratch_shapes, *operands):
    in_specs = [pl.BlockSpec(memory_space=pltpu.SMEM)]
    in_specs += [pl.BlockSpec(memory_space=pltpu.VMEM)] * (len(operands) - 1)
    return pl.pallas_call(
        kernel,
        out_shape=out_shapes,
        in_specs=in_specs,
        out_specs=[pl.BlockSpec(memory_space=pltpu.VMEM)] * len(out_shapes),
        scratch_shapes=scratch_shapes,
        compiler_params=pltpu.CompilerParams(vmem_limit_bytes=32 * 1024 * 1024),
    )(*operands)


def on_device_paired(inputs, weight, cotangent):
    bands = D // BLOCK
    groups = lax.axis_size("dp")
    cores = groups // bands
    members = lax.axis_size("pre")
    core = lax.axis_index("dp") % cores
    band = lax.axis_index("dp") // cores
    plane = lax.axis_index("pre")
    tokens = inputs.shape[0]
    ahead = 1 - 2 * core
    spot = jnp.where(band % 2 == 0, band // 2, bands - 1 - band // 2)

    ring = list(range(0, bands, 2)) + list(range(bands - 1, 0, -2))

    def swap_core(array):
        return lax.ppermute(array, "dp", [(g, g ^ 1) for g in range(groups)])

    def swap_plane(array):
        return lax.ppermute(array, "pre", [(c, members - 1 - c) for c in range(members)])

    def deal(array, hop):
        pairs = [
            (
                (k * cores + c) * members + m,
                ((k ^ OFFSETS[m][hop]) * cores + c) * members + m,
            )
            for k in range(bands)
            for c in range(cores)
            for m in range(members)
        ]
        return lax.ppermute(array, ("dp", "pre"), pairs)

    hops = range(len(OFFSETS[0]))
    bands_out = [band ^ jnp.where(plane == 0, OFFSETS[0][hop], OFFSETS[1][hop]) for hop in hops]
    *packed, own_band = call(
        pack_kernel,
        [jax.ShapeDtypeStruct((tokens, BLOCK), inputs.dtype)] * (len(hops) + 2),
        [],
        jnp.stack(bands_out + [band ^ SHARED, band]).astype(jnp.int32),
        inputs,
    )

    def exchange(array, offset):
        pairs = [
            (k * cores + c, (k ^ offset) * cores + c) for k in range(bands) for c in range(cores)
        ]
        return lax.ppermute(array, "dp", pairs)

    outputs = jnp.dot(inputs, weight, preferred_element_type=jnp.float32).astype(jnp.bfloat16)
    far_cot, outputs = lax.optimization_barrier((exchange(cotangent, 4), outputs))
    near = [deal(packed[hop], hop) for hop in hops]
    shared = exchange(packed[-1], SHARED)
    pair = jnp.concatenate([cotangent, far_cot])
    cots = [pair] + [exchange(pair, offset) for offset in PAIR_OFFSETS[1:]]
    far = [swap_plane(piece) for piece in near]
    (partial_tile,) = call(
        tile_kernel,
        [jax.ShapeDtypeStruct((BLOCK, BLOCK), jnp.float32)],
        [pltpu.VMEM((bands * tokens, BLOCK), inputs.dtype)] * 2,
        jnp.stack([plane, band]).astype(jnp.int32),
        own_band,
        shared,
        *near,
        *far,
        *cots,
    )
    other_partial = swap_core(partial_tile)
    side = jnp.stack([core, plane]).astype(jnp.int32)
    rows = BLOCK // members // cores
    near_piece, next_piece, far_piece = call(
        update_kernel,
        [jax.ShapeDtypeStruct((rows, BLOCK), jnp.bfloat16)] * 3,
        [pltpu.VMEM((BLOCK, BLOCK), jnp.bfloat16)],
        side,
        partial_tile,
        other_partial,
    )

    def turn(array):
        pairs = [
            (ring[k] * cores + c, ring[(k + 1 - 2 * c) % bands] * cores + c)
            for k in range(bands)
            for c in range(cores)
        ]
        return lax.ppermute(array, "dp", pairs)

    half_way = bands // 2
    crossed = swap_plane(far_piece)
    heads = [crossed, swap_core(crossed), near_piece, next_piece]
    columns = [jnp.zeros((bands, cores, rows, BLOCK), jnp.bfloat16)] * 2

    def put(chunk, piece, position, half):
        columns[chunk] = lax.dynamic_update_slice(
            columns[chunk], piece[None, None], (ring_band(position, bands), half, 0, 0)
        )

    for hop in range(half_way + 1):
        for k, head in enumerate(heads):
            chunk, half = k // 2, (core if k % 2 == 0 else 1 - core)
            if hop == half_way and k % 2 == 1:
                continue
            if hop > 0:
                heads[k] = head = turn(head)
                put(chunk, swap_core(head), spot + ahead * hop, 1 - half)
            put(chunk, head, spot - ahead * hop, half)
    latter, former = (column.reshape(bands, cores * rows, BLOCK) for column in columns)
    update = jnp.where(
        plane == 0,
        jnp.concatenate([former, latter], axis=-1),
        jnp.concatenate([latter, former], axis=-1),
    )
    return (outputs, update)


def solution(mesh):
    placed = (P("dp", None), P(None, "pre"), P("dp", "pre"))
    paired = mesh.shape["dp"] == 2 * D // BLOCK and mesh.shape["pre"] == CB == 2
    return jax.shard_map(
        on_device_paired if paired else on_device_general,
        mesh=mesh,
        in_specs=placed,
        out_specs=(P("dp", "pre"), P(None, "pre", None)),
        check_vma=False,
    )
```
